32 devices in a mesh: dp: 16 (over z, y, x), tensor: 2 (over core).
Axes of the slice: x: 2, y: 2, z: 4, core: 2. Of those that a mesh axis runs over, the one named last changes fastest.
Arguments:
- embedded: float32 [32768, 512], P(('dp', 'tensor')), may hold values from -6 to 6
- piece_lengths: int32 [32, 8], P('dp'), may hold values from 1 to 512, 1024 in all within a row
- pair_tags: int32 [32], P('dp'), may hold values from 0 to 3
- pair_embedding: bfloat16 [4, 512], P(None, 'dp'), may hold values from -3 to 3
- w_query: bfloat16 [512, 512], P('dp', 'tensor'), may hold values from -0.25 to 0.25
- w_key: bfloat16 [512, 512], P('dp', 'tensor'), may hold values from -0.25 to 0.25
- w_value: bfloat16 [512, 512], P('dp', 'tensor'), may hold values from -0.25 to 0.25
- w_output: bfloat16 [512, 512], P('tensor', 'dp'), may hold values from -1 to 1
- w_hidden: bfloat16 [512, 2048], P('dp', 'tensor'), may hold values from -0.25 to 0.25
- w_down: bfloat16 [2048, 512], P('tensor', 'dp'), may hold values from -0.125 to 0.125
- first_gain: bfloat16 [512], P('dp'), may hold values from 0.5 to 1.5
- first_shift: bfloat16 [512], P('dp'), may hold values from -2 to 2
- second_gain: bfloat16 [512], P('dp'), may hold values from 0.5 to 1.5
- second_shift: bfloat16 [512], P('dp'), may hold values from -2 to 2
- cotangent: float32 [32768, 512], P(('dp', 'tensor')), may hold values from -6 to 6
Outputs:
- activations: float32 [32768, 512], P(('dp', 'tensor'))
- input_grad: float32 [32768, 512], P(('dp', 'tensor'))
- embedding_grad: float32 [4, 512], P(None, 'dp')
- query_grad: float32 [512, 512], P('dp', 'tensor')
- key_grad: float32 [512, 512], P('dp', 'tensor')
- value_grad: float32 [512, 512], P('dp', 'tensor')
- output_grad: float32 [512, 512], P('tensor', 'dp')
- hidden_grad: float32 [512, 2048], P('dp', 'tensor')
- down_grad: float32 [2048, 512], P('tensor', 'dp')
- first_gain_grad: float32 [512], P('dp')
- first_shift_grad: float32 [512], P('dp')
- second_gain_grad: float32 [512], P('dp')
- second_shift_grad: float32 [512], P('dp')
The draws below stay inside these ranges and needn't reach their ends.
Inputs may be any that keep to these rules, and one draw needn't show every extreme that they name: `piece_lengths`: the 8 piece lengths of each packed sequence sum to 1024; the last piece is padding.
All inputs are finite; a program needn't handle non-finite values.
Results may differ from the reference program's by a relative error of at most 0.02.
Values may be sent and summed in bfloat16 or wider, within the bound.
No kernel may reach another device: no remote copies, remote signals or barrier semaphores. Data moves between devices by JAX's collectives and lax.ppermute only.
A program may use at most 256 MiB of HBM per device.

```python
import math
import jax
import jax.numpy as jnp
import numpy as np
from jax import lax

D = 512
FF = 2048
HEADS = 8
HEAD_DIM = 64
SEQS = 2
LEN = 1024
PIECES = 8
PAIRS = 4
NSEQ = 32
TOKENS = 32768
N_DP = 16


def with_ends(array, rng, low, largest):
    shape = array.shape
    place = [jax.random.randint(jax.random.fold_in(rng, axis), (), 0, shape[axis]) for axis in range(len(shape))]
    array = array.at[tuple(place)].set(low)
    longest = shape.index(max(shape))
    place[longest] = (place[longest] + 1) % shape[longest]
    return array.at[tuple(place)].set(largest)


def raised(array, stream_key, source, target, blocks, factor):
    owner, partner = [(jnp.arange(array.shape[axis_at]) // (array.shape[axis_at] // blocks)).reshape([-1 if axis == axis_at else 1 for axis in range(array.ndim)]) for axis_at in (source, target)]
    chosen = jax.random.permutation(stream_key, blocks)[partner]
    strong = (owner == chosen) | (owner == (partner + blocks // 2) % blocks)
    return jnp.where(strong, factor * array, array)


def block_scale(stream_key, dims, cuts, least, largest):
    factor_of, own = 1.0, jax.random.fold_in(stream_key, 6)
    for position, parts in cuts:
        steps = jnp.exp(jax.random.uniform(jax.random.fold_in(own, position), (parts,), jnp.float32, least / len(cuts), largest / len(cuts)))
        factor_of = factor_of * jnp.repeat(steps, dims[position] // parts).reshape([-1 if axis == position else 1 for axis in range(len(dims))])
    return factor_of


def profile(number_of, total, reach, skew):
    weights = [(1 << 20) // math.isqrt(rank ** skew) + 1 for rank in range(2, number_of + 1)]
    surplus, holding = total - reach - (number_of - 1), [1] * (number_of - 1)
    while surplus > 0:
        free = [i for i in range(number_of - 1) if holding[i] < reach]
        pool, budget = sum([weights[i] for i in free]), surplus
        for i in free:
            extra = min(reach - holding[i], max(1, budget * weights[i] // pool), surplus)
            holding[i] = holding[i] + extra
            surplus = surplus - extra
    return np.array([reach] + holding)


def ragged(key, number_of, total, bound, lean):
    if number_of == 2:
        one = jax.random.randint(key, (), max(1, total - bound), min(bound, total - 1) + 1)
        return jnp.stack([one, total - one])
    lengths = jnp.asarray(profile(number_of, total, bound, lean), jnp.int32)
    pairs = (number_of - 1) // 2
    giver, sink = lengths[1:1 + 2 * pairs:2], lengths[2:2 + 2 * pairs:2]
    slack = jnp.minimum(giver - 1, bound - sink)
    moved = jax.random.randint(jax.random.fold_in(key, 1), (pairs,), 0, 1 << 20) % (slack + 1)
    lengths = lengths.at[1:1 + 2 * pairs:2].set(giver - moved).at[2:2 + 2 * pairs:2].set(sink + moved)
    return lengths[jax.random.permutation(jax.random.fold_in(key, 2), number_of)]


def centred(rng, dims, spread, bound, split=(), kind=jnp.bfloat16):
    array = spread * jax.random.normal(rng, dims, jnp.float32)
    if split:
        array = array * block_scale(rng, dims, split, -0.22, 0.18)
    return jnp.clip(array, -bound, bound).astype(kind)


def noise_with(stream_key, extent, scale, limit, cuts, heavy, kind=jnp.bfloat16):
    drawn = scale * jax.random.normal(stream_key, extent, jnp.float32)
    if cuts:
        drawn = drawn * block_scale(stream_key, extent, cuts, -0.22, 0.18)
    return jnp.clip(raised(drawn, jax.random.fold_in(stream_key, 3), *heavy), -limit, limit).astype(kind)


def setup_inputs(seed: int = 0) -> dict:
    streams_of = jax.random.split(jax.random.key(seed), 16)
    return {
        "embedded": centred(streams_of[0], (TOKENS, D), 1.0, 6.0, ((0, 32),), jnp.float32),
        "piece_lengths": jax.vmap(lambda own: ragged(own, PIECES, LEN, LEN // 2, 1))(jax.random.split(streams_of[1], NSEQ)).reshape((NSEQ, PIECES)).astype(jnp.int32),
        "pair_tags": with_ends(jax.random.randint(streams_of[2], (NSEQ,), 0, PAIRS), jax.random.fold_in(streams_of[2], 1), 0, PAIRS - 1).astype(jnp.int32),
        "pair_embedding": centred(streams_of[3], (PAIRS, D), 0.5, 3.0, ((1, 16),)),
        "w_query": centred(streams_of[4], (D, D), D ** -0.5, 0.25, ((0, 16), (1, 2))),
        "w_key": centred(streams_of[5], (D, D), D ** -0.5, 0.25, ((0, 16), (1, 2))),
        "w_value": centred(streams_of[6], (D, D), D ** -0.5, 0.25, ((0, 16), (1, 2))),
        "w_output": centred(streams_of[7], (D, D), (D // 16) ** -0.5, 1.0, ((0, 2), (1, 16))),
        "w_hidden": centred(streams_of[8], (D, FF), D ** -0.5, 0.25, ((0, 16), (1, 2))),
        "w_down": centred(streams_of[9], (FF, D), FF ** -0.5, 0.125, ((0, 2), (1, 16))),
        "first_gain": jnp.clip(1.0 + 0.1 * jax.random.normal(streams_of[10], (D,), jnp.float32), 0.5, 1.5).astype(jnp.bfloat16),
        "first_shift": centred(streams_of[11], (D,), 0.3, 2.0, ((0, 16),)),
        "second_gain": jnp.clip(1.0 + 0.1 * jax.random.normal(streams_of[12], (D,), jnp.float32), 0.5, 1.5).astype(jnp.bfloat16),
        "second_shift": centred(streams_of[13], (D,), 0.3, 2.0, ((0, 16),)),
        "cotangent": noise_with(streams_of[14], (TOKENS, D), 1.0, 6.0, ((0, 32),), (0, 1, 32, 2.75), jnp.float32),
    }


HIGH = lax.Precision.HIGHEST
NEGATIVE = -1e+30

@jax.custom_vjp
def low(v):
    return lax.optimization_barrier(v.astype(jnp.bfloat16)).astype(jnp.float32)

@jax.custom_vjp
def low_back(v):
    return v

def low_keep(v):
    return (low(v), None)

def low_pass(kept, grad):
    return (grad,)

def back_keep(v):
    return (v, None)

def back_low(kept, grad):
    return (low(grad),)
low.defvjp(low_keep, low_pass)
low_back.defvjp(back_keep, back_low)

def norm_rows(values, gain, shift):
    center = values - lax.optimization_barrier(jnp.mean(values, axis=-1, keepdims=True))
    spread_sq = lax.optimization_barrier(jnp.mean(center * center, axis=-1, keepdims=True))
    return center * lax.rsqrt(spread_sq + 1e-05) * gain + shift

def segments(pieces):
    ends = jnp.cumsum(pieces, axis=-1)
    places = jnp.arange(LEN, dtype=jnp.int32)
    return lax.optimization_barrier(jnp.sum((places[None, :, None] >= ends[:, None, :]).astype(jnp.int32), axis=2))

def project(rows, weight):
    return jnp.einsum('bld,de->ble', rows, weight, precision=HIGH)

def layer(rows, params, allowed):
    w_query, w_key, w_value, w_output, w_hidden, w_down, first_gain, first_shift, second_gain, second_shift = params
    batch = rows.shape[0]
    low_in = low(rows)
    scaling = float(HEAD_DIM) ** (-0.5)

    def split_heads(weight):
        return low_back(low(project(low_in, weight))).reshape(batch, LEN, HEADS, HEAD_DIM)
    queries = split_heads(w_query)
    keys = split_heads(w_key)
    values = split_heads(w_value)
    scores = low_back(jnp.einsum('bqhd,bkhd->bhqk', queries, keys, precision=HIGH) * scaling)
    scores = jnp.where(allowed[:, None], scores, NEGATIVE)
    highest = lax.optimization_barrier(jnp.max(scores, axis=-1, keepdims=True))
    expd = jnp.exp(scores - highest)
    probs = expd / lax.optimization_barrier(jnp.sum(expd, axis=-1, keepdims=True))
    mixed = jnp.einsum('bhqk,bkhd->bqhd', low(probs), values, precision=HIGH).reshape(batch, LEN, D)
    mixed = low_back(low(mixed))
    summed = rows + low_back(project(mixed, w_output))
    normed = norm_rows(summed, first_gain, first_shift)
    hidden = low_back(project(low(normed), w_hidden))
    active = low(jax.nn.gelu(hidden, approximate=True))
    total = normed + low_back(jnp.einsum('blf,fd->bld', active, w_down, precision=HIGH))
    return norm_rows(total, second_gain, second_shift)

def reference(embedded, piece_lengths, pair_tags, pair_embedding, w_query, w_key, w_value, w_output, w_hidden, w_down, first_gain, first_shift, second_gain, second_shift, cotangent):
    params = tuple((a.astype(jnp.float32) for a in (w_query, w_key, w_value, w_output, w_hidden, w_down, first_gain, first_shift, second_gain, second_shift)))
    table = pair_embedding.astype(jnp.float32)
    group_rows = embedded.reshape(N_DP, SEQS, LEN, D)
    group_seed = cotangent.reshape(N_DP, SEQS, LEN, D)
    group_pieces = piece_lengths.reshape(N_DP, SEQS, PIECES)
    group_tags = pair_tags.reshape(N_DP, SEQS)

    def step(carry, item):
        rows, pieces, tags, seed_grad = item
        segment_ids = segments(pieces)
        valid = segment_ids < PIECES - 1
        places = jnp.arange(LEN, dtype=jnp.int32)
        allowed = (segment_ids[:, :, None] == segment_ids[:, None, :]) & (valid[:, None, :] | (places[:, None] == places[None, :])[None])
        pairs = (tags[:, None] == jnp.arange(PAIRS, dtype=jnp.int32)[None, :]).astype(jnp.float32)

        def forward(start_rows, table_in, params_in):
            begin = start_rows + jnp.dot(pairs, table_in, precision=HIGH)[:, None, :]
            return layer(layer(begin, params_in, allowed), params_in, allowed)
        result, pull = jax.vjp(forward, rows, table, params)
        grad_rows, grad_table, grad_params = pull(seed_grad * valid[:, :, None].astype(jnp.float32))
        carry = (carry[0] + grad_table, jax.tree.map(jnp.add, carry[1], grad_params))
        return (carry, (result, grad_rows))
    initial = (jnp.zeros_like(table), tuple((jnp.zeros_like(a) for a in params)))
    (grad_table, grad_params), (results, grads) = lax.scan(step, initial, (group_rows, group_pieces, group_tags, group_seed))
    return (results.reshape(TOKENS, D), grads.reshape(TOKENS, D), grad_table, grad_params[0], grad_params[1], grad_params[2], grad_params[3], grad_params[4], grad_params[5], grad_params[6], grad_params[7], grad_params[8], grad_params[9])
```

```python
import functools
import math

import jax
import jax.numpy as jnp
from jax import lax
from jax.sharding import PartitionSpec as P
from jax.experimental import pallas as pl
from jax.experimental.pallas import tpu as pltpu

HEAD_DIM = 64
LEN = 1024
PIECES = 8
PAIRS = 4
D = 512
FF = 2048
HALF = 256
QB = 128
NQ = LEN // QB
BIG = 1e30
LOG2E = math.log2(math.e)
QSCALE = LOG2E / math.sqrt(HEAD_DIM)
KSCALE = math.log(2.0)
WIDTHS = (1, 2, 3, 4, 5, 6, 8)
EPS = 1e-5
C1 = math.sqrt(2.0 / math.pi)
C2 = C1 * 0.044715
F32 = jnp.float32
BF = jnp.bfloat16
VMEM_LIMIT = 60 * 1024 * 1024


def nn(a, b):
    return jnp.dot(a, b, preferred_element_type=F32)


def nt(a, b):
    return lax.dot_general(a, b, (((1,), (1,)), ((), ())), preferred_element_type=F32)


def tn(a, b):
    return lax.dot_general(a, b, (((0,), (0,)), ((), ())), preferred_element_type=F32)


def piece_ends(pieces_ref):
    ends, at = [], 0
    for j in range(PIECES):
        at = at + pieces_ref[j]
        ends.append(at)
    return ends


def window(block, ends):
    first = block * QB
    last = first + QB - 1
    low, high = jnp.int32(0), jnp.int32(LEN)
    for end in ends[:-1]:
        low = jnp.maximum(low, jnp.where(end <= first, end, 0))
        high = jnp.minimum(high, jnp.where(end > last, end, LEN))
    low = jnp.where(first >= ends[-2], first, low)
    high = jnp.where(last >= ends[-2], last + 1, high)
    return low // QB, (high + QB - 1) // QB


def over_widths(block, ends, run):
    low, high = window(block, ends)
    count = high - low
    previous = 0
    for wide in WIDTHS:
        begin = jnp.minimum(low, NQ - wide)

        @pl.when((count > previous) & (count <= wide))
        def _(wide=wide, begin=begin):
            run(wide, pl.multiple_of(begin * QB, QB))

        previous = wide


def segment_codes(ends, segq_ref, segk_ref):
    rows = lax.broadcasted_iota(jnp.int32, (LEN, 128), 0)
    lanes = lax.broadcasted_iota(jnp.int32, (LEN, 128), 1)
    ids = jnp.zeros((LEN, 128), jnp.int32)
    for end in ends[:-1]:
        ids = ids + jnp.where(rows >= end, 1, 0)
    same = lanes == ids
    segk_ref[...] = jnp.where(same, 1.0, 0.0).astype(BF)
    free = (lanes >= PIECES) | (same & (lanes < PIECES - 1))
    segq_ref[...] = jnp.where(free, 0.0, -BIG).astype(BF)


def lane_half(shape):
    return lax.broadcasted_iota(jnp.int32, shape, 1) < HEAD_DIM


def two_heads(block):
    left = lane_half(block.shape)
    zero = jnp.zeros_like(block)
    return jnp.where(left, block, zero), jnp.where(left, zero, block)


def attend_kernel(pieces_ref, x_ref, w_ref, q_ref, k_ref, v_ref, mixed_ref, exact_ref, inv_ref, p_ref,
                  segq_ref, segk_ref, vt_ref):
    step = pl.program_id(0)
    ends = piece_ends(pieces_ref)

    @pl.when(step == 0)
    def _():
        low = x_ref[...].astype(BF)
        q_ref[...] = (nn(low, w_ref[:, :HALF]) * QSCALE).astype(BF)
        k_ref[...] = nn(low, w_ref[:, HALF:2 * HALF]).astype(BF)
        values = nn(low, w_ref[:, 2 * HALF:])
        v_ref[...] = values.astype(BF)
        for pair in range(2):
            vt_ref[pair, :128, :] = values[:, pair * 128:(pair + 1) * 128].T.astype(BF)
            vt_ref[pair, 128:, :] = jnp.ones((16, LEN), BF)
        segment_codes(ends, segq_ref, segk_ref)

    rows = pl.ds(pl.multiple_of(step * QB, QB), QB)

    def run(wide, begin):
        keys = pl.ds(begin, wide * QB)
        segq = segq_ref[rows, :]
        segk = segk_ref[keys, :]
        pad = lax.broadcasted_iota(jnp.int32, (QB, 128), 0) + step * QB >= ends[-2]
        for pair in range(2):
            cols = slice(pair * 128, (pair + 1) * 128)
            even, odd = two_heads(q_ref[rows, cols])
            query = jnp.concatenate(
                [jnp.concatenate([even, segq], axis=1), jnp.concatenate([odd, segq], axis=1)], axis=0)
            key = jnp.concatenate([k_ref[keys, cols], segk], axis=1)
            scores = nt(key, query)
            top = jnp.max(scores, axis=0, keepdims=True)
            probs = jnp.exp2(scores - top).astype(BF)
            p_ref[0, pair, :wide * QB, :] = probs
            out = nn(vt_ref[pair, :, keys], probs)
            inv = 1.0 / out[128:129, :]
            inv_both = jnp.concatenate(
                [jnp.broadcast_to(inv[:, :128], (64, 128)), jnp.broadcast_to(inv[:, 128:], (64, 128))], axis=0)
            out_both = jnp.concatenate([out[:64, :128], out[64:128, 128:]], axis=0) * inv_both
            exact = out_both.T
            exact_ref[:, cols] = exact
            mixed_ref[:, cols] = jnp.where(pad, v_ref[rows, cols].astype(F32), exact).astype(BF)
            inv_ref[:, cols] = inv_both.T

    over_widths(step, ends, run)


def attend(pieces, x, w):
    whole = lambda i: (0, 0)
    block = lambda i: (i, 0)
    return pl.pallas_call(
        attend_kernel,
        grid=(NQ,),
        in_specs=[
            pl.BlockSpec(memory_space=pltpu.SMEM),
            pl.BlockSpec((LEN, D), whole),
            pl.BlockSpec((D, 3 * HALF), whole),
        ],
        out_specs=[
            pl.BlockSpec((LEN, HALF), whole),
            pl.BlockSpec((LEN, HALF), whole),
            pl.BlockSpec((LEN, HALF), whole),
            pl.BlockSpec((QB, HALF), block),
            pl.BlockSpec((QB, HALF), block),
            pl.BlockSpec((QB, HALF), block),
            pl.BlockSpec((1, 2, LEN, 256), lambda i: (i, 0, 0, 0)),
        ],
        out_shape=[
            jax.ShapeDtypeStruct((LEN, HALF), BF),
            jax.ShapeDtypeStruct((LEN, HALF), BF),
            jax.ShapeDtypeStruct((LEN, HALF), BF),
            jax.ShapeDtypeStruct((LEN, HALF), BF),
            jax.ShapeDtypeStruct((LEN, HALF), F32),
            jax.ShapeDtypeStruct((LEN, HALF), F32),
            jax.ShapeDtypeStruct((NQ, 2, LEN, 256), BF),
        ],
        scratch_shapes=[
            pltpu.VMEM((LEN, 128), BF),
            pltpu.VMEM((LEN, 128), BF),
            pltpu.VMEM((2, 144, LEN), BF),
        ],
        compiler_params=pltpu.CompilerParams(vmem_limit_bytes=VMEM_LIMIT),
    )(pieces, x, w)


def attend_back_kernel(pieces_ref, base_ref, x_ref, w_ref, q_ref, k_ref, v_ref, mixed_ref, grad_ref, p_ref,
                       old_ref, dx_ref, dw_ref, dk_ref, dv_ref, grads_ref, kt_ref):
    step = pl.program_id(0)
    ends = piece_ends(pieces_ref)

    @pl.when(step == 0)
    def _():
        dk_ref[...] = jnp.zeros_like(dk_ref)
        dv_ref[...] = jnp.zeros_like(dv_ref)
        for pair in range(2):
            kt_ref[pair] = k_ref[:, pair * 128:(pair + 1) * 128].astype(F32).T.astype(BF)

    rows = pl.ds(pl.multiple_of(step * QB, QB), QB)

    def run(wide, begin):
        keys = pl.ds(begin, wide * QB)
        for pair in range(2):
            cols = slice(pair * 128, (pair + 1) * 128)
            grad = grad_ref[rows, cols]
            inner = grad.astype(F32) * mixed_ref[rows, cols]
            high = inner.astype(BF)
            rest = pltpu.roll(inner - high.astype(F32), HEAD_DIM, 1).astype(BF)
            left = lane_half(inner.shape)
            inner = jnp.concatenate([jnp.where(left, high, rest), jnp.where(left, rest, high)], axis=0)
            outer = jnp.concatenate(two_heads(grad), axis=0)
            both = jnp.concatenate([outer, inner], axis=1)
            value = jnp.concatenate([v_ref[keys, cols], jnp.full((wide * QB, 128), -1.0, BF)], axis=1)
            probs = p_ref[0, pair, :wide * QB, :]
            slope = nt(value, both)
            scores = (probs.astype(F32) * slope).astype(BF)
            query = jnp.concatenate(two_heads(q_ref[rows, cols]), axis=0)
            dv_ref[pair, keys, :] += nn(probs, outer)
            dk_ref[pair, keys, :] += nn(scores, query)
            out = nn(kt_ref[pair, :, keys], scores)
            out = jnp.concatenate([out[:64, :128], out[64:, 128:]], axis=0)
            grads_ref[rows, cols] = (out.T * (HEAD_DIM ** -0.5)).astype(BF)

    over_widths(step, ends, run)

    @pl.when(step == NQ - 1)
    def _():
        for pair in range(2):
            cols = slice(HALF + pair * 128, HALF + (pair + 1) * 128)
            grads_ref[:, cols] = (dk_ref[pair] * KSCALE).astype(BF)
            cols = slice(2 * HALF + pair * 128, 2 * HALF + (pair + 1) * 128)
            grads_ref[:, cols] = dv_ref[pair].astype(BF)
        low = x_ref[...].astype(BF)
        dw_ref[...] = (tn(low, grads_ref[...]) + old_ref[...].astype(F32)).astype(BF)
        dx_ref[...] = base_ref[...] + nt(grads_ref[...], w_ref[...])


def attend_back(pieces, base, x, w, q, k, v, mixed, grad, p, old):
    whole = lambda i: (0, 0)
    return pl.pallas_call(
        attend_back_kernel,
        grid=(NQ,),
        in_specs=[
            pl.BlockSpec(memory_space=pltpu.SMEM),
            pl.BlockSpec((LEN, D), whole),
            pl.BlockSpec((LEN, D), whole),
            pl.BlockSpec((D, 3 * HALF), whole),
            pl.BlockSpec((LEN, HALF), whole),
            pl.BlockSpec((LEN, HALF), whole),
            pl.BlockSpec((LEN, HALF), whole),
            pl.BlockSpec((LEN, HALF), whole),
            pl.BlockSpec((LEN, HALF), whole),
            pl.BlockSpec((1, 2, LEN, 256), lambda i: (i, 0, 0, 0)),
            pl.BlockSpec((D, 3 * HALF), whole),
        ],
        out_specs=[pl.BlockSpec((LEN, D), whole), pl.BlockSpec((D, 3 * HALF), whole)],
        out_shape=[jax.ShapeDtypeStruct((LEN, D), F32), jax.ShapeDtypeStruct((D, 3 * HALF), BF)],
        scratch_shapes=[
            pltpu.VMEM((2, LEN, 128), F32),
            pltpu.VMEM((2, LEN, 128), F32),
            pltpu.VMEM((LEN, 3 * HALF), BF),
            pltpu.VMEM((2, 128, LEN), BF),
        ],
        compiler_params=pltpu.CompilerParams(vmem_limit_bytes=VMEM_LIMIT),
    )(pieces, base, x, w, q, k, v, mixed, grad, p, old)


TM = 256


def unit_rows(values):
    center = values - jnp.mean(values, axis=-1, keepdims=True)
    spread = jnp.mean(center * center, axis=-1, keepdims=True)
    inv = lax.rsqrt(spread + EPS)
    return center * inv, inv


def feed_kernel(x_ref, ma_ref, mb_ref, wo_ref, wh_ref, wd_ref, par_ref, out_ref, unit1_ref, inv1_ref,
                norm_ref, act_ref, slope_ref, unit2_ref, inv2_ref):
    summed = x_ref[...] + nt(ma_ref[...], wo_ref[:, :HALF]) + nt(mb_ref[...], wo_ref[:, HALF:])
    unit, inv = unit_rows(summed)
    unit1_ref[...] = unit.astype(BF)
    inv1_ref[...] = inv
    normed = unit * par_ref[0:1, :] + par_ref[1:2, :]
    low = normed.astype(BF)
    norm_ref[...] = low
    for at in range(0, FF, 512):
        cols = slice(at, at + 512)
        hidden = nn(low, wh_ref[:, cols])
        square = hidden * hidden
        gate = 0.5 + 0.5 * jnp.tanh(hidden * (C1 + C2 * square))
        act_ref[:, cols] = (hidden * gate).astype(BF)
        slope_ref[:, cols] = (gate + gate * (1.0 - gate) * hidden * (2 * C1 + 6 * C2 * square)).astype(BF)
    total = normed + nt(act_ref[...], wd_ref[...])
    unit, inv = unit_rows(total)
    unit2_ref[...] = unit.astype(BF)
    inv2_ref[...] = inv
    out_ref[...] = unit * par_ref[2:3, :] + par_ref[3:4, :]


def feed(x, ma, mb, wo, wh, wd, par):
    whole = lambda i: (0, 0)
    block = lambda i: (i, 0)
    wide = [(D, F32), (D, BF), (1, F32), (D, BF), (FF, BF), (FF, BF), (D, BF), (1, F32)]
    return pl.pallas_call(
        feed_kernel,
        grid=(LEN // TM,),
        in_specs=[
            pl.BlockSpec((TM, D), block),
            pl.BlockSpec((TM, HALF), block),
            pl.BlockSpec((TM, HALF), block),
            pl.BlockSpec((D, D), whole),
            pl.BlockSpec((D, FF), whole),
            pl.BlockSpec((D, FF), whole),
            pl.BlockSpec((8, D), whole),
        ],
        out_specs=[pl.BlockSpec((TM, w), block) for w, _ in wide],
        out_shape=[jax.ShapeDtypeStruct((LEN, w), t) for w, t in wide],
        compiler_params=pltpu.CompilerParams(vmem_limit_bytes=VMEM_LIMIT),
    )(x, ma, mb, wo, wh, wd, par)


def unit_back(grad, unit, inv, gain):
    scaled = grad * gain
    first = jnp.mean(scaled, axis=-1, keepdims=True)
    second = jnp.mean(scaled * unit, axis=-1, keepdims=True)
    return inv * (scaled - first - unit * second)


def fold_rows(values):
    return jnp.sum(values.reshape(-1, 8, values.shape[-1]), axis=0)


def feed_back_kernel(grad_ref, unit1_ref, inv1_ref, norm_ref, act_ref, slope_ref, unit2_ref, inv2_ref,
                     ma_ref, mb_ref, ia_ref, ib_ref, wo_ref, wh_ref, wd_ref, par_ref,
                     old_d_ref, old_h_ref, old_o_ref,
                     base_ref, ga_ref, gb_ref, dd_ref, dh_ref, do_ref, small_ref,
                     acc_d_ref, acc_h_ref, acc_o_ref):
    step = pl.program_id(0)

    @pl.when(step == 0)
    def _():
        acc_d_ref[...] = old_d_ref[...].astype(F32)
        acc_h_ref[...] = old_h_ref[...].astype(F32)
        acc_o_ref[...] = old_o_ref[...].astype(F32)
        small_ref[...] = jnp.zeros_like(small_ref)

    grad = grad_ref[...]
    unit2 = unit2_ref[...].astype(F32)
    small_ref[16:24, :] += fold_rows(grad * unit2)
    small_ref[24:32, :] += fold_rows(grad)
    total = unit_back(grad, unit2, inv2_ref[...], par_ref[2:3, :])
    low = total.astype(BF)
    normed = total
    for at in range(0, FF, 512):
        cols = slice(at, at + 512)
        acc_d_ref[:, cols] += tn(low, act_ref[:, cols])
        hidden = (nn(low, wd_ref[:, cols]) * slope_ref[:, cols].astype(F32)).astype(BF)
        acc_h_ref[:, cols] += tn(norm_ref[...], hidden)
        normed = normed + nt(hidden, wh_ref[:, cols])
    unit1 = unit1_ref[...].astype(F32)
    small_ref[0:8, :] += fold_rows(normed * unit1)
    small_ref[8:16, :] += fold_rows(normed)
    summed = unit_back(normed, unit1, inv1_ref[...], par_ref[0:1, :])
    base_ref[...] = summed
    low = summed.astype(BF)
    acc_o_ref[:, :HALF] += tn(low, ma_ref[...])
    acc_o_ref[:, HALF:] += tn(low, mb_ref[...])
    ga_ref[...] = (nn(low, wo_ref[:, :HALF]) * ia_ref[...]).astype(BF)
    gb_ref[...] = (nn(low, wo_ref[:, HALF:]) * ib_ref[...]).astype(BF)

    @pl.when(step == LEN // TM - 1)
    def _():
        dd_ref[...] = acc_d_ref[...].astype(BF)
        dh_ref[...] = acc_h_ref[...].astype(BF)
        do_ref[...] = acc_o_ref[...].astype(BF)


def feed_back(grad, saved, ma, mb, ia, ib, wo, wh, wd, par, old):
    whole = lambda i: (0, 0)
    block = lambda i: (i, 0)
    ins = [(D, F32), (D, BF), (1, F32), (D, BF), (FF, BF), (FF, BF), (D, BF), (1, F32),
           (HALF, BF), (HALF, BF), (HALF, F32), (HALF, F32)]
    big = [pl.BlockSpec((D, FF), whole), pl.BlockSpec((D, FF), whole), pl.BlockSpec((D, D), whole)]
    return pl.pallas_call(
        feed_back_kernel,
        grid=(LEN // TM,),
        in_specs=[pl.BlockSpec((TM, w), block) for w, _ in ins]
        + [pl.BlockSpec((D, D), whole), pl.BlockSpec((D, FF), whole), pl.BlockSpec((D, FF), whole),
           pl.BlockSpec((8, D), whole)] + big,
        out_specs=[pl.BlockSpec((TM, D), block), pl.BlockSpec((TM, HALF), block), pl.BlockSpec((TM, HALF), block)]
        + big + [pl.BlockSpec((32, D), whole)],
        out_shape=[
            jax.ShapeDtypeStruct((LEN, D), F32),
            jax.ShapeDtypeStruct((LEN, HALF), BF),
            jax.ShapeDtypeStruct((LEN, HALF), BF),
            jax.ShapeDtypeStruct((D, FF), BF),
            jax.ShapeDtypeStruct((D, FF), BF),
            jax.ShapeDtypeStruct((D, D), BF),
            jax.ShapeDtypeStruct((32, D), F32),
        ],
        scratch_shapes=[pltpu.VMEM((D, FF), F32), pltpu.VMEM((D, FF), F32), pltpu.VMEM((D, D), F32)],
        compiler_params=pltpu.CompilerParams(vmem_limit_bytes=VMEM_LIMIT),
    )(grad, *saved, ma, mb, ia, ib, wo, wh, wd, par, *old)


GROUP = ("dp", "tensor")
FIRST = 3 * HALF + 128
REST = HALF + FF


def plan(dp):
    if dp == 16:
        return (8, 4, 1, 2), (8, 4, 2, 1)
    bits = [1 << i for i in range(dp.bit_length() - 1)]
    side = len(bits) // 3
    x, y, z = bits[:side], bits[side:2 * side], bits[2 * side:]
    return tuple(z[::-1] + x[::-1] + y[::-1]), tuple(z[::-1] + y[::-1] + x[::-1])


def flip(value, dp, masks):
    pairs = [(d * 2 + t, (d ^ masks[t]) * 2 + t) for d in range(dp) for t in range(2)]
    return lax.ppermute(value, GROUP, pairs)


def swap(value):
    return lax.ppermute(value, "tensor", [(0, 1), (1, 0)])


def gather(own, dp):
    held = own[None]
    for masks in zip(*plan(dp)):
        held = jnp.concatenate([held, flip(held, dp, masks)], axis=0)
    return held


def places(dp, mine, tensor, last_first):
    rel = jnp.arange(dp, dtype=jnp.int32) ^ mine
    found = []
    for order in plan(dp):
        at = jnp.zeros((dp,), jnp.int32)
        for i, mask in enumerate(order):
            bit = (rel & mask) // mask
            at = at + bit * (1 << (i if not last_first else i))
        found.append(at)
    return jnp.where(tensor == 0, found[0], found[1])


def order_kernel(dp, spans, at_ref, own_ref, other_ref, *refs):
    outs, sem = refs[:-1], refs[-1]
    copies = []
    rows = D // dp
    for b in range(dp):
        for half, ref in enumerate((own_ref, other_ref)):
            for out, (out_half, begin, width, to) in zip([outs[s[0]] for s in spans], [s[1:] for s in spans]):
                if out_half != half:
                    continue
                copies.append(pltpu.make_async_copy(
                    ref.at[at_ref[half, b], :, pl.ds(begin, width)],
                    out.at[pl.ds(b * rows, rows), pl.ds(to, width)], sem.at[len(copies)]))
    for c in copies:
        c.start()
    for c in copies:
        c.wait()


def order(at, own, other, spans, widths):
    dp = own.shape[0]
    return pl.pallas_call(
        functools.partial(order_kernel, dp, spans),
        in_specs=[pl.BlockSpec(memory_space=pltpu.SMEM), pl.BlockSpec(memory_space=pl.ANY),
                  pl.BlockSpec(memory_space=pl.ANY)],
        out_specs=[pl.BlockSpec(memory_space=pl.ANY)] * len(widths),
        out_shape=[jax.ShapeDtypeStruct((D, w), BF) for w in widths],
        scratch_shapes=[pltpu.SemaphoreType.DMA((dp * len(spans),))],
    )(at, own, other)


def reduce(keep, send, dp):
    held = add(keep, swap(send))
    phases = list(zip(*plan(dp)))[::-1]
    for i, masks in enumerate(phases):
        half = held.shape[0] // 2
        arrived = flip(held[half:], dp, masks)
        held = add(held[:half], arrived, F32 if i == len(phases) - 1 else BF)
    return held[0]


def add(a, b, kind=BF):
    return (a.astype(F32) + b.astype(F32)).astype(kind)


def body(embedded, piece_lengths, pair_tags, pair_embedding, w_query, w_key, w_value, w_output, w_hidden,
         w_down, first_gain, first_shift, second_gain, second_shift, cotangent):
    dp = lax.axis_size("dp")
    mine, tensor = lax.axis_index("dp"), lax.axis_index("tensor")
    rows = D // dp
    pieces = lax.dynamic_index_in_dim(piece_lengths, tensor, 0, keepdims=False)
    tag = lax.dynamic_index_in_dim(pair_tags, tensor, 0, keepdims=False)
    small = jnp.stack([first_gain, first_shift, second_gain, second_shift], axis=1)
    small = jnp.concatenate([small, pair_embedding.T, jnp.zeros((rows, 120), BF)], axis=1)
    first = gather(jnp.concatenate([w_query, w_key, w_value, small], axis=1), dp)
    rest = gather(jnp.concatenate([w_output.T, w_hidden, w_down.T], axis=1), dp)
    at = jnp.stack([places(dp, mine, tensor, False), places(dp, mine, 1 - tensor, False)])
    wa, wb, small = order(at, first, swap(first),
                          ((0, 0, 0, 3 * HALF, 0), (1, 1, 0, 3 * HALF, 0), (2, 0, 3 * HALF, 128, 0)),
                          (3 * HALF, 3 * HALF, 128))
    wo, wh, wd = order(at, rest, swap(rest),
                       ((0, 0, 0, HALF, 0), (0, 1, 0, HALF, HALF),
                        (1, 0, HALF, FF // 2, 0), (1, 1, HALF, FF // 2, FF // 2),
                        (2, 0, HALF + FF // 2, FF // 2, 0), (2, 1, HALF + FF // 2, FF // 2, FF // 2)),
                       (D, FF, FF))
    par = small[:, :8].T.astype(F32)
    tags = jnp.arange(PAIRS, dtype=jnp.int32) == tag
    start = embedded + jnp.sum(jnp.where(tags[:, None], par[4:], 0.0), axis=0)[None]

    def forward(x):
        qa, ka, va, ma, ea, ia, pa = attend(pieces, x, wa)
        qb, kb, vb, mb, eb, ib, pb = attend(pieces, x, wb)
        out, *saved = feed(x, ma, mb, wo, wh, wd, par)
        return out, (x, (qa, ka, va), (qb, kb, vb), (ma, mb), (ea, eb), (ia, ib), (pa, pb), saved)

    def backward(grad, kept, old):
        x, ha, hb, mixed, exact, inv, probs, saved = kept
        base, ga, gb, dd, dh, do, stats = feed_back(grad, saved, *mixed, *inv, wo, wh, wd, par, old[:3])
        base, da = attend_back(pieces, base, x, wa, *ha, exact[0], ga, probs[0], old[3])
        base, db = attend_back(pieces, base, x, wb, *hb, exact[1], gb, probs[1], old[4])
        return base, (dd, dh, do, da, db), stats

    hidden, kept_first = forward(start)
    result, kept_second = forward(hidden)
    valid = jnp.arange(LEN, dtype=jnp.int32)[:, None] < jnp.sum(pieces[:-1])
    zeros = lambda n: jnp.zeros((D, n), BF)
    old = (zeros(FF), zeros(FF), zeros(D), zeros(3 * HALF), zeros(3 * HALF))
    grad, old, stats_second = backward(jnp.where(valid, cotangent, 0.0), kept_second, old)
    grad, new, stats_first = backward(grad, kept_first, old)
    dd, dh, do, da, db = new
    stats = (stats_first + stats_second).reshape(4, 8, D).sum(axis=1)
    table = jnp.where(tags[:, None], jnp.sum(grad, axis=0)[None], 0.0)
    stats = jnp.concatenate([stats, table], axis=0).T.astype(BF)
    stats = jnp.concatenate([stats, jnp.zeros((D, 120), BF)], axis=1)

    def blocks(value, partner):
        to = places(dp, mine, 1 - tensor if partner else tensor, True)
        back = jnp.zeros((dp,), jnp.int32).at[to].set(jnp.arange(dp, dtype=jnp.int32))
        return value.reshape(dp, rows, -1)[back]

    half = FF // 2
    keep = jnp.concatenate([do[:, :HALF], dh[:, :half], dd[:, :half]], axis=1)
    send = jnp.concatenate([do[:, HALF:], dh[:, half:], dd[:, half:]], axis=1)
    total = reduce(blocks(keep, False), blocks(send, True), dp)
    do, dh, dd = total[:, :HALF], total[:, HALF:HALF + half], total[:, HALF + half:]
    total = reduce(blocks(jnp.concatenate([da, stats], axis=1), False),
                   blocks(jnp.concatenate([db, stats], axis=1), True), dp)
    small = total[:, 3 * HALF:3 * HALF + 8].T
    return (result, grad, small[4:], total[:, :HALF], total[:, HALF:2 * HALF], total[:, 2 * HALF:3 * HALF],
            do.T, dh, dd.T, small[0], small[1], small[2], small[3])


def solution(mesh):
    both = P(GROUP, None)
    params = (P("dp", "tensor"),) * 3 + (P("tensor", "dp"), P("dp", "tensor"), P("tensor", "dp"))
    in_specs = (both, P("dp", None), P("dp"), P(None, "dp")) + params + (P("dp"),) * 4 + (both,)
    out_specs = (both, both, P(None, "dp")) + params + (P("dp"),) * 4
    return jax.shard_map(body, mesh=mesh, in_specs=in_specs, out_specs=out_specs, check_vma=False)
```

```python
import functools
import math

import jax
import jax.numpy as jnp
from jax import lax
from jax.sharding import PartitionSpec as P
from jax.experimental import pallas as pl
from jax.experimental.pallas import tpu as pltpu

HEAD_DIM = 64
LEN = 1024
PIECES = 8
PAIRS = 4
D = 512
FF = 2048
HALF = 256
HEADS2 = 4
QB = 256
KB = 128
NQ = LEN // QB
NK = LEN // KB
BIG = 1e30
LOG2E = math.log2(math.e)
QSCALE = LOG2E / math.sqrt(HEAD_DIM)
KSCALE = math.log(2.0)
WIDTHS = (2, 3, 4, 5, 6, 7, 8)
EPS = 1e-5
C1 = math.sqrt(2.0 / math.pi)
C2 = C1 * 0.044715
F32 = jnp.float32
BF = jnp.bfloat16
VMEM_LIMIT = 60 * 1024 * 1024
TM = 256


def nn(a, b):
    return jnp.dot(a, b, preferred_element_type=F32)


def nt(a, b):
    return lax.dot_general(a, b, (((1,), (1,)), ((), ())), preferred_element_type=F32)


def tn(a, b):
    return lax.dot_general(a, b, (((0,), (0,)), ((), ())), preferred_element_type=F32)


def piece_ends(pieces_ref):
    ends, at = [], 0
    for j in range(PIECES):
        at = at + pieces_ref[j]
        ends.append(at)
    return ends


def window(block, ends):
    first = block * QB
    last = first + QB - 1
    low, high = jnp.int32(0), jnp.int32(LEN)
    for end in ends[:-1]:
        low = jnp.maximum(low, jnp.where(end <= first, end, 0))
        high = jnp.minimum(high, jnp.where(end > last, end, LEN))
    low = jnp.where(first >= ends[-2], first, low)
    high = jnp.where(last >= ends[-2], last + 1, high)
    return low // KB, (high + KB - 1) // KB


def over_widths(block, ends, run):
    low, high = window(block, ends)
    count = high - low
    previous = 0
    for wide in WIDTHS:
        begin = jnp.minimum(low, NK - wide)

        @pl.when((count > previous) & (count <= wide))
        def _(wide=wide, begin=begin):
            run(wide, pl.multiple_of(begin * KB, KB))

        previous = wide


def segment_codes(ends, segq_ref, segk_ref):
    rows = lax.broadcasted_iota(jnp.int32, (LEN, 128), 0)
    lanes = lax.broadcasted_iota(jnp.int32, (LEN, 128), 1)
    ids = jnp.zeros((LEN, 128), jnp.int32)
    for end in ends[:-1]:
        ids = ids + jnp.where(rows >= end, 1, 0)
    same = lanes == ids
    segk_ref[...] = jnp.where(same, 1.0, 0.0).astype(BF)
    free = (lanes >= PIECES) | (same & (lanes < PIECES - 1))
    segq_ref[...] = jnp.where(free, 0.0, -BIG).astype(BF)


def lane_half(shape):
    return lax.broadcasted_iota(jnp.int32, shape, 1) < HEAD_DIM


def two_heads(block):
    left = lane_half(block.shape)
    zero = jnp.zeros_like(block)
    return jnp.where(left, block, zero), jnp.where(left, zero, block)


def block_rows(index, size):
    return pl.ds(pl.multiple_of(index * size, size), size)


def head_norms(values, half):
    heads = lax.broadcasted_iota(jnp.int32, (HALF, 128), 0) // HEAD_DIM + half * (HALF // HEAD_DIM)
    pick = jnp.where(heads == lax.broadcasted_iota(jnp.int32, (HALF, 128), 1), 1.0, 0.0).astype(BF)
    return jnp.max(nn((values * values).astype(BF), pick), axis=0, keepdims=True)


def project_stage(x_ref, w_refs, q_ref, k_ref, v_ref, vt_ref):
    def chunk(i, carry):
        rows = block_rows(i, TM)
        low = x_ref[rows, :]
        q_top, k_top = carry
        for half in range(2):
            cols = slice(half * HALF, (half + 1) * HALF)
            queries = nn(low, w_refs[half][:, :HALF]) * QSCALE
            keys = nn(low, w_refs[half][:, HALF:2 * HALF])
            q_ref[rows, cols] = queries.astype(BF)
            k_ref[rows, cols] = keys.astype(BF)
            q_top = jnp.maximum(q_top, head_norms(queries, half))
            k_top = jnp.maximum(k_top, head_norms(keys, half))
            values = nn(low, w_refs[half][:, 2 * HALF:])
            v_ref[rows, cols] = values.astype(BF)
            for pair in range(2):
                vt_ref[half * 2 + pair, :128, rows] = values[:, pair * 128:(pair + 1) * 128].T.astype(BF)
        return q_top, k_top

    zero = jnp.zeros((1, 128), F32)
    q_top, k_top = lax.fori_loop(0, LEN // TM, chunk, (zero, zero))
    for pair in range(HEADS2):
        vt_ref[pair, 128:, :] = jnp.ones((16, LEN), BF)
    return jnp.max(q_top * k_top)


def probs_copy(p_slots, p_ref, sem, i, wide):
    slot = i % 2
    return pltpu.make_async_copy(p_slots.at[slot, :, pl.ds(0, wide * KB), :],
                                 p_ref.at[i, :, pl.ds(0, wide * KB), :], sem.at[slot])


def attend_stage(ends, shifted, q_ref, k_ref, v_ref, vt_ref, segq_ref, segk_ref, mixed_ref, exact_ref, inv_ref,
                 p_slots, p_out, p_sem):
    def block(i, carry):
        rows = block_rows(i, QB)
        p_ref = p_slots.at[i % 2]

        @pl.when(i >= 2)
        def _():
            over_widths(i - 2, ends, lambda wide, begin: probs_copy(p_slots, p_out, p_sem, i - 2, wide).wait())

        def run(wide, begin):
            keys = pl.ds(begin, wide * KB)
            segq = segq_ref[rows, :]
            segk = segk_ref[keys, :]
            pad = lax.broadcasted_iota(jnp.int32, (QB, 128), 0) + i * QB >= ends[-2]
            span = [slice(pair * 128, (pair + 1) * 128) for pair in range(HEADS2)]

            def score(pair):
                even, odd = two_heads(q_ref[rows, span[pair]])
                query = jnp.concatenate(
                    [jnp.concatenate([even, segq], axis=1), jnp.concatenate([odd, segq], axis=1)], axis=0)
                key = jnp.concatenate([k_ref[keys, span[pair]], segk], axis=1)
                return nt(key, query)

            def soften(pair, scores):
                if shifted:
                    scores = scores - jnp.max(scores, axis=0, keepdims=True)
                probs = jnp.exp2(scores).astype(BF)
                p_ref[pair, :wide * KB, :] = probs
                return probs

            def mix(pair, probs):
                return nn(vt_ref[pair, :, keys], probs)

            def finish(pair, out):
                cols = span[pair]
                inv = 1.0 / jnp.maximum(out[128:129, :], 1e-30)
                inv_both = jnp.concatenate(
                    [jnp.broadcast_to(inv[:, :QB], (64, QB)), jnp.broadcast_to(inv[:, QB:], (64, QB))], axis=0)
                out_both = jnp.concatenate([out[:64, :QB], out[64:128, QB:]], axis=0) * inv_both
                exact = out_both.T
                exact_ref[rows, cols] = exact
                mixed_ref[rows, cols] = jnp.where(pad, v_ref[rows, cols].astype(F32), exact).astype(BF)
                inv_ref[rows, cols] = inv_both.T

            s = {0: score(0), 1: score(1)}
            p, o = {}, {}
            for pair in range(HEADS2):
                p[pair] = soften(pair, s[pair])
                if pair + 2 < HEADS2:
                    s[pair + 2] = score(pair + 2)
                if pair:
                    o[pair - 1] = mix(pair - 1, p[pair - 1])
                if pair > 1:
                    finish(pair - 2, o[pair - 2])
            probs_copy(p_slots, p_out, p_sem, i, wide).start()
            o[HEADS2 - 1] = mix(HEADS2 - 1, p[HEADS2 - 1])
            finish(HEADS2 - 2, o[HEADS2 - 2])
            finish(HEADS2 - 1, o[HEADS2 - 1])

        over_widths(i, ends, run)
        return carry

    lax.fori_loop(0, NQ, block, 0)
    for i in range(NQ - 2, NQ):
        over_widths(i, ends, lambda wide, begin, i=i: probs_copy(p_slots, p_out, p_sem, i, wide).wait())


def probs_fetch(p_in, p_slots, sem, i, wide):
    return pltpu.make_async_copy(p_in.at[i, :, pl.ds(0, wide * KB), :],
                                 p_slots.at[i, :, pl.ds(0, wide * KB), :], sem.at[i])


def probs_start(ends, p_in, p_slots, sem):
    for i in range(NQ):
        over_widths(i, ends, lambda wide, begin, i=i: probs_fetch(p_in, p_slots, sem, i, wide).start())


def attend_back_stage(ends, q_ref, k_ref, v_ref, kt_ref, exact_ref, grad_ref, p_in, p_slots, p_sem,
                      dk_ref, dv_ref, grads_ref):
    dk_ref[...] = jnp.zeros_like(dk_ref)
    dv_ref[...] = jnp.zeros_like(dv_ref)
    for pair in range(HEADS2):
        kt_ref[pair] = k_ref[:, pair * 128:(pair + 1) * 128].astype(F32).T.astype(BF)
    span = [slice(pair * 128, (pair + 1) * 128) for pair in range(HEADS2)]

    def block(i, carry):
        rows = block_rows(i, QB)
        p_ref = p_slots.at[i]

        def run(wide, begin):
            keys = pl.ds(begin, wide * KB)
            probs_fetch(p_in, p_slots, p_sem, i, wide).wait()

            def outer(pair):
                return jnp.concatenate(two_heads(grad_ref[rows, span[pair]]), axis=0)

            def slope(pair):
                grad = grad_ref[rows, span[pair]]
                inner = grad.astype(F32) * exact_ref[rows, span[pair]]
                high = inner.astype(BF)
                rest = pltpu.roll(inner - high.astype(F32), HEAD_DIM, 1).astype(BF)
                left = lane_half(inner.shape)
                inner = jnp.concatenate([jnp.where(left, high, rest), jnp.where(left, rest, high)], axis=0)
                both = jnp.concatenate([outer(pair), inner], axis=1)
                value = jnp.concatenate([v_ref[keys, span[pair]], jnp.full((wide * KB, 128), -1.0, BF)], axis=1)
                return nt(value, both)

            def bend(pair, slope):
                return (p_ref[pair, :wide * KB, :].astype(F32) * slope).astype(BF)

            def values(pair):
                dv_ref[pair, keys, :] += nn(p_ref[pair, :wide * KB, :], outer(pair))

            def rest(pair, scores):
                query = jnp.concatenate(two_heads(q_ref[rows, span[pair]]), axis=0)
                dk_ref[pair, keys, :] += nn(scores, query)
                out = nn(kt_ref[pair, :, keys], scores)
                out = jnp.concatenate([out[:64, :QB], out[64:, QB:]], axis=0)
                grads_ref[rows, span[pair]] = (out.T * (HEAD_DIM ** -0.5)).astype(BF)

            s = {0: slope(0), 1: slope(1)}
            d = {}
            for pair in range(HEADS2):
                d[pair] = bend(pair, s[pair])
                values(pair)
                if pair + 2 < HEADS2:
                    s[pair + 2] = slope(pair + 2)
                if pair:
                    rest(pair - 1, d[pair - 1])
            rest(HEADS2 - 1, d[HEADS2 - 1])

        over_widths(i, ends, run)
        return carry

    lax.fori_loop(0, NQ, block, 0)
    for pair in range(HEADS2):
        grads_ref[:, D + pair * 128:D + (pair + 1) * 128] = (dk_ref[pair] * KSCALE).astype(BF)
        grads_ref[:, 2 * D + pair * 128:2 * D + (pair + 1) * 128] = dv_ref[pair].astype(BF)


def unit_rows(values):
    center = values - jnp.mean(values, axis=-1, keepdims=True)
    spread = jnp.mean(center * center, axis=-1, keepdims=True)
    inv = lax.rsqrt(spread + EPS)
    return center * inv, inv


def feed_stage(x_ref, mixed_ref, wo_ref, wh_ref, wd_ref, par_ref, out_ref, unit1_ref, inv1_ref,
               norm_ref, act_ref, slope_ref, unit2_ref, inv2_ref, tm=512):
    def chunk(i, carry):
        rows = block_rows(i, tm)
        summed = x_ref[rows, :] + nt(mixed_ref[rows, :], wo_ref[...])
        unit, inv = unit_rows(summed)
        unit1_ref[rows, :] = unit.astype(BF)
        inv1_ref[rows, :] = inv
        normed = unit * par_ref[0:1, :] + par_ref[1:2, :]
        low = normed.astype(BF)
        norm_ref[rows, :] = low
        total = normed
        for at in range(0, FF, 512):
            cols = slice(at, at + 512)
            hidden = nn(low, wh_ref[:, cols])
            square = hidden * hidden
            gate = 0.5 + 0.5 * jnp.tanh(hidden * (C1 + C2 * square))
            act = (hidden * gate).astype(BF)
            act_ref[rows, cols] = act
            slope_ref[rows, cols] = (gate + gate * (1.0 - gate) * hidden * (2 * C1 + 6 * C2 * square)).astype(BF)
        total = normed + nt(act_ref[rows, :], wd_ref[...])
        unit, inv = unit_rows(total)
        unit2_ref[rows, :] = unit.astype(BF)
        inv2_ref[rows, :] = inv
        out_ref[rows, :] = unit * par_ref[2:3, :] + par_ref[3:4, :]
        return carry

    lax.fori_loop(0, LEN // tm, chunk, 0)


def unit_back(grad, unit, inv, gain):
    scaled = grad * gain
    first = jnp.mean(scaled, axis=-1, keepdims=True)
    second = jnp.mean(scaled * unit, axis=-1, keepdims=True)
    return inv * (scaled - first - unit * second)


def fold_rows(values):
    return jnp.sum(values.reshape(-1, 8, values.shape[-1]), axis=0)


def total_stage(limit, grad_ref, unit2_ref, inv2_ref, par_ref, total_ref, low_ref, small_ref, tm=512):
    small_ref[...] = jnp.zeros_like(small_ref)

    def chunk(i, carry):
        rows = block_rows(i, tm)
        grad = grad_ref[rows, :]
        if limit is not None:
            grad = jnp.where(lax.broadcasted_iota(jnp.int32, grad.shape, 0) + i * tm < limit, grad, 0.0)
        unit2 = unit2_ref[rows, :].astype(F32)
        small_ref[16:24, :] += fold_rows(grad * unit2)
        small_ref[24:32, :] += fold_rows(grad)
        total = unit_back(grad, unit2, inv2_ref[rows, :], par_ref[2:3, :])
        total_ref[rows, :] = total
        low_ref[rows, :] = total.astype(BF)
        return carry

    lax.fori_loop(0, LEN // tm, chunk, 0)


def feed_back_stage(total_ref, low_ref, unit1_ref, inv1_ref, slope_ref, inv_ref, wo_ref, wh_ref, wd_ref, par_ref,
                    base_ref, gm_ref, small_ref, hid_ref, att_ref, tm=512):
    def chunk(i, carry):
        rows = block_rows(i, tm)
        low = low_ref[rows, :]
        for at in range(0, FF, 512):
            cols = slice(at, at + 512)
            hid_ref[rows, cols] = (nn(low, wd_ref[:, cols]) * slope_ref[rows, cols].astype(F32)).astype(BF)
        normed = total_ref[rows, :] + nt(hid_ref[rows, :], wh_ref[...])
        unit1 = unit1_ref[rows, :].astype(F32)
        small_ref[0:8, :] += fold_rows(normed * unit1)
        small_ref[8:16, :] += fold_rows(normed)
        summed = unit_back(normed, unit1, inv1_ref[rows, :], par_ref[0:1, :])
        base_ref[rows, :] = summed
        low = summed.astype(BF)
        att_ref[rows, :] = low
        gm_ref[rows, :] = (nn(low, wo_ref[...]) * inv_ref[rows, :]).astype(BF)
        return carry

    lax.fori_loop(0, LEN // tm, chunk, 0)


def weight_stage(left_ref, right_ref, old_ref, out_ref, width=512):
    def chunk(i, carry):
        cols = block_rows(i, width)
        value = tn(left_ref[...], right_ref[:, cols])
        if old_ref is not None:
            value = value + old_ref[:, cols].astype(F32)
        out_ref[:, cols] = value.astype(BF)
        return carry

    lax.fori_loop(0, out_ref.shape[1] // width, chunk, 0)


def input_stage(base_ref, grads_ref, w_refs, out_ref):
    def chunk(i, carry):
        rows = block_rows(i, TM)
        value = base_ref[rows, :]
        for half in range(2):
            for part in range(3):
                value = value + nt(grads_ref[rows, part * D + half * HALF:part * D + (half + 1) * HALF],
                                   w_refs[half][:, part * HALF:(part + 1) * HALF])
        out_ref[rows, :] = value
        return carry

    lax.fori_loop(0, LEN // TM, chunk, 0)


LIMIT = 64.0 ** 2
P_SHAPE = (NQ, HEADS2, LEN, 2 * QB)
VMEM = pltpu.VMEM


class Moves:
    def __init__(self, sem):
        self.sem, self.count, self.open = sem, 0, []

    def fetch(self, source, target):
        copy = pltpu.make_async_copy(source, target, self.sem.at[self.count])
        self.count += 1
        copy.start()
        return copy

    def send(self, source, target):
        self.open.append(self.fetch(source, target))

    def finish(self):
        for copy in self.open:
            copy.wait()


def wait(*copies):
    for copy in copies:
        copy.wait()


def rows_in(moves, at_ref, half, source, target, begin, width, to):
    if len(source.shape) == 2:
        return [moves.fetch(source.at[:, pl.ds(begin, width)], target.at[:, pl.ds(to, width)])]
    dp, rows, _ = source.shape
    return [moves.fetch(source.at[at_ref[half, b], :, pl.ds(begin, width)],
                        target.at[pl.ds(b * rows, rows), pl.ds(to, width)]) for b in range(dp)]


def rows_out(moves, to_ref, half, source, begin, width, target, to):
    if len(target.shape) == 2:
        moves.send(source.at[:, pl.ds(begin, width)], target.at[:, pl.ds(to, width)])
        return
    dp, rows, _ = target.shape
    for b in range(dp):
        moves.send(source.at[pl.ds(b * rows, rows), pl.ds(begin, width)],
                   target.at[to_ref[half, b], :, pl.ds(to, width)])


ANY = pl.BlockSpec(memory_space=pl.ANY)
SMEM = pl.BlockSpec(memory_space=pltpu.SMEM)


def shaped(*shapes):
    return [jax.ShapeDtypeStruct(s, t) for s, t in shapes]


def like(shapes):
    return [VMEM(s, t) for s, t in shapes]


def full(width, kind=BF):
    return ((LEN, width), kind)


ATTEND_OUT = (full(D), full(D), full(D), full(D), full(D, F32), full(D, F32))
ATTEND_WORK = [VMEM((HEADS2, 144, LEN), BF), VMEM((LEN, 128), BF), VMEM((LEN, 128), BF),
               VMEM((2,) + P_SHAPE[1:], BF), pltpu.SemaphoreType.DMA((2,))]


def attend_whole(ends, moves, low_s, weights, outs, scratch, p_out, work):
    q, k, v, mixed, exact, inv = scratch
    vt, segq, segk, p_slots, p_sem = work
    bound = project_stage(low_s, weights, q, k, v, vt)
    for i in range(3):
        moves.send(scratch[i], outs[i])
    for shifted in (False, True):
        @pl.when((bound > LIMIT) if shifted else (bound <= LIMIT))
        def _(shifted=shifted):
            attend_stage(ends, shifted, q, k, v, vt, segq, segk, mixed, exact, inv, p_slots, p_out, p_sem)
    for i in range(3, 6):
        moves.send(scratch[i], outs[i])


def call(kernel, ins, outs, scratch, sems, flops, *args):
    smem = sum(a.dtype == jnp.int32 for a in args)
    return pl.pallas_call(
        kernel,
        in_specs=[SMEM] * smem + [ANY] * (len(args) - smem),
        out_specs=[ANY] * len(outs),
        out_shape=shaped(*outs),
        scratch_shapes=scratch + [pltpu.SemaphoreType.DMA((sems,))],
        compiler_params=pltpu.CompilerParams(vmem_limit_bytes=VMEM_LIMIT),
        cost_estimate=pl.CostEstimate(flops=flops, bytes_accessed=8 << 20, transcendentals=0),
    )(*args)


def open_kernel(pieces_ref, tag_ref, at_ref, emb_ref, own_ref, other_ref, *refs):
    outs, refs = refs[:12], refs[12:]
    x_o, low_o, par_o, wa_o, wb_o, p_o = outs[:6]
    x_s, low_s, par_s, wa_s, wb_s, small_s = refs[:6]
    scratch, work, sem = refs[6:12], refs[12:17], refs[17]
    moves = Moves(sem)
    ends = piece_ends(pieces_ref)
    first = moves.fetch(emb_ref, x_s)
    small = rows_in(moves, at_ref, 0, own_ref, small_s, 3 * HALF, 128, 0)
    weights = rows_in(moves, at_ref, 0, own_ref, wa_s, 0, 3 * HALF, 0)
    weights += rows_in(moves, at_ref, 1, other_ref, wb_s, 0, 3 * HALF, 0)
    segment_codes(ends, work[1], work[2])
    wait(*small)
    par_s[...] = small_s[...].astype(F32).T[:8, :]
    moves.send(par_s, par_o)
    wait(first)
    row = par_s[pl.ds(4 + tag_ref[0], 1), :]

    def chunk(i, carry):
        rows = block_rows(i, TM)
        value = x_s[rows, :] + row
        x_s[rows, :] = value
        low_s[rows, :] = value.astype(BF)
        return carry

    lax.fori_loop(0, LEN // TM, chunk, 0)
    moves.send(x_s, x_o)
    moves.send(low_s, low_o)
    wait(*weights)
    moves.send(wa_s, wa_o)
    moves.send(wb_s, wb_o)
    attend_whole(ends, moves, low_s, (wa_s, wb_s), outs[6:], scratch, p_o, work)
    moves.finish()


def open_visit(pieces, tag, at, embedded, own, other):
    own_outs = (full(D, F32), full(D), ((8, D), F32), ((D, 3 * HALF), BF), ((D, 3 * HALF), BF))
    outs = own_outs + ((P_SHAPE, BF),) + ATTEND_OUT
    scratch = like(own_outs) + [VMEM((D, 128), BF)] + like(ATTEND_OUT) + ATTEND_WORK
    x, low, par, wa, wb, p, *rest = call(open_kernel, None, outs, scratch, 3 * 64 + 16, 7_000_000_000,
                                         pieces, tag, at, embedded, own, other)
    return x, low, par, wa, wb, (*rest, p)


SAVED = (full(D), full(1, F32), full(D), full(FF), full(FF), full(D), full(1, F32))


def second_kernel(pieces_ref, at_ref, x_ref, mixed_ref, own_ref, other_ref, par_ref, wa_ref, wb_ref, *refs):
    weight_o, saved_o, x_o, low_o, p_o, outs = refs[:3], refs[3:10], refs[10], refs[11], refs[12], refs[13:19]
    refs = refs[19:]
    x_s, mix_s, par_s, wa_s, wb_s = refs[:5]
    weight_s, saved_s, low_s = refs[5:8], refs[8:15], refs[15]
    scratch, work, sem = refs[16:22], refs[22:27], refs[27]
    moves = Moves(sem)
    ends = piece_ends(pieces_ref)
    wo_s, wh_s, wd_s = weight_s
    first = [moves.fetch(x_ref, x_s), moves.fetch(mixed_ref, mix_s), moves.fetch(par_ref, par_s)]
    for half, ref in enumerate((own_ref, other_ref)):
        first += rows_in(moves, at_ref, half, ref, wo_s, 0, HALF, half * HALF)
        first += rows_in(moves, at_ref, half, ref, wh_s, HALF, FF // 2, half * (FF // 2))
        first += rows_in(moves, at_ref, half, ref, wd_s, HALF + FF // 2, FF // 2, half * (FF // 2))
    later = [moves.fetch(wa_ref, wa_s), moves.fetch(wb_ref, wb_s)]
    segment_codes(ends, work[1], work[2])
    wait(*first)
    feed_stage(x_s, mix_s, wo_s, wh_s, wd_s, par_s, x_s, *saved_s)
    for a, b in zip(weight_s + saved_s + (x_s,), weight_o + saved_o + (x_o,)):
        moves.send(a, b)

    def chunk(i, carry):
        rows = block_rows(i, TM)
        low_s[rows, :] = x_s[rows, :].astype(BF)
        return carry

    lax.fori_loop(0, LEN // TM, chunk, 0)
    moves.send(low_s, low_o)
    wait(*later)
    attend_whole(ends, moves, low_s, (wa_s, wb_s), outs, scratch, p_o, work)
    moves.finish()


def second_visit(pieces, at, x, mixed, own, other, par, wa, wb):
    weights = (((D, D), BF), ((D, FF), BF), ((D, FF), BF))
    outs = weights + SAVED + (full(D, F32), full(D), (P_SHAPE, BF)) + ATTEND_OUT
    scratch = (like((full(D, F32), full(D), ((8, D), F32), ((D, 3 * HALF), BF), ((D, 3 * HALF), BF)) + weights + SAVED
                    + (full(D),) + ATTEND_OUT) + ATTEND_WORK)
    got = call(second_kernel, None, outs, scratch, 6 * 64 + 32, 12_000_000_000,
               pieces, at, x, mixed, own, other, par, wa, wb)
    return got[:3], got[3:10], got[10], got[11], (*got[13:], got[12])


def middle_kernel(pieces_ref, x_ref, mixed_ref, inv_ref, cot_ref, wo_ref, wh_ref, wd_ref, par_ref, *refs):
    outs, refs = refs[:7], refs[7:]
    ins, refs = refs[:8], refs[8:]
    saved, refs = refs[:7], refs[7:]
    result, total, low, hid, att = refs[:5]
    base, gm, dd, dh, do, small = refs[5:11]
    x, mixed, inv, cot, wo, wh, wd, par = ins
    unit1, inv1, norm, act, slope, unit2, inv2 = saved
    moves = Moves(refs[11])
    ends = piece_ends(pieces_ref)
    order = ((x_ref, x), (mixed_ref, mixed), (wo_ref, wo), (par_ref, par), (wh_ref, wh), (wd_ref, wd))
    first = [moves.fetch(a, b) for a, b in order]
    later = [moves.fetch(cot_ref, cot), moves.fetch(inv_ref, inv)]
    wait(*first)
    feed_stage(x, mixed, wo, wh, wd, par, result, *saved)
    moves.send(result, outs[0])
    wait(*later)
    total_stage(ends[-2], cot, unit2, inv2, par, total, low, small)
    feed_back_stage(total, low, unit1, inv1, slope, inv, wo, wh, wd, par, base, gm, small, hid, att)
    moves.send(base, outs[1])
    moves.send(gm, outs[2])
    moves.send(small, outs[6])
    weight_stage(low, act, None, dd)
    moves.send(dd, outs[3])
    weight_stage(norm, hid, None, dh)
    moves.send(dh, outs[4])
    weight_stage(att, mixed, None, do)
    moves.send(do, outs[5])
    moves.finish()


def middle(pieces, x, mixed, inv, cot, wo, wh, wd, par):
    outs = (full(D, F32), full(D, F32), full(D), ((D, FF), BF), ((D, FF), BF), ((D, D), BF), ((32, D), F32))
    ins = (full(D, F32), full(D), full(D, F32), full(D, F32), ((D, D), BF), ((D, FF), BF), ((D, FF), BF), ((8, D), F32))
    scratch = like(ins + SAVED + (full(D, F32), full(D, F32), full(D), full(FF), full(D)) + outs[1:])
    return call(middle_kernel, None, outs, scratch, 32, 20_000_000_000,
                pieces, x, mixed, inv, cot, wo, wh, wd, par)


BACK_WORK = [VMEM(P_SHAPE, BF), VMEM((HEADS2, 128, LEN), BF), VMEM((HEADS2, LEN, 128), F32),
             VMEM((HEADS2, LEN, 128), F32), VMEM((LEN, 3 * D), BF), pltpu.SemaphoreType.DMA((NQ,))]
BACK_IN = (full(D), full(D), full(D), full(D, F32), full(D), full(D))


def pack_grads(low, grads, olds, outs):
    for half in range(2):
        for part in range(3):
            cols = slice(part * HALF, (part + 1) * HALF)
            value = tn(low[...], grads[:, part * D + half * HALF:part * D + (half + 1) * HALF])
            if olds is not None:
                value = value + olds[half][:, cols].astype(F32)
            outs[half][:, cols] = value.astype(BF)


def back_kernel(pieces_ref, q_ref, k_ref, v_ref, exact_ref, gm_ref, low_ref, p_ref, base_ref, wa_ref, wb_ref, *refs):
    dx_o, da_o, db_o = refs[:3]
    ins, refs = refs[3:9], refs[9:]
    base, wa, wb, dx, da, db = refs[:6]
    p_slots, kt, dk, dv, grads, p_sem, sem = refs[6:]
    moves = Moves(sem)
    ends = piece_ends(pieces_ref)
    first = [moves.fetch(a, b) for a, b in zip((q_ref, k_ref, v_ref, exact_ref, gm_ref), ins)]
    probs_start(ends, p_ref, p_slots, p_sem)
    later = [moves.fetch(a, b) for a, b in ((low_ref, ins[5]), (base_ref, base), (wa_ref, wa), (wb_ref, wb))]
    wait(*first)
    q, k, v, exact, gm, low = ins
    attend_back_stage(ends, q, k, v, kt, exact, gm, p_ref, p_slots, p_sem, dk, dv, grads)
    wait(*later)
    input_stage(base, grads, (wa, wb), dx)
    moves.send(dx, dx_o)
    pack_grads(low, grads, None, (da, db))
    moves.send(da, da_o)
    moves.send(db, db_o)
    moves.finish()


def back(pieces, heads, low, gm, base, wa, wb):
    q, k, v, mixed, exact, inv, p = heads
    pair = (((D, 3 * HALF), BF),) * 2
    outs = (full(D, F32),) + pair
    scratch = like(BACK_IN + (full(D, F32),) + pair + outs) + BACK_WORK
    return call(back_kernel, None, outs, scratch, 16, 14_000_000_000,
                pieces, q, k, v, exact, gm, low, p, base, wa, wb)


def down_kernel(to_ref, grad_ref, unit2_ref, inv2_ref, par_ref, act_ref, old_ref, *refs):
    total_o, low_o, small_o, keep_o, send_o = refs[:5]
    grad, unit2, inv2, par, act, old, total, low, small, dd, sem = refs[5:]
    moves = Moves(sem)
    first = [moves.fetch(a, b) for a, b in ((grad_ref, grad), (unit2_ref, unit2), (inv2_ref, inv2), (par_ref, par))]
    later = [moves.fetch(act_ref, act), moves.fetch(old_ref, old)]
    wait(*first)
    total_stage(None, grad, unit2, inv2, par, total, low, small)
    moves.send(total, total_o)
    moves.send(low, low_o)
    moves.send(small, small_o)
    wait(*later)
    weight_stage(low, act, old, dd)
    for half, target in enumerate((keep_o, send_o)):
        rows_out(moves, to_ref, half, dd, half * (FF // 2), FF // 2, target, 0)
    moves.finish()


def down(to, part, grad, unit2, inv2, par, act, old):
    outs = (full(D, F32), full(D), ((32, D), F32), (part(FF // 2), BF), (part(FF // 2), BF))
    scratch = like((full(D, F32), full(D), full(1, F32), ((8, D), F32), full(FF), ((D, FF), BF))
                   + outs[:3] + (((D, FF), BF),))
    return call(down_kernel, None, outs, scratch, 160, 3_000_000_000, to, grad, unit2, inv2, par, act, old)


def hidden_kernel(to_ref, total_ref, low_ref, small_ref, unit1_ref, inv1_ref, norm_ref, slope_ref, inv_ref, mixed_ref,
                  wo_ref, wh_ref, wd_ref, par_ref, old_h_ref, old_o_ref, *refs):
    base_o, gm_o, small_o, keep_o, send_o = refs[:5]
    ins, refs = refs[5:20], refs[20:]
    base, gm, hid, att, dh, do, sem = refs
    total, low, small, unit1, inv1, norm, slope, inv, mixed, wo, wh, wd, par, old_h, old_o = ins
    moves = Moves(sem)
    first = [moves.fetch(a, b) for a, b in (
        (low_ref, low), (wd_ref, wd), (slope_ref, slope), (wh_ref, wh), (total_ref, total), (small_ref, small),
        (unit1_ref, unit1), (inv1_ref, inv1), (par_ref, par), (wo_ref, wo), (inv_ref, inv))]
    later = [moves.fetch(a, b) for a, b in (
        (norm_ref, norm), (old_h_ref, old_h), (mixed_ref, mixed), (old_o_ref, old_o))]
    wait(*first)
    feed_back_stage(total, low, unit1, inv1, slope, inv, wo, wh, wd, par, base, gm, small, hid, att)
    moves.send(base, base_o)
    moves.send(gm, gm_o)
    moves.send(small, small_o)
    wait(*later)
    weight_stage(norm, hid, old_h, dh)
    for half, target in enumerate((keep_o, send_o)):
        rows_out(moves, to_ref, half, dh, half * (FF // 2), FF // 2, target, HALF)
    weight_stage(att, mixed, old_o, do)
    for half, target in enumerate((keep_o, send_o)):
        rows_out(moves, to_ref, half, do, half * HALF, HALF, target, 0)
    moves.finish()


def hidden_back(to, part, total, low, small, unit1, inv1, norm, slope, inv, mixed, wo, wh, wd, par, old_h, old_o):
    outs = (full(D, F32), full(D), ((32, D), F32), (part(REST_H), BF), (part(REST_H), BF))
    args = (total, low, small, unit1, inv1, norm, slope, inv, mixed, wo, wh, wd, par, old_h, old_o)
    scratch = like(tuple((a.shape, a.dtype) for a in args) + outs[:2]
                   + (full(FF), full(D), ((D, FF), BF), ((D, D), BF)))
    return call(hidden_kernel, None, outs, scratch, 320, 12_000_000_000, to, *args)


REST_H = HALF + FF // 2
FIRST = 3 * HALF + 128


def last_kernel(pieces_ref, tag_ref, to_ref, q_ref, k_ref, v_ref, exact_ref, gm_ref, low_ref, p_ref, base_ref, wa_ref,
                wb_ref, old_a_ref, old_b_ref, small_a_ref, small_b_ref, *refs):
    grads_o, keep_o, send_o = refs[:3]
    ins, refs = refs[3:9], refs[9:]
    base, wa, wb, old_a, old_b, small_a, small_b, da, db, stats = refs[:10]
    p_slots, kt, dk, dv, grads, p_sem, sem = refs[10:]
    moves = Moves(sem)
    ends = piece_ends(pieces_ref)
    first = [moves.fetch(a, b) for a, b in zip((q_ref, k_ref, v_ref, exact_ref, gm_ref), ins)]
    probs_start(ends, p_ref, p_slots, p_sem)
    later = [moves.fetch(a, b) for a, b in (
        (low_ref, ins[5]), (base_ref, base), (wa_ref, wa), (wb_ref, wb), (old_a_ref, old_a), (old_b_ref, old_b),
        (small_a_ref, small_a), (small_b_ref, small_b))]
    wait(*first)
    q, k, v, exact, gm, low = ins
    attend_back_stage(ends, q, k, v, kt, exact, gm, p_ref, p_slots, p_sem, dk, dv, grads)
    moves.send(grads, grads_o)
    wait(*later)
    pack_grads(low, grads, (old_a, old_b), (da, db))
    rows_out(moves, to_ref, 0, da, 0, 3 * HALF, keep_o, 0)
    rows_out(moves, to_ref, 1, db, 0, 3 * HALF, send_o, 0)
    sums = nn(jnp.ones((8, LEN), BF), grads[...])
    high = sums.astype(BF)
    rest = (sums - high.astype(F32)).astype(BF)
    column = jnp.sum(base[...], axis=0, keepdims=True)
    for half, w in enumerate((wa, wb)):
        for part in range(3):
            at = part * D + half * HALF
            for piece in (high, rest):
                column = column + nt(piece[:, at:at + HALF], w[:, part * HALF:(part + 1) * HALF])[:1]
    norms = jnp.sum((small_a[...] + small_b[...]).reshape(4, 8, D), axis=1)
    tags = lax.broadcasted_iota(jnp.int32, (PAIRS, D), 0) == tag_ref[0]
    table = jnp.where(tags, jnp.broadcast_to(column, (PAIRS, D)), 0.0)
    rows = jnp.concatenate([norms, table, jnp.zeros((120, D), F32)], axis=0)
    stats[...] = rows.T.astype(BF)
    rows_out(moves, to_ref, 0, stats, 0, 128, keep_o, 3 * HALF)
    rows_out(moves, to_ref, 1, stats, 0, 128, send_o, 3 * HALF)
    moves.finish()


def last_back(pieces, tag, to, part, heads, low, gm, base, wa, wb, old_a, old_b, small_a, small_b):
    q, k, v, mixed, exact, inv, p = heads
    pair = (((D, 3 * HALF), BF),) * 2
    outs = (full(3 * D), (part(FIRST), BF), (part(FIRST), BF))
    stats = ((32, D), F32)
    scratch = like(BACK_IN + (full(D, F32),) + pair + pair + (stats, stats) + pair + (((D, 128), BF),)) + BACK_WORK
    return call(last_kernel, None, outs, scratch, 4 * 64 + 32, 12_000_000_000,
                pieces, tag, to, q, k, v, exact, gm, low, p, base, wa, wb, old_a, old_b, small_a, small_b)


def input_kernel(base_ref, grads_ref, wa_ref, wb_ref, out_ref):
    input_stage(base_ref, grads_ref, (wa_ref, wb_ref), out_ref)


def input_back(base, grads, wa, wb):
    return pl.pallas_call(
        input_kernel,
        out_shape=jax.ShapeDtypeStruct((LEN, D), F32),
        compiler_params=pltpu.CompilerParams(vmem_limit_bytes=VMEM_LIMIT),
        cost_estimate=pl.CostEstimate(flops=1_600_000_000, bytes_accessed=9 << 20, transcendentals=0),
    )(base, grads, wa, wb)


GROUP = ("dp", "tensor")


def plan(dp):
    if dp == 16:
        return (8, 4, 1, 2), (8, 4, 2, 1)
    bits = [1 << i for i in range(dp.bit_length() - 1)]
    side = len(bits) // 3
    x, y, z = bits[:side], bits[side:2 * side], bits[2 * side:]
    return tuple(z[::-1] + x[::-1] + y[::-1]), tuple(z[::-1] + y[::-1] + x[::-1])


def flip(value, dp, masks):
    pairs = [(d * 2 + t, (d ^ masks[t]) * 2 + t) for d in range(dp) for t in range(2)]
    return lax.ppermute(value, GROUP, pairs)


def swap(value):
    return lax.ppermute(value, "tensor", [(0, 1), (1, 0)])


def gather(own, dp):
    held = own[None]
    for masks in zip(*plan(dp)):
        held = jnp.concatenate([held, flip(held, dp, masks)], axis=0)
    return held


def places(dp, mine, tensor):
    rel = jnp.arange(dp, dtype=jnp.int32) ^ mine
    found = []
    for order in plan(dp):
        found.append(sum(((rel & mask) // mask) << i for i, mask in enumerate(order)))
    return jnp.stack([jnp.where(tensor == t, found[0], found[1]) for t in (0, 1)])


def reduce(keep, send, dp):
    held = add(keep, swap(send))
    phases = list(zip(*plan(dp)))[::-1]
    for i, masks in enumerate(phases):
        half = held.shape[0] // 2
        arrived = flip(held[half:], dp, masks)
        held = add(held[:half], arrived, F32 if i == len(phases) - 1 else BF)
    return held[0]


def add(a, b, kind=BF):
    return (a.astype(F32) + b.astype(F32)).astype(kind)


def body(embedded, piece_lengths, pair_tags, pair_embedding, w_query, w_key, w_value, w_output, w_hidden,
         w_down, first_gain, first_shift, second_gain, second_shift, cotangent):
    dp = lax.axis_size("dp")
    mine, tensor = lax.axis_index("dp"), lax.axis_index("tensor")
    rows = D // dp
    blocked = rows % 16 == 0
    pieces = lax.dynamic_index_in_dim(piece_lengths, tensor, 0, keepdims=False)
    tag = lax.dynamic_index_in_dim(pair_tags, tensor, 0, keepdims=True)
    small = jnp.stack([first_gain, first_shift, second_gain, second_shift], axis=1)
    small = jnp.concatenate([small, pair_embedding.T, jnp.zeros((rows, 120), BF)], axis=1)
    first = gather(jnp.concatenate([w_query, w_key, w_value, small], axis=1), dp)
    rest = gather(jnp.concatenate([w_output.T, w_hidden, w_down.T], axis=1), dp)
    at = places(dp, mine, tensor)

    def arranged(held):
        both = held, swap(held)
        if blocked:
            return both
        return tuple(h[at[i]].reshape(D, -1) for i, h in enumerate(both))

    def part(width):
        return (dp, rows, width) if blocked else (D, width)

    def summed(keep, send):
        if not blocked:
            keep, send = (v.reshape(dp, rows, -1)[jnp.zeros((dp,), jnp.int32).at[at[i]].set(jnp.arange(dp))]
                          for i, v in enumerate((keep, send)))
        return reduce(keep, send, dp)

    x, low, par, wa, wb, heads = open_visit(pieces, tag, at, embedded, *arranged(first))
    (wo, wh, wd), saved, x_second, low_second, heads_second = second_visit(
        pieces, at, x, heads[3], *arranged(rest), par, wa, wb)
    result, base, gm, dd, dh, do, small_second = middle(
        pieces, x_second, heads_second[3], heads_second[5], cotangent, wo, wh, wd, par)
    grad, da, db = back(pieces, heads_second, low_second, gm, base, wa, wb)
    unit1, inv1, norm, act, slope, unit2, inv2 = saved
    total, low_total, small, *dd = down(at, part, grad, unit2, inv2, par, act, dd)
    dd = summed(*dd)
    base, gm, small, *dh = hidden_back(at, part, total, low_total, small, unit1, inv1, norm, slope, heads[5], heads[3],
                                       wo, wh, wd, par, dh, do)
    dh = summed(*dh)
    grads, *da = last_back(pieces, tag, at, part, heads, low, gm, base, wa, wb, da, db, small_second, small)
    grad = input_back(base, grads, wa, wb)
    da = summed(*da)
    small = da[:, 3 * HALF:3 * HALF + 8].T
    return (result, grad, small[4:], da[:, :HALF], da[:, HALF:2 * HALF], da[:, 2 * HALF:3 * HALF],
            dh[:, :HALF].T, dh[:, HALF:], dd.T, small[0], small[1], small[2], small[3])


def solution(mesh):
    both = P(GROUP, None)
    params = (P("dp", "tensor"),) * 3 + (P("tensor", "dp"), P("dp", "tensor"), P("tensor", "dp"))
    in_specs = (both, P("dp", None), P("dp"), P(None, "dp")) + params + (P("dp"),) * 4 + (both,)
    out_specs = (both, both, P(None, "dp")) + params + (P("dp"),) * 4
    return jax.shard_map(body, mesh=mesh, in_specs=in_specs, out_specs=out_specs, check_vma=False)
```

```python
import functools
import math

import jax
import jax.numpy as jnp
from jax import lax
from jax.sharding import PartitionSpec as P
from jax.experimental import pallas as pl
from jax.experimental.pallas import tpu as pltpu

HEAD_DIM = 64
LEN = 1024
PIECES = 8
PAIRS = 4
D = 512
FF = 2048
HALF = 256
HEADS2 = 4
QB = 256
KB = 128
NQ = LEN // QB
NK = LEN // KB
BIG = 1e30
LOG2E = math.log2(math.e)
QSCALE = LOG2E / math.sqrt(HEAD_DIM)
KSCALE = math.log(2.0)
WIDTHS = (2, 3, 4, 5, 6, 7, 8)
EPS = 1e-5
C1 = math.sqrt(2.0 / math.pi)
C2 = C1 * 0.044715
F32 = jnp.float32
BF = jnp.bfloat16
VMEM_LIMIT = 60 * 1024 * 1024
TM = 256


def nn(a, b):
    return jnp.dot(a, b, preferred_element_type=F32)


def nt(a, b):
    return lax.dot_general(a, b, (((1,), (1,)), ((), ())), preferred_element_type=F32)


def tn(a, b):
    return lax.dot_general(a, b, (((0,), (0,)), ((), ())), preferred_element_type=F32)


def piece_ends(pieces_ref):
    ends, at = [], 0
    for j in range(PIECES):
        at = at + pieces_ref[j]
        ends.append(at)
    return ends


def window(block, ends):
    first = block * QB
    last = first + QB - 1
    low, high = jnp.int32(0), jnp.int32(LEN)
    for end in ends[:-1]:
        low = jnp.maximum(low, jnp.where(end <= first, end, 0))
        high = jnp.minimum(high, jnp.where(end > last, end, LEN))
    low = jnp.where(first >= ends[-2], first, low)
    high = jnp.where(last >= ends[-2], last + 1, high)
    return low // KB, (high + KB - 1) // KB


def over_widths(block, ends, run):
    low, high = window(block, ends)
    count = high - low
    previous = 0
    for wide in WIDTHS:
        begin = jnp.minimum(low, NK - wide)

        @pl.when((count > previous) & (count <= wide))
        def _(wide=wide, begin=begin):
            run(wide, pl.multiple_of(begin * KB, KB))

        previous = wide


def segment_codes(ends, segq_ref, segk_ref):
    rows = lax.broadcasted_iota(jnp.int32, (LEN, 128), 0)
    lanes = lax.broadcasted_iota(jnp.int32, (LEN, 128), 1)
    ids = jnp.zeros((LEN, 128), jnp.int32)
    for end in ends[:-1]:
        ids = ids + jnp.where(rows >= end, 1, 0)
    same = lanes == ids
    segk_ref[...] = jnp.where(same, 1.0, 0.0).astype(BF)
    free = (lanes >= PIECES) | (same & (lanes < PIECES - 1))
    segq_ref[...] = jnp.where(free, 0.0, -BIG).astype(BF)


def lane_half(shape):
    return lax.broadcasted_iota(jnp.int32, shape, 1) < HEAD_DIM


def two_heads(block):
    left = lane_half(block.shape)
    zero = jnp.zeros_like(block)
    return jnp.where(left, block, zero), jnp.where(left, zero, block)


def block_rows(index, size):
    return pl.ds(pl.multiple_of(index * size, size), size)


def head_norms(values, half):
    heads = lax.broadcasted_iota(jnp.int32, (HALF, 128), 0) // HEAD_DIM + half * (HALF // HEAD_DIM)
    pick = jnp.where(heads == lax.broadcasted_iota(jnp.int32, (HALF, 128), 1), 1.0, 0.0).astype(BF)
    return jnp.max(nn((values * values).astype(BF), pick), axis=0, keepdims=True)


def project_stage(x_ref, w_refs, q_ref, k_ref, v_ref, vt_ref):
    def chunk(i, carry):
        rows = block_rows(i, TM)
        low = x_ref[rows, :]
        q_top, k_top = carry
        for half in range(2):
            cols = slice(half * HALF, (half + 1) * HALF)
            queries = nn(low, w_refs[half][:, :HALF]) * QSCALE
            keys = nn(low, w_refs[half][:, HALF:2 * HALF])
            q_ref[rows, cols] = queries.astype(BF)
            k_ref[rows, cols] = keys.astype(BF)
            q_top = jnp.maximum(q_top, head_norms(queries, half))
            k_top = jnp.maximum(k_top, head_norms(keys, half))
            values = nn(low, w_refs[half][:, 2 * HALF:3 * HALF])
            v_ref[rows, cols] = values.astype(BF)
            for pair in range(2):
                vt_ref[half * 2 + pair, :128, rows] = values[:, pair * 128:(pair + 1) * 128].T.astype(BF)
        return q_top, k_top

    zero = jnp.zeros((1, 128), F32)
    q_top, k_top = lax.fori_loop(0, LEN // TM, chunk, (zero, zero))
    for pair in range(HEADS2):
        vt_ref[pair, 128:, :] = jnp.ones((16, LEN), BF)
    return jnp.max(q_top * k_top)


def probs_copy(p_slots, p_hbm, sem, i, wide, out):
    slot = i % 2
    here = p_slots.at[slot, :, pl.ds(0, wide * KB), :]
    there = p_hbm.at[i, :, pl.ds(0, wide * KB), :]
    return pltpu.make_async_copy(here, there, sem.at[slot]) if out else pltpu.make_async_copy(there, here, sem.at[slot])


def attend_stage(ends, shifted, resident, q_ref, k_ref, v_ref, mixed_ref, low_ref, inv_ref, vt_ref, segq_ref, segk_ref,
                 p_slots, p_out, p_sem, done):
    def block(i, carry):
        rows = block_rows(i, QB)
        p_ref = p_slots.at[i % 2]

        @pl.when(i >= 2)
        def _():
            over_widths(i - 2, ends, lambda wide, begin: probs_copy(p_slots, p_out, p_sem, i - 2, wide, True).wait())

        def run(wide, begin):
            keys = pl.ds(begin, wide * KB)
            segq = segq_ref[rows, :]
            segk = segk_ref[keys, :]
            pad = lax.broadcasted_iota(jnp.int32, (QB, 128), 0) + i * QB >= ends[-2]
            span = [slice(pair * 128, (pair + 1) * 128) for pair in range(HEADS2)]

            def score(pair):
                even, odd = two_heads(q_ref[rows, span[pair]])
                query = jnp.concatenate(
                    [jnp.concatenate([even, segq], axis=1), jnp.concatenate([odd, segq], axis=1)], axis=0)
                key = jnp.concatenate([k_ref[keys, span[pair]], segk], axis=1)
                return nt(key, query)

            def soften(pair, scores):
                if shifted:
                    scores = scores - jnp.max(scores, axis=0, keepdims=True)
                probs = jnp.exp2(scores).astype(BF)
                p_ref[pair, :wide * KB, :] = probs
                return probs

            def mix(pair, probs):
                return nn(vt_ref[pair, :, keys], probs)

            def finish(pair, out):
                cols = span[pair]
                inv = 1.0 / jnp.maximum(out[128:129, :], 1e-30)
                inv_ref[pl.ds(i * HEADS2 + pair, 1), :] = inv
                inv_both = jnp.concatenate(
                    [jnp.broadcast_to(inv[:, :QB], (64, QB)), jnp.broadcast_to(inv[:, QB:], (64, QB))], axis=0)
                exact = (jnp.concatenate([out[:64, :QB], out[64:128, QB:]], axis=0) * inv_both).T
                mixed = jnp.where(pad, v_ref[rows, cols].astype(F32), exact).astype(BF)
                mixed_ref[rows, cols] = mixed
                low_ref[rows, cols] = (exact - mixed.astype(F32)).astype(BF)

            s = {0: score(0), 1: score(1)}
            p, o = {}, {}
            for pair in range(HEADS2):
                p[pair] = soften(pair, s[pair])
                if pair + 2 < HEADS2:
                    s[pair + 2] = score(pair + 2)
                if pair:
                    o[pair - 1] = mix(pair - 1, p[pair - 1])
                if pair > 1:
                    finish(pair - 2, o[pair - 2])
            out = probs_copy(p_slots, p_out, p_sem, i, wide, True)
            if resident:
                pl.when(i < NQ - 2)(out.start)
            else:
                out.start()
            o[HEADS2 - 1] = mix(HEADS2 - 1, p[HEADS2 - 1])
            finish(HEADS2 - 2, o[HEADS2 - 2])
            finish(HEADS2 - 1, o[HEADS2 - 1])

        over_widths(i, ends, run)
        done(i, rows)
        return carry

    lax.fori_loop(0, NQ, block, 0)
    if not resident:
        for i in range(NQ - 2, NQ):
            over_widths(i, ends, lambda wide, begin, i=i: probs_copy(p_slots, p_out, p_sem, i, wide, True).wait())


def grad_columns(part, pair):
    at = pair // 2 * 3 * HALF + part * HALF + pair % 2 * 128
    return slice(at, at + 128)


def attend_back_stage(ends, resident, q_ref, k_ref, v_ref, mixed_ref, low_ref, grad_ref, kt_ref, p_in, p_slots, p_sem,
                      dk_ref, dv_ref, grads_ref, first=(), later=()):
    if not resident:
        for i in (NQ - 1, NQ - 2):
            over_widths(i, ends, lambda wide, begin, i=i: probs_copy(p_slots, p_in, p_sem, i, wide, False).start())
    dk_ref[...] = jnp.zeros_like(dk_ref)
    dv_ref[...] = jnp.zeros_like(dv_ref)
    wait(*first)
    for pair in range(HEADS2):
        kt_ref[pair, :128, :] = k_ref[:, pair * 128:(pair + 1) * 128].astype(F32).T.astype(BF)
    span = [slice(pair * 128, (pair + 1) * 128) for pair in range(HEADS2)]

    def block(j, carry):
        i = NQ - 1 - j
        rows = block_rows(i, QB)
        p_ref = p_slots.at[i % 2]

        def run(wide, begin):
            keys = pl.ds(begin, wide * KB)
            arrived = probs_copy(p_slots, p_in, p_sem, i, wide, False)
            if resident:
                pl.when(j >= 2)(arrived.wait)
            else:
                arrived.wait()

            def outer(pair):
                return jnp.concatenate(two_heads(grad_ref[rows, span[pair]]), axis=0)

            def slope(pair):
                grad = grad_ref[rows, span[pair]]
                exact = mixed_ref[rows, span[pair]].astype(F32) + low_ref[rows, span[pair]].astype(F32)
                inner = grad.astype(F32) * exact
                high = inner.astype(BF)
                rest = pltpu.roll(inner - high.astype(F32), HEAD_DIM, 1).astype(BF)
                left = lane_half(inner.shape)
                inner = jnp.concatenate([jnp.where(left, high, rest), jnp.where(left, rest, high)], axis=0)
                both = jnp.concatenate([outer(pair), inner], axis=1)
                value = jnp.concatenate([v_ref[keys, span[pair]], jnp.full((wide * KB, 128), -1.0, BF)], axis=1)
                return nt(value, both)

            def bend(pair, slope):
                return (p_ref[pair, :wide * KB, :].astype(F32) * slope).astype(BF)

            def values(pair):
                dv_ref[keys, span[pair]] += nn(p_ref[pair, :wide * KB, :], outer(pair))

            def rest(pair, scores):
                query = jnp.concatenate(two_heads(q_ref[rows, span[pair]]), axis=0)
                dk_ref[keys, span[pair]] += nn(scores, query)
                out = nn(kt_ref[pair, :128, keys], scores)
                out = jnp.concatenate([out[:64, :QB], out[64:, QB:]], axis=0)
                grads_ref[rows, grad_columns(0, pair)] = (out.T * (HEAD_DIM ** -0.5)).astype(BF)

            s = {0: slope(0), 1: slope(1)}
            d = {}
            for pair in range(HEADS2):
                d[pair] = bend(pair, s[pair])
                values(pair)
                if pair + 2 < HEADS2:
                    s[pair + 2] = slope(pair + 2)
                if pair:
                    rest(pair - 1, d[pair - 1])
            rest(HEADS2 - 1, d[HEADS2 - 1])

        over_widths(i, ends, run)

        if later:
            @pl.when(j == 0)
            def _():
                for copy in later:
                    copy.start()

        @pl.when(j < NQ - 2)
        def _():
            over_widths(i - 2, ends, lambda wide, begin: probs_copy(p_slots, p_in, p_sem, i - 2, wide, False).start())

        return carry

    lax.fori_loop(0, NQ, block, 0)
    for pair in range(HEADS2):
        grads_ref[:, grad_columns(1, pair)] = (dk_ref[:, span[pair]] * KSCALE).astype(BF)
        grads_ref[:, grad_columns(2, pair)] = dv_ref[:, span[pair]].astype(BF)


def unit_rows(values):
    center = values - jnp.mean(values, axis=-1, keepdims=True)
    spread = jnp.mean(center * center, axis=-1, keepdims=True)
    inv = lax.rsqrt(spread + EPS)
    return center * inv, inv


HID = HALF
DOWN = HALF + FF // 2
REST = HALF + FF
FIRST = 3 * HALF + 128
STEP = 512
PER_HALF = FF // 2 // STEP


def feed_stage(x_ref, mixed_ref, w_refs, par_ref, out_ref, unit1_ref, inv1_ref, norm_ref, act_ref, slope_ref,
               unit2_ref, inv2_ref, tm=512):
    def chunk(i, carry):
        rows = block_rows(i, tm)
        summed = x_ref[rows, :]
        for half in range(2):
            summed = summed + nt(mixed_ref[rows, half * HALF:(half + 1) * HALF], w_refs[half][:, :HALF])
        unit, inv = unit_rows(summed)
        unit1_ref[rows, :] = unit.astype(BF)
        inv1_ref[rows, :] = inv
        normed = unit * par_ref[0:1, :] + par_ref[1:2, :]
        low = normed.astype(BF)
        norm_ref[rows, :] = low
        for part in range(2 * PER_HALF):
            cols = slice(part * STEP, (part + 1) * STEP)
            at = HID + part % PER_HALF * STEP
            hidden = nn(low, w_refs[part // PER_HALF][:, at:at + STEP])
            square = hidden * hidden
            gate = 0.5 + 0.5 * jnp.tanh(hidden * (C1 + C2 * square))
            act_ref[rows, cols] = (hidden * gate).astype(BF)
            slope_ref[rows, cols] = (gate + gate * (1.0 - gate) * hidden * (2 * C1 + 6 * C2 * square)).astype(BF)
        total = normed
        for half in range(2):
            total = total + nt(act_ref[rows, half * (FF // 2):(half + 1) * (FF // 2)], w_refs[half][:, DOWN:])
        unit, inv = unit_rows(total)
        unit2_ref[rows, :] = unit.astype(BF)
        inv2_ref[rows, :] = inv
        out_ref[rows, :] = unit * par_ref[2:3, :] + par_ref[3:4, :]
        return carry

    lax.fori_loop(0, LEN // tm, chunk, 0)


def unit_back(grad, unit, inv, gain):
    scaled = grad * gain
    first = jnp.mean(scaled, axis=-1, keepdims=True)
    second = jnp.mean(scaled * unit, axis=-1, keepdims=True)
    return inv * (scaled - first - unit * second)


def fold_rows(values):
    return jnp.sum(values.reshape(-1, 8, values.shape[-1]), axis=0)


def total_stage(limit, grad_ref, unit2_ref, inv2_ref, par_ref, total_ref, low_ref, small_ref, tm=512):
    small_ref[...] = jnp.zeros_like(small_ref)

    def chunk(i, carry):
        rows = block_rows(i, tm)
        grad = grad_ref[rows, :]
        if limit is not None:
            grad = jnp.where(lax.broadcasted_iota(jnp.int32, grad.shape, 0) + i * tm < limit, grad, 0.0)
        unit2 = unit2_ref[rows, :].astype(F32)
        small_ref[16:24, :] += fold_rows(grad * unit2)
        small_ref[24:32, :] += fold_rows(grad)
        total = unit_back(grad, unit2, inv2_ref[rows, :], par_ref[2:3, :])
        total_ref[rows, :] = total
        low_ref[rows, :] = total.astype(BF)
        return carry

    lax.fori_loop(0, LEN // tm, chunk, 0)


def feed_back_stage(total_ref, low_ref, unit1_ref, inv1_ref, slope_ref, inv_ref, w_refs, par_ref,
                    base_ref, gm_ref, small_ref, hid_ref, att_ref, tm=512):
    def chunk(i, carry):
        rows = block_rows(i, tm)
        low = low_ref[rows, :]
        for part in range(2 * PER_HALF):
            cols = slice(part * STEP, (part + 1) * STEP)
            at = DOWN + part % PER_HALF * STEP
            slope = nn(low, w_refs[part // PER_HALF][:, at:at + STEP])
            hid_ref[rows, cols] = (slope * slope_ref[rows, cols].astype(F32)).astype(BF)
        normed = total_ref[rows, :]
        for half in range(2):
            normed = normed + nt(hid_ref[rows, half * (FF // 2):(half + 1) * (FF // 2)], w_refs[half][:, HID:DOWN])
        unit1 = unit1_ref[rows, :].astype(F32)
        small_ref[0:8, :] += fold_rows(normed * unit1)
        small_ref[8:16, :] += fold_rows(normed)
        summed = unit_back(normed, unit1, inv1_ref[rows, :], par_ref[0:1, :])
        base_ref[rows, :] = summed
        low = summed.astype(BF)
        att_ref[rows, :] = low
        for half in range(2):
            grad = nn(low, w_refs[half][:, :HALF])
            for pair in range(2):
                for part in range(tm // QB):
                    inv = inv_ref[pl.ds((i * (tm // QB) + part) * HEADS2 + half * 2 + pair, 1), :]
                    inv = jnp.concatenate([jnp.broadcast_to(inv[:, :QB], (64, QB)),
                                           jnp.broadcast_to(inv[:, QB:], (64, QB))], axis=0).T
                    value = grad[part * QB:(part + 1) * QB, pair * 128:(pair + 1) * 128] * inv
                    gm_ref[pl.ds(pl.multiple_of(i * tm + part * QB, QB), QB),
                           half * HALF + pair * 128:half * HALF + (pair + 1) * 128] = value.astype(BF)
        return carry

    lax.fori_loop(0, LEN // tm, chunk, 0)


def weight_stage(left_ref, right_ref, olds, outs, offset, width):
    cols = slice(offset, offset + width)
    for half in range(2):
        value = tn(left_ref[...], right_ref[:, half * width:(half + 1) * width])
        if olds is not None:
            value = value + olds[half][:, cols].astype(F32)
        outs[half][:, cols] = value.astype(BF)


def project_grad_stage(low_ref, grads_ref, olds, outs):
    for half in range(2):
        value = tn(low_ref[...], grads_ref[:, half * 3 * HALF:(half + 1) * 3 * HALF])
        if olds is not None:
            value = value + olds[half][...].astype(F32)
        outs[half][:, :3 * HALF] = value.astype(BF)


def input_stage(base_ref, grads_ref, w_refs, out_ref, size=LEN):
    def chunk(i, carry):
        rows = block_rows(i, TM)
        value = base_ref[rows, :]
        for half in range(2):
            value = value + nt(grads_ref[rows, half * 3 * HALF:(half + 1) * 3 * HALF], w_refs[half][:, :3 * HALF])
        out_ref[rows, :] = value
        return carry

    lax.fori_loop(0, size // TM, chunk, 0)


def add_row(x_ref, row, low_ref, keep):
    def chunk(i, carry):
        rows = block_rows(i, TM)
        value = x_ref[rows, :] + row
        if keep:
            x_ref[rows, :] = value
        if low_ref is not None:
            low_ref[rows, :] = value.astype(BF)
        return carry

    lax.fori_loop(0, LEN // TM, chunk, 0)


LIMIT = 64.0 ** 2
P_SHAPE = (NQ, HEADS2, LEN, 2 * QB)
VMEM = pltpu.VMEM


class Moves:
    def __init__(self, sem):
        self.sem, self.count, self.open = sem, 0, []

    def make(self, source, target):
        copy = pltpu.make_async_copy(source, target, self.sem.at[self.count])
        self.count += 1
        return copy

    def fetch(self, source, target):
        copy = self.make(source, target)
        copy.start()
        return copy

    def send(self, source, target):
        copy = self.fetch(source, target)
        self.open.append(copy)
        return copy

    def finish(self):
        wait(*self.open)
        self.open = []


def wait(*copies):
    for copy in copies:
        copy.wait()


class Either:
    def __init__(self, moves, index, count, make):
        self.low, self.copies = index < count, []
        at = moves.count
        for ref, place in ((0, index), (1, index - count)):
            moves.count = at
            self.copies.append(moves.make(*make(ref, jnp.clip(place, 0, count - 1))))

    def start(self):
        pl.when(self.low)(self.copies[0].start)
        pl.when(jnp.logical_not(self.low))(self.copies[1].start)

    def wait(self):
        self.copies[0].wait()


def parts_in(moves, at_ref, half, sources, target):
    if len(sources) == 1:
        return rows_in(moves, at_ref, half, sources[0], target)
    count, rows, _ = sources[0].shape
    copies = []
    for b in range(2 * count):
        copy = Either(moves, at_ref[half, b], count,
                      lambda ref, place, b=b: (sources[ref].at[place], target.at[pl.ds(b * rows, rows), :]))
        copy.start()
        copies.append(copy)
    return copies


def parts_out(moves, at_ref, half, source, targets):
    if len(targets) == 1:
        return rows_out(moves, at_ref, half, source, targets[0])
    count, rows, _ = targets[0].shape
    for b in range(2 * count):
        copy = Either(moves, at_ref[half, b], count,
                      lambda ref, place, b=b: (source.at[pl.ds(b * rows, rows), :], targets[ref].at[place]))
        copy.start()
        moves.open.append(copy)


def rows_in(moves, at_ref, half, source, target, start=True):
    move = moves.fetch if start else moves.make
    if len(source.shape) == 2:
        return [move(source, target)]
    dp, rows, _ = source.shape
    return [move(source.at[at_ref[half, b]], target.at[pl.ds(b * rows, rows), :]) for b in range(dp)]


def rows_out(moves, at_ref, half, source, target):
    if len(target.shape) == 2:
        moves.send(source, target)
        return
    dp, rows, _ = target.shape
    for b in range(dp):
        moves.send(source.at[pl.ds(b * rows, rows), :], target.at[at_ref[half, b]])


ANY = pl.BlockSpec(memory_space=pl.ANY)
SMEM = pl.BlockSpec(memory_space=pltpu.SMEM)


def like(shapes):
    return [VMEM(s, t) for s, t in shapes]


def full(width, kind=BF):
    return ((LEN, width), kind)


def call(kernel, outs, scratch, sems, flops, *args):
    smem = sum(a.dtype == jnp.int32 for a in args)
    return pl.pallas_call(
        kernel,
        in_specs=[SMEM] * smem + [ANY] * (len(args) - smem),
        out_specs=[ANY] * len(outs),
        out_shape=[jax.ShapeDtypeStruct(s, t) for s, t in outs],
        scratch_shapes=scratch + [pltpu.SemaphoreType.DMA((sems,))],
        compiler_params=pltpu.CompilerParams(vmem_limit_bytes=VMEM_LIMIT),
        cost_estimate=pl.CostEstimate(flops=flops, bytes_accessed=8 << 20, transcendentals=0),
    )(*args)


HEADS_OUT = (full(D), full(D), full(D), full(D), full(D), ((NQ * HEADS2, 2 * QB), F32))
ATTEND_WORK = [VMEM((HEADS2, 144, LEN), BF), VMEM((LEN, 128), BF), VMEM((LEN, 128), BF),
               VMEM((2,) + P_SHAPE[1:], BF), pltpu.SemaphoreType.DMA((2,))]


def either(ends, bound, resident, heads, work, p_out, done):
    for shifted in (False, True):
        @pl.when((bound > LIMIT) if shifted else (bound <= LIMIT))
        def _(shifted=shifted):
            attend_stage(ends, shifted, resident, *heads, *work[:4], p_out, work[4], done)


VT = ((HEADS2, 144, LEN), BF)


def open_kernel(pieces_ref, tag_ref, at_ref, emb_ref, own_ref, other_ref, *refs):
    outs, par_o, bound_o, refs = refs[:4], refs[4], refs[5], refs[6:]
    heads, par, x, low, wa, wb, sem = refs[:4], refs[4], refs[5], refs[6], refs[7], refs[8], refs[9]
    moves = Moves(sem)
    first = rows_in(moves, at_ref, 0, own_ref, wa)
    third = moves.fetch(emb_ref, x)
    second = rows_in(moves, at_ref, 1, other_ref, wb)
    wait(*first)
    par[...] = wa[:, 3 * HALF:].astype(F32).T[:8, :]
    moves.send(par, par_o)
    wait(third)
    add_row(x, par[pl.ds(4 + tag_ref[0], 1), :], low, False)
    wait(*second)
    bound_o[0] = project_stage(low, (wa, wb), *heads)
    for a, b in zip(heads, outs):
        moves.send(a, b)
    moves.finish()


def open_visit(pieces, tag, at, embedded, own, other):
    outs = (full(D), full(D), full(D), VT, ((8, D), F32))
    scratch = like(outs + (full(D, F32), full(D), ((D, FIRST), BF), ((D, FIRST), BF)))
    got = pl.pallas_call(
        open_kernel,
        in_specs=[SMEM] * 3 + [ANY] * 3,
        out_specs=[ANY] * 5 + [SMEM],
        out_shape=[jax.ShapeDtypeStruct(s, t) for s, t in outs + (((1,), F32),)],
        scratch_shapes=scratch + [pltpu.SemaphoreType.DMA((160,))],
        compiler_params=pltpu.CompilerParams(vmem_limit_bytes=VMEM_LIMIT),
        cost_estimate=pl.CostEstimate(flops=4_000_000_000, bytes_accessed=8 << 20, transcendentals=0),
    )(pieces, tag, at, embedded, own, other)
    return got[:4], got[4], got[5]


def attend_kernel(pieces_ref, bound_ref, q_ref, k_ref, v_ref, vt_ref, *refs):
    outs, p_o, refs = refs[:3], refs[3], refs[4:]
    heads, work, row_sem, sem = refs[:6], refs[6:11], refs[11], refs[12]
    moves = Moves(sem)
    ends = piece_ends(pieces_ref)
    first = [moves.fetch(a, b) for a, b in zip((q_ref, k_ref, vt_ref, v_ref), heads[:2] + work[:1] + heads[2:3])]
    segment_codes(ends, work[1], work[2])
    wait(*first)

    def sent(i, rows):
        return [pltpu.make_async_copy(heads[n].at[rows, :], outs[n - 3].at[rows, :], row_sem.at[n - 3, i])
                for n in (3, 4)]

    def done(i, rows):
        for copy in sent(i, rows):
            copy.start()

    either(ends, bound_ref[0], False, heads, work, p_o, done)
    moves.send(heads[5], outs[2])
    for i in range(NQ):
        wait(*sent(i, pl.ds(i * QB, QB)))
    moves.finish()


def attend_visit(pieces, bound, q, k, v, vt):
    outs = HEADS_OUT[3:] + ((P_SHAPE, BF),)
    scratch = like(HEADS_OUT) + ATTEND_WORK + [pltpu.SemaphoreType.DMA((2, NQ)), pltpu.SemaphoreType.DMA((16,))]
    got = pl.pallas_call(
        attend_kernel,
        in_specs=[SMEM] * 2 + [ANY] * 4,
        out_specs=[ANY] * 4,
        out_shape=[jax.ShapeDtypeStruct(s, t) for s, t in outs],
        scratch_shapes=scratch,
        compiler_params=pltpu.CompilerParams(vmem_limit_bytes=VMEM_LIMIT),
        cost_estimate=pl.CostEstimate(flops=8_000_000_000, bytes_accessed=8 << 20, transcendentals=0),
    )(pieces, bound, q, k, v, vt)
    return got[:3], got[3]


SAVED = (full(D), full(1, F32), full(D), full(FF), full(FF), full(D), full(1, F32))


def middle_kernel(parts, pieces_ref, tag_ref, at_ref, emb_ref, mixed_ref, inv_ref, par_ref, fa_ref, fb_ref, *refs):
    ra_ref, rb_ref, cot_ref, refs = refs[:parts], refs[parts:2 * parts], refs[2 * parts], refs[2 * parts + 1:]
    saved_o, refs = refs[:7], refs[7:]
    result_o, p_o, base_o, gm_o, small_o, pro_o = refs[:5] + (refs[5:7],)
    keep_o, send_o, refs = refs[7:7 + parts], refs[7 + parts:7 + 2 * parts], refs[7 + 2 * parts:]
    x, result, cot, par, wf, wr, low, att, gm, small, small_b = (
        refs[0], refs[1], refs[2], refs[3], refs[4:6], refs[6:8], refs[8], refs[9], refs[10], refs[11], refs[12])
    saved, heads, sums, pro = refs[13:20], refs[20:26], refs[26:28], refs[28:30]
    work, sem = refs[30:35], refs[35]
    unit1, inv1, norm, act, slope, unit2, inv2 = saved
    mixed, inv = heads[3], heads[5]
    moves = Moves(sem)
    ends = piece_ends(pieces_ref)
    first = [moves.fetch(emb_ref, x), moves.fetch(mixed_ref, mixed), moves.fetch(par_ref, par)]
    second = parts_in(moves, at_ref, 0, ra_ref, wr[0]) + parts_in(moves, at_ref, 1, rb_ref, wr[1])
    segment_codes(ends, work[1], work[2])
    wait(*first)
    add_row(x, par[pl.ds(4 + tag_ref[0], 1), :], None, True)
    wait(*second)
    third = rows_in(moves, at_ref, 0, fa_ref, wf[0]) + rows_in(moves, at_ref, 1, fb_ref, wf[1])
    feed_stage(x, mixed, wr, par, x, *saved)
    for a, b in zip(saved, saved_o):
        moves.send(a, b)
    add_row(x, 0.0, low, False)
    wait(*third)
    bound = project_stage(low, wf, heads[0], heads[1], heads[2], work[0])
    either(ends, bound, True, heads, work, p_o, lambda i, rows: None)
    seed = moves.fetch(cot_ref, cot)
    moves.finish()
    feed_stage(x, mixed, wr, par, result, *saved)
    out = moves.fetch(result, result_o)
    wait(seed)
    total_stage(ends[-2], cot, unit2, inv2, par, cot, att, small)
    weight_stage(att, act, None, sums, DOWN, FF // 2)
    again = [moves.fetch(saved_o[n], saved[n]) for n in (3, 5, 6)]
    feed_back_stage(cot, att, unit1, inv1, slope, inv, wr, par, x, gm, small, slope, att)
    weight_stage(att, mixed, None, sums, 0, HALF)
    weight_stage(norm, slope, None, sums, HID, FF // 2)
    later = [moves.fetch(saved_o[n], saved[n]) for n in (0, 1, 2)] + [moves.fetch(inv_ref, inv)]
    wait(out)
    grads = slope.at[:, :3 * D]
    attend_back_stage(ends, True, *heads[:5], gm, work[0], p_o, work[3], work[4], result, cot, grads)
    later.append(moves.fetch(mixed_ref, mixed))
    input_stage(x, grads, wf, x)
    project_grad_stage(low, grads, None, pro)
    moves.send(pro[0], pro_o[0])
    moves.send(pro[1], pro_o[1])
    later.append(moves.fetch(saved_o[4], slope))
    wait(*again)
    total_stage(None, x, unit2, inv2, par, x, att, small_b)
    weight_stage(att, act, sums, sums, DOWN, FF // 2)
    wait(*later)
    feed_back_stage(x, att, unit1, inv1, slope, inv, wr, par, x, gm, small_b, slope, att)
    moves.send(x, base_o)
    moves.send(gm, gm_o)
    small[...] += small_b[...]
    moves.send(small, small_o)
    weight_stage(att, mixed, sums, sums, 0, HALF)
    weight_stage(norm, slope, sums, sums, HID, FF // 2)
    parts_out(moves, at_ref, 0, sums[0], keep_o)
    parts_out(moves, at_ref, 1, sums[1], send_o)
    moves.finish()


def middle(pieces, tag, at, embedded, mixed, inv, par, first, rest, cot):
    two = lambda *shape: ((shape, BF),) * 2
    small = ((32, D), F32)
    outs = (SAVED + (full(D, F32), (P_SHAPE, BF), full(D, F32), full(D), small) + two(D, 3 * HALF)
            + tuple((r.shape, BF) for r in rest))
    parts = len(rest) // 2
    scratch = like((full(D, F32),) * 3 + (((8, D), F32),) + two(D, FIRST) + two(D, REST) + (full(D),) * 3
                   + (small, small) + SAVED + HEADS_OUT + two(D, REST) + two(D, 3 * HALF)) + ATTEND_WORK
    got = call(functools.partial(middle_kernel, parts), outs, scratch, 4 * 64 + 200, 60_000_000_000,
               pieces, tag, at, embedded, mixed, inv, par, *first, *rest, cot)
    return got[7], got[9], got[10], got[11], got[12:14], got[14:]


def heads_back_kernel(pieces_ref, q_ref, k_ref, v_ref, mixed_ref, low_ref, gm_ref, p_ref, grads_o, *refs):
    heads, refs = refs[:6], refs[6:]
    p_slots, kt, dk, dv, grads, p_sem, sem = refs
    moves = Moves(sem)
    ends = piece_ends(pieces_ref)
    first = [moves.fetch(a, b) for a, b in zip((q_ref, k_ref, v_ref, mixed_ref, low_ref, gm_ref), heads)]
    attend_back_stage(ends, False, *heads, kt, p_ref, p_slots, p_sem, dk, dv, grads, first)
    moves.send(grads, grads_o)
    moves.finish()


def heads_back(pieces, heads, gm, p):
    scratch = like((full(D),) * 6)
    scratch += [VMEM((2,) + P_SHAPE[1:], BF), VMEM((HEADS2, 128, LEN), BF), VMEM((LEN, D), F32), VMEM((LEN, D), F32),
                VMEM((LEN, 3 * D), BF), pltpu.SemaphoreType.DMA((2,))]
    return call(heads_back_kernel, (full(3 * D),), scratch, 16, 18_000_000_000, pieces, *heads, gm, p)[0]


def last_kernel(tag_ref, at_ref, grads_ref, emb_ref, par_ref, base_ref, fa_ref, fb_ref, old_a_ref, old_b_ref, small_ref,
                *refs):
    out_o, keep_o, send_o = refs[:3]
    grads, x, low, par, base, wf, old, small, pro, sem = (
        refs[3], refs[4], refs[5], refs[6], refs[7], refs[8:10], refs[10:12], refs[12], refs[13:15], refs[15])
    moves = Moves(sem)
    first = [moves.fetch(a, b) for a, b in ((par_ref, par), (emb_ref, x), (grads_ref, grads))]
    second = [moves.fetch(a, b) for a, b in ((old_a_ref, old[0]), (old_b_ref, old[1]))]
    third = [moves.fetch(a, b) for a, b in ((base_ref, base), (small_ref, small))]
    third += rows_in(moves, at_ref, 0, fa_ref, wf[0]) + rows_in(moves, at_ref, 1, fb_ref, wf[1])
    wait(*first[:2])
    add_row(x, par[pl.ds(4 + tag_ref[0], 1), :], low, False)
    wait(*first[2:], *second)
    project_grad_stage(low, grads, old, pro)
    wait(*third)
    input_stage(base, grads, wf, base)
    moves.send(base, out_o)
    column = jnp.sum(base[...], axis=0, keepdims=True)
    norms = jnp.sum(small[...].reshape(4, 8, D), axis=1)
    tags = lax.broadcasted_iota(jnp.int32, (PAIRS, D), 0) == tag_ref[0]
    table = jnp.where(tags, jnp.broadcast_to(column, (PAIRS, D)), 0.0)
    stats = jnp.concatenate([norms, table, jnp.zeros((120, D), F32)], axis=0).T.astype(BF)
    for half, target in enumerate((keep_o, send_o)):
        pro[half][:, 3 * HALF:] = stats
        rows_out(moves, at_ref, half, pro[half], target)
    moves.finish()


def last_back(tag, at, part, grads, embedded, par, base, first, old, small):
    two = lambda *shape: ((shape, BF),) * 2
    scratch = like((full(3 * D), full(D, F32), full(D), ((8, D), F32), full(D, F32)) + two(D, FIRST)
                   + two(D, 3 * HALF) + (((32, D), F32),) + two(D, FIRST))
    return call(last_kernel, (full(D, F32),) + two(*part(FIRST)), scratch, 4 * 64 + 40, 8_000_000_000,
                tag, at, grads, embedded, par, base, *first, *old, small)


GROUP = ("dp", "tensor")


def plan(dp):
    if dp == 16:
        return (8, 4, 1, 2), (8, 4, 2, 1)
    bits = [1 << i for i in range(dp.bit_length() - 1)]
    side = len(bits) // 3
    x, y, z = bits[:side], bits[side:2 * side], bits[2 * side:]
    return tuple(z[::-1] + x[::-1] + y[::-1]), tuple(z[::-1] + y[::-1] + x[::-1])


def flip(value, dp, masks):
    pairs = [(d * 2 + t, (d ^ masks[t]) * 2 + t) for d in range(dp) for t in range(2)]
    return lax.ppermute(value, GROUP, pairs)


def swap(value):
    return lax.ppermute(value, "tensor", [(0, 1), (1, 0)])


def doubled(held, dp, masks):
    return jnp.concatenate([held, flip(held, dp, masks)], axis=0)


def after(value, *others):
    return lax.optimization_barrier((value, *others))[0]


def places(dp, mine, tensor):
    rel = jnp.arange(dp, dtype=jnp.int32) ^ mine
    found = []
    for order in plan(dp):
        found.append(sum(((rel & mask) // mask) << i for i, mask in enumerate(order)))
    return jnp.stack([jnp.where(tensor == t, found[0], found[1]) for t in (0, 1)])


def reduced(held, dp, masks, kind=BF):
    half = held.shape[0] // 2
    return add(held[:half], flip(held[half:], dp, masks), kind)


def add(a, b, kind=BF):
    return (a.astype(F32) + b.astype(F32)).astype(kind)


def body(embedded, piece_lengths, pair_tags, pair_embedding, w_query, w_key, w_value, w_output, w_hidden,
         w_down, first_gain, first_shift, second_gain, second_shift, cotangent):
    dp = lax.axis_size("dp")
    mine, tensor = lax.axis_index("dp"), lax.axis_index("tensor")
    rows = D // dp
    blocked = rows % 16 == 0
    pieces = lax.dynamic_index_in_dim(piece_lengths, tensor, 0, keepdims=False)
    tag = lax.dynamic_index_in_dim(pair_tags, tensor, 0, keepdims=True)
    small = jnp.concatenate([jnp.stack([first_gain, first_shift, second_gain, second_shift]), pair_embedding], axis=0)
    small = tn(small, jnp.eye(8, 128, dtype=BF)).astype(BF)
    at = places(dp, mine, tensor)

    def arranged(held):
        both = held, swap(held)
        if blocked:
            return both
        return tuple(h[at[i]].reshape(D, -1) for i, h in enumerate(both))

    def part(width):
        return (dp, rows, width) if blocked else (D, width)

    def swapped(keep, send):
        if not blocked:
            keep, send = (v.reshape(dp, rows, -1)[jnp.zeros((dp,), jnp.int32).at[at[i]].set(jnp.arange(dp))]
                          for i, v in enumerate((keep, send)))
        return add(keep, swap(send))

    def summed(held, phases):
        for i, masks in enumerate(phases):
            held = reduced(held, dp, masks, F32 if i == len(phases) - 1 else BF)
        return held[0]

    phases = list(zip(*plan(dp)))
    split = len(phases) - 1
    first = jnp.concatenate([w_query, w_key, w_value, small], axis=1)[None]
    rest = jnp.concatenate([w_output.T, w_hidden, w_down.T], axis=1)[None]
    for i, masks in enumerate(phases):
        first = doubled(first, dp, masks)
        if i < split - 1:
            rest = doubled(after(rest, first, *((tag, pieces, at) if i == 0 else ())), dp, masks)
        elif i == split - 1:
            rest = after(rest, first)
            arrived = flip(rest, dp, masks)
    first = arranged(after(first, rest))
    heads, par, bound = open_visit(pieces, tag, at, embedded, *first)
    rest = jnp.concatenate([after(rest, *heads), arrived], axis=0)
    rest, heads = lax.optimization_barrier((rest, heads))
    arrived, swapped_rest = flip(rest, dp, phases[-1]), swap(rest)
    q, k, v, vt = heads
    (mixed, low, inv), probs = attend_visit(pieces, bound, q, k, v, vt)
    arrived = after(arrived, mixed)
    if blocked:
        rest = (rest, arrived, swapped_rest, swap(arrived))
    else:
        rest = arranged(jnp.concatenate([rest, arrived], axis=0))
    result, base, gm, stats, old, sums = middle(pieces, tag, at, embedded, mixed, inv, par, first, rest, cotangent)
    if blocked:
        keep, keep_out, send, send_out = sums
        out = add(keep_out, swap(send_out))
        gm = after(gm, out)
        out = flip(out, dp, phases[-1])
        sums = add(add(keep, swap(send), F32), out)
    else:
        sums = reduced(swapped(*sums), dp, phases[-1])
    grads = heads_back(pieces, (q, k, v, mixed, low), gm, probs)
    sums, grads = lax.optimization_barrier((sums, grads))
    half = sums.shape[0] // 2
    out = flip(sums[half:], dp, phases[-2])
    grad, *da = last_back(tag, at, part, grads, embedded, par, base, first, old, stats)
    *da, out = lax.optimization_barrier((*da, out))
    sums = add(sums[:half], out)
    da = swapped(*da)
    sums = summed(sums, phases[-3::-1])
    da = summed(da, phases[::-1])
    small = da[:, 3 * HALF:3 * HALF + 8].T
    return (result, grad, small[4:], da[:, :HALF], da[:, HALF:2 * HALF], da[:, 2 * HALF:3 * HALF],
            sums[:, :HALF].T, sums[:, HID:DOWN], sums[:, DOWN:].T, small[0], small[1], small[2], small[3])


def solution(mesh):
    both = P(GROUP, None)
    params = (P("dp", "tensor"),) * 3 + (P("tensor", "dp"), P("dp", "tensor"), P("tensor", "dp"))
    in_specs = (both, P("dp", None), P("dp"), P(None, "dp")) + params + (P("dp"),) * 4 + (both,)
    out_specs = (both, both, P(None, "dp")) + params + (P("dp"),) * 4
    return jax.shard_map(body, mesh=mesh, in_specs=in_specs, out_specs=out_specs, check_vma=False)
```

```python
import functools
import math

import jax
import jax.numpy as jnp
from jax import lax
from jax.sharding import PartitionSpec as P
from jax.experimental import pallas as pl
from jax.experimental.pallas import tpu as pltpu

HEAD_DIM = 64
LEN = 1024
PIECES = 8
PAIRS = 4
D = 512
FF = 2048
HALF = 256
HEADS2 = 4
QB = 256
KB = 128
NQ = LEN // QB
NK = LEN // KB
BIG = 1e30
LOG2E = math.log2(math.e)
QSCALE = LOG2E / math.sqrt(HEAD_DIM)
KSCALE = math.log(2.0)
WIDTHS = (3, 5, 8)
EPS = 1e-5
C1 = math.sqrt(2.0 / math.pi)
C2 = C1 * 0.044715
F32 = jnp.float32
BF = jnp.bfloat16
VMEM_LIMIT = 60 * 1024 * 1024
TM = 512


def nn(a, b):
    return jnp.dot(a, b, preferred_element_type=F32)


def nt(a, b):
    return lax.dot_general(a, b, (((1,), (1,)), ((), ())), preferred_element_type=F32)


def tn(a, b):
    return lax.dot_general(a, b, (((0,), (0,)), ((), ())), preferred_element_type=F32)


def piece_ends(pieces_ref):
    ends, at = [], 0
    for j in range(PIECES):
        at = at + pieces_ref[j]
        ends.append(at)
    return ends


def window(block, ends):
    first = block * QB
    last = first + QB - 1
    low, high = jnp.int32(0), jnp.int32(LEN)
    for end in ends[:-1]:
        low = jnp.maximum(low, jnp.where(end <= first, end, 0))
        high = jnp.minimum(high, jnp.where(end > last, end, LEN))
    low = jnp.where(first >= ends[-2], first, low)
    high = jnp.where(last >= ends[-2], last + 1, high)
    return low // KB, (high + KB - 1) // KB


def over_widths(block, ends, run):
    low, high = window(block, ends)
    count = high - low
    previous = 0
    for wide in WIDTHS:
        begin = jnp.minimum(low, NK - wide)

        @pl.when((count > previous) & (count <= wide))
        def _(wide=wide, begin=begin):
            run(wide, pl.multiple_of(begin * KB, KB))

        previous = wide


def segment_codes(ends, segq_ref, segk_ref):
    rows = lax.broadcasted_iota(jnp.int32, (LEN, 128), 0)
    lanes = lax.broadcasted_iota(jnp.int32, (LEN, 128), 1)
    ids = jnp.zeros((LEN, 128), jnp.int32)
    for end in ends[:-1]:
        ids = ids + jnp.where(rows >= end, 1, 0)
    same = lanes == ids
    segk_ref[...] = jnp.where(same, 1.0, 0.0).astype(BF)
    free = (lanes >= PIECES) | (same & (lanes < PIECES - 1))
    segq_ref[...] = jnp.where(free, 0.0, -BIG).astype(BF)


def lane_half(shape):
    return lax.broadcasted_iota(jnp.int32, shape, 1) < HEAD_DIM


def two_heads(block):
    left = lane_half(block.shape)
    zero = jnp.zeros_like(block)
    return jnp.where(left, block, zero), jnp.where(left, zero, block)


def block_rows(index, size):
    return pl.ds(pl.multiple_of(index * size, size), size)


def head_norms(values, half):
    heads = lax.broadcasted_iota(jnp.int32, (HALF, 128), 0) // HEAD_DIM + half * (HALF // HEAD_DIM)
    pick = jnp.where(heads == lax.broadcasted_iota(jnp.int32, (HALF, 128), 1), 1.0, 0.0).astype(BF)
    return jnp.max(nn((values * values).astype(BF), pick), axis=0, keepdims=True)


def project_stage(x_ref, w_refs, q_ref, k_ref, v_ref, vt_ref):
    def chunk(i, carry):
        rows = block_rows(i, TM)
        low = x_ref[rows, :]
        q_top, k_top = carry
        for half in range(2):
            cols = slice(half * HALF, (half + 1) * HALF)
            queries = nn(low, w_refs[half][:, :HALF]) * QSCALE
            keys = nn(low, w_refs[half][:, HALF:2 * HALF])
            q_ref[rows, cols] = queries.astype(BF)
            k_ref[rows, cols] = keys.astype(BF)
            q_top = jnp.maximum(q_top, head_norms(queries, half))
            k_top = jnp.maximum(k_top, head_norms(keys, half))
            values = nn(low, w_refs[half][:, 2 * HALF:3 * HALF])
            v_ref[rows, cols] = values.astype(BF)
            for pair in range(2):
                vt_ref[half * 2 + pair, :128, rows] = values[:, pair * 128:(pair + 1) * 128].T.astype(BF)
        return q_top, k_top

    zero = jnp.zeros((1, 128), F32)
    q_top, k_top = lax.fori_loop(0, LEN // TM, chunk, (zero, zero))
    for pair in range(HEADS2):
        vt_ref[pair, 128:, :] = jnp.ones((16, LEN), BF)
    return jnp.max(q_top * k_top)


def pair_columns(pair):
    return pl.ds(pl.multiple_of(pair * 128, 128), 128)


def probs_copy(p_slots, p_hbm, sem, i, wide, out):
    slot = i % 2
    here = p_slots.at[slot, :, pl.ds(0, wide * KB), :]
    there = p_hbm.at[i, :, pl.ds(0, wide * KB), :]
    return pltpu.make_async_copy(here, there, sem.at[slot]) if out else pltpu.make_async_copy(there, here, sem.at[slot])


def attend_stage(ends, shifted, resident, q_ref, k_ref, v_ref, mixed_ref, low_ref, inv_ref, vt_ref, segq_ref, segk_ref,
                 p_slots, p_out, p_sem, done):
    def block(i, carry):
        rows = block_rows(i, QB)
        p_ref = p_slots.at[i % 2]

        @pl.when(i >= 2)
        def _():
            over_widths(i - 2, ends, lambda wide, begin: probs_copy(p_slots, p_out, p_sem, i - 2, wide, True).wait())

        pad = lax.broadcasted_iota(jnp.int32, (QB, 128), 0) + i * QB >= ends[-2]

        def run(wide, begin):
            keys = pl.ds(begin, wide * KB)
            segq = segq_ref[rows, :]

            def query(cols):
                even, odd = two_heads(q_ref[rows, cols])
                return jnp.concatenate(
                    [jnp.concatenate([even, segq], axis=1), jnp.concatenate([odd, segq], axis=1)], axis=0)

            def score(query, cols, keys):
                return nt(jnp.concatenate([k_ref[keys, cols], segk_ref[keys, :]], axis=1), query)

            def finish(pair, cols, out):
                inv = 1.0 / jnp.maximum(out[128:129, :], 1e-30)
                inv_ref[pl.ds(i * HEADS2 + pair, 1), :] = inv
                inv_both = jnp.concatenate(
                    [jnp.broadcast_to(inv[:, :QB], (64, QB)), jnp.broadcast_to(inv[:, QB:], (64, QB))], axis=0)
                exact = (jnp.concatenate([out[:64, :QB], out[64:128, QB:]], axis=0) * inv_both).T
                mixed = jnp.where(pad, v_ref[rows, cols].astype(F32), exact).astype(BF)
                mixed_ref[rows, cols] = mixed
                low_ref[rows, cols] = (exact - mixed.astype(F32)).astype(BF)

            def shifted_pair(pair, carry):
                cols = pair_columns(pair)
                asked = query(cols)

                def part(c):
                    return score(asked, cols, pl.ds(pl.multiple_of(begin + c * KB, KB), KB))

                top = lax.fori_loop(0, wide, lambda c, top: jnp.maximum(top, jnp.max(part(c), axis=0, keepdims=True)),
                                    jnp.full((1, 2 * QB), -2 * BIG, F32))

                def add_part(c, out):
                    at = pl.multiple_of(c * KB, KB)
                    probs = jnp.exp2(part(c) - top).astype(BF)
                    p_ref[pair, pl.ds(at, KB), :] = probs
                    return out + nn(vt_ref[pair, :, pl.ds(pl.multiple_of(begin + at, KB), KB)], probs)

                finish(pair, cols, lax.fori_loop(0, wide, add_part, jnp.zeros((144, 2 * QB), F32)))
                return carry

            def group(g, carry):
                pairs = [2 * g + r for r in range(2)]
                cols = [pair_columns(pair) for pair in pairs]
                scores = [score(query(c), c, keys) for c in cols]
                outs = []
                for pair, value in zip(pairs, scores):
                    probs = jnp.exp2(value).astype(BF)
                    p_ref[pair, :wide * KB, :] = probs
                    outs.append(nn(vt_ref[pair, :, keys], probs))
                for args in zip(pairs, cols, outs):
                    finish(*args)
                return carry

            if shifted:
                lax.fori_loop(0, HEADS2, shifted_pair, 0)
            else:
                lax.fori_loop(0, HEADS2 // 2, group, 0)
            out = probs_copy(p_slots, p_out, p_sem, i, wide, True)
            if resident:
                pl.when(i < NQ - 2)(out.start)
            else:
                out.start()

        over_widths(i, ends, run)
        done(i, rows)
        return carry

    lax.fori_loop(0, NQ, block, 0)
    if not resident:
        for i in range(NQ - 2, NQ):
            over_widths(i, ends, lambda wide, begin, i=i: probs_copy(p_slots, p_out, p_sem, i, wide, True).wait())


def grad_columns(part, pair):
    at = pair // 2 * 3 * HALF + part * HALF + pair % 2 * 128
    return slice(at, at + 128)


def attend_back_stage(ends, resident, q_ref, k_ref, v_ref, mixed_ref, low_ref, grad_ref, kt_ref, p_in, p_slots, p_sem,
                      dk_ref, dv_ref, grads_ref, first=(), later=()):
    if not resident:
        for i in (NQ - 1, NQ - 2):
            over_widths(i, ends, lambda wide, begin, i=i: probs_copy(p_slots, p_in, p_sem, i, wide, False).start())
    dk_ref[...] = jnp.zeros_like(dk_ref)
    dv_ref[...] = jnp.zeros_like(dv_ref)
    wait(*first)
    for pair in range(HEADS2):
        kt_ref[pair, :128, :] = k_ref[:, pair * 128:(pair + 1) * 128].astype(F32).T.astype(BF)
    span = [slice(pair * 128, (pair + 1) * 128) for pair in range(HEADS2)]

    def block(j, carry):
        i = NQ - 1 - j
        rows = block_rows(i, QB)
        p_ref = p_slots.at[i % 2]

        def run(wide, begin):
            keys = pl.ds(begin, wide * KB)
            arrived = probs_copy(p_slots, p_in, p_sem, i, wide, False)
            if resident:
                pl.when(j >= 2)(arrived.wait)
            else:
                arrived.wait()

            def outer(cols):
                return jnp.concatenate(two_heads(grad_ref[rows, cols]), axis=0)

            def slope(cols):
                grad = grad_ref[rows, cols]
                exact = mixed_ref[rows, cols].astype(F32) + low_ref[rows, cols].astype(F32)
                inner = grad.astype(F32) * exact
                high = inner.astype(BF)
                rest = pltpu.roll(inner - high.astype(F32), HEAD_DIM, 1).astype(BF)
                left = lane_half(inner.shape)
                inner = jnp.concatenate([jnp.where(left, high, rest), jnp.where(left, rest, high)], axis=0)
                both = jnp.concatenate([outer(cols), inner], axis=1)
                value = jnp.concatenate([v_ref[keys, cols], jnp.full((wide * KB, 128), -1.0, BF)], axis=1)
                return nt(value, both)

            def rest(pair, cols, target, scores):
                query = jnp.concatenate(two_heads(q_ref[rows, cols]), axis=0)
                dk_ref[keys, cols] += nn(scores, query)
                out = nn(kt_ref[pair, :128, keys], scores)
                out = jnp.concatenate([out[:64, :QB], out[64:, QB:]], axis=0)
                grads_ref[rows, target] = (out.T * (HEAD_DIM ** -0.5)).astype(BF)

            def group(g, carry):
                pairs = [2 * g + r for r in range(2)]
                cols = [pair_columns(pair) for pair in pairs]
                slopes = [slope(c) for c in cols]
                scores = []
                for pair, c, value in zip(pairs, cols, slopes):
                    probs = p_ref[pair, :wide * KB, :]
                    scores.append((probs.astype(F32) * value).astype(BF))
                    dv_ref[keys, c] += nn(probs, outer(c))
                for r in range(2):
                    target = pl.ds(pl.multiple_of(g * 3 * HALF + r * 128, 128), 128)
                    rest(pairs[r], cols[r], target, scores[r])
                return carry

            lax.fori_loop(0, HEADS2 // 2, group, 0)

        over_widths(i, ends, run)

        if later:
            @pl.when(j == 0)
            def _():
                for copy in later:
                    copy.start()

        @pl.when(j < NQ - 2)
        def _():
            over_widths(i - 2, ends, lambda wide, begin: probs_copy(p_slots, p_in, p_sem, i - 2, wide, False).start())

        return carry

    lax.fori_loop(0, NQ, block, 0)
    for pair in range(HEADS2):
        grads_ref[:, grad_columns(1, pair)] = (dk_ref[:, span[pair]] * KSCALE).astype(BF)
        grads_ref[:, grad_columns(2, pair)] = dv_ref[:, span[pair]].astype(BF)


def attend_stage_wide(ends, shifted, resident, q_ref, k_ref, v_ref, mixed_ref, low_ref, inv_ref, vt_ref, segq_ref, segk_ref,
                 p_slots, p_out, p_sem, done):
    def block(i, carry):
        rows = block_rows(i, QB)
        p_ref = p_slots.at[i % 2]

        @pl.when(i >= 2)
        def _():
            over_widths(i - 2, ends, lambda wide, begin: probs_copy(p_slots, p_out, p_sem, i - 2, wide, True).wait())

        def run(wide, begin):
            keys = pl.ds(begin, wide * KB)
            segq = segq_ref[rows, :]
            segk = segk_ref[keys, :]
            pad = lax.broadcasted_iota(jnp.int32, (QB, 128), 0) + i * QB >= ends[-2]
            span = [slice(pair * 128, (pair + 1) * 128) for pair in range(HEADS2)]

            def score(pair):
                even, odd = two_heads(q_ref[rows, span[pair]])
                query = jnp.concatenate(
                    [jnp.concatenate([even, segq], axis=1), jnp.concatenate([odd, segq], axis=1)], axis=0)
                key = jnp.concatenate([k_ref[keys, span[pair]], segk], axis=1)
                return nt(key, query)

            def soften(pair, scores):
                probs = jnp.exp2(scores).astype(BF)
                p_ref[pair, :wide * KB, :] = probs
                return probs

            def mix(pair, probs):
                return nn(vt_ref[pair, :, keys], probs)

            def finish(pair, out):
                cols = span[pair]
                inv = 1.0 / jnp.maximum(out[128:129, :], 1e-30)
                inv_ref[pl.ds(i * HEADS2 + pair, 1), :] = inv
                inv_both = jnp.concatenate(
                    [jnp.broadcast_to(inv[:, :QB], (64, QB)), jnp.broadcast_to(inv[:, QB:], (64, QB))], axis=0)
                exact = (jnp.concatenate([out[:64, :QB], out[64:128, QB:]], axis=0) * inv_both).T
                mixed = jnp.where(pad, v_ref[rows, cols].astype(F32), exact).astype(BF)
                mixed_ref[rows, cols] = mixed
                low_ref[rows, cols] = (exact - mixed.astype(F32)).astype(BF)

            s = {0: score(0), 1: score(1)}
            p, o = {}, {}
            for pair in range(HEADS2):
                p[pair] = soften(pair, s[pair])
                if pair + 2 < HEADS2:
                    s[pair + 2] = score(pair + 2)
                if pair:
                    o[pair - 1] = mix(pair - 1, p[pair - 1])
                if pair > 1:
                    finish(pair - 2, o[pair - 2])
            out = probs_copy(p_slots, p_out, p_sem, i, wide, True)
            if resident:
                pl.when(i < NQ - 2)(out.start)
            else:
                out.start()
            o[HEADS2 - 1] = mix(HEADS2 - 1, p[HEADS2 - 1])
            finish(HEADS2 - 2, o[HEADS2 - 2])
            finish(HEADS2 - 1, o[HEADS2 - 1])

        over_widths(i, ends, run)
        done(i, rows)
        return carry

    lax.fori_loop(0, NQ, block, 0)
    if not resident:
        for i in range(NQ - 2, NQ):
            over_widths(i, ends, lambda wide, begin, i=i: probs_copy(p_slots, p_out, p_sem, i, wide, True).wait())


def attend_back_stage_wide(ends, resident, q_ref, k_ref, v_ref, mixed_ref, low_ref, grad_ref, kt_ref, p_in, p_slots, p_sem,
                      dk_ref, dv_ref, grads_ref, first=(), later=()):
    if not resident:
        for i in (NQ - 1, NQ - 2):
            over_widths(i, ends, lambda wide, begin, i=i: probs_copy(p_slots, p_in, p_sem, i, wide, False).start())
    dk_ref[...] = jnp.zeros_like(dk_ref)
    dv_ref[...] = jnp.zeros_like(dv_ref)
    wait(*first)
    for pair in range(HEADS2):
        kt_ref[pair, :128, :] = k_ref[:, pair * 128:(pair + 1) * 128].astype(F32).T.astype(BF)
    span = [slice(pair * 128, (pair + 1) * 128) for pair in range(HEADS2)]

    def block(j, carry):
        i = NQ - 1 - j
        rows = block_rows(i, QB)
        p_ref = p_slots.at[i % 2]

        def run(wide, begin):
            keys = pl.ds(begin, wide * KB)
            arrived = probs_copy(p_slots, p_in, p_sem, i, wide, False)
            if resident:
                pl.when(j >= 2)(arrived.wait)
            else:
                arrived.wait()

            def outer(pair):
                return jnp.concatenate(two_heads(grad_ref[rows, span[pair]]), axis=0)

            def slope(pair):
                grad = grad_ref[rows, span[pair]]
                exact = mixed_ref[rows, span[pair]].astype(F32) + low_ref[rows, span[pair]].astype(F32)
                inner = grad.astype(F32) * exact
                high = inner.astype(BF)
                rest = pltpu.roll(inner - high.astype(F32), HEAD_DIM, 1).astype(BF)
                left = lane_half(inner.shape)
                inner = jnp.concatenate([jnp.where(left, high, rest), jnp.where(left, rest, high)], axis=0)
                both = jnp.concatenate([outer(pair), inner], axis=1)
                value = jnp.concatenate([v_ref[keys, span[pair]], jnp.full((wide * KB, 128), -1.0, BF)], axis=1)
                return nt(value, both)

            def bend(pair, slope):
                return (p_ref[pair, :wide * KB, :].astype(F32) * slope).astype(BF)

            def values(pair):
                dv_ref[keys, span[pair]] += nn(p_ref[pair, :wide * KB, :], outer(pair))

            def rest(pair, scores):
                query = jnp.concatenate(two_heads(q_ref[rows, span[pair]]), axis=0)
                dk_ref[keys, span[pair]] += nn(scores, query)
                out = nn(kt_ref[pair, :128, keys], scores)
                out = jnp.concatenate([out[:64, :QB], out[64:, QB:]], axis=0)
                grads_ref[rows, grad_columns(0, pair)] = (out.T * (HEAD_DIM ** -0.5)).astype(BF)

            s = {0: slope(0), 1: slope(1)}
            d = {}
            for pair in range(HEADS2):
                d[pair] = bend(pair, s[pair])
                values(pair)
                if pair + 2 < HEADS2:
                    s[pair + 2] = slope(pair + 2)
                if pair:
                    rest(pair - 1, d[pair - 1])
            rest(HEADS2 - 1, d[HEADS2 - 1])

        over_widths(i, ends, run)

        if later:
            @pl.when(j == 0)
            def _():
                for copy in later:
                    copy.start()

        @pl.when(j < NQ - 2)
        def _():
            over_widths(i - 2, ends, lambda wide, begin: probs_copy(p_slots, p_in, p_sem, i - 2, wide, False).start())

        return carry

    lax.fori_loop(0, NQ, block, 0)
    for pair in range(HEADS2):
        grads_ref[:, grad_columns(1, pair)] = (dk_ref[:, span[pair]] * KSCALE).astype(BF)
        grads_ref[:, grad_columns(2, pair)] = dv_ref[:, span[pair]].astype(BF)


def unit_rows(values):
    center = values - jnp.mean(values, axis=-1, keepdims=True)
    spread = jnp.mean(center * center, axis=-1, keepdims=True)
    inv = lax.rsqrt(spread + EPS)
    return center * inv, inv


HID = HALF
DOWN = HALF + FF // 2
REST = HALF + FF
FIRST = 3 * HALF + 128
STEP = 512
PER_HALF = FF // 2 // STEP


def feed_stage(x_ref, mixed_ref, w_refs, par_ref, out_ref, unit1_ref, inv1_ref, norm_ref, act_ref, slope_ref,
               unit2_ref, inv2_ref, tm=512):
    def chunk(i, carry):
        rows = block_rows(i, tm)
        summed = x_ref[rows, :]
        for half in range(2):
            summed = summed + nt(mixed_ref[rows, half * HALF:(half + 1) * HALF], w_refs[half][:, :HALF])
        unit, inv = unit_rows(summed)
        unit1_ref[rows, :] = unit.astype(BF)
        inv1_ref[rows, :] = inv
        normed = unit * par_ref[0:1, :] + par_ref[1:2, :]
        low = normed.astype(BF)
        norm_ref[rows, :] = low
        for part in range(2 * PER_HALF):
            cols = slice(part * STEP, (part + 1) * STEP)
            at = HID + part % PER_HALF * STEP
            hidden = nn(low, w_refs[part // PER_HALF][:, at:at + STEP])
            square = hidden * hidden
            gate = 0.5 + 0.5 * jnp.tanh(hidden * (C1 + C2 * square))
            act_ref[rows, cols] = (hidden * gate).astype(BF)
            slope_ref[rows, cols] = (gate + gate * (1.0 - gate) * hidden * (2 * C1 + 6 * C2 * square)).astype(BF)
        total = normed
        for half in range(2):
            total = total + nt(act_ref[rows, half * (FF // 2):(half + 1) * (FF // 2)], w_refs[half][:, DOWN:])
        unit, inv = unit_rows(total)
        unit2_ref[rows, :] = unit.astype(BF)
        inv2_ref[rows, :] = inv
        out_ref[rows, :] = unit * par_ref[2:3, :] + par_ref[3:4, :]
        return carry

    lax.fori_loop(0, LEN // tm, chunk, 0)


def unit_back(grad, unit, inv, gain):
    scaled = grad * gain
    first = jnp.mean(scaled, axis=-1, keepdims=True)
    second = jnp.mean(scaled * unit, axis=-1, keepdims=True)
    return inv * (scaled - first - unit * second)


def fold_rows(values):
    return jnp.sum(values.reshape(-1, 8, values.shape[-1]), axis=0)


def total_stage(limit, grad_ref, unit2_ref, inv2_ref, par_ref, total_ref, low_ref, small_ref, tm=1024):
    def chunk(i, carry):
        rows = block_rows(i, tm)
        grad = grad_ref[rows, :]
        grad = jnp.where(lax.broadcasted_iota(jnp.int32, grad.shape, 0) + i * tm < limit, grad, 0.0)
        unit2 = unit2_ref[rows, :].astype(F32)
        small_ref[16:24, :] += fold_rows(grad * unit2)
        small_ref[24:32, :] += fold_rows(grad)
        total = unit_back(grad, unit2, inv2_ref[rows, :], par_ref[2:3, :])
        total_ref[rows, :] = total
        low_ref[rows, :] = total.astype(BF)
        return carry

    lax.fori_loop(0, LEN // tm, chunk, 0)


def feed_back_stage(total_ref, low_ref, unit1_ref, inv1_ref, slope_ref, inv_ref, w_refs, par_ref,
                    base_ref, gm_ref, small_ref, hid_ref, att_ref, tm=512):
    def chunk(i, carry):
        rows = block_rows(i, tm)
        low = low_ref[rows, :]
        for part in range(2 * PER_HALF):
            cols = slice(part * STEP, (part + 1) * STEP)
            at = DOWN + part % PER_HALF * STEP
            slope = nn(low, w_refs[part // PER_HALF][:, at:at + STEP])
            hid_ref[rows, cols] = (slope * slope_ref[rows, cols].astype(F32)).astype(BF)
        normed = total_ref[rows, :]
        for half in range(2):
            normed = normed + nt(hid_ref[rows, half * (FF // 2):(half + 1) * (FF // 2)], w_refs[half][:, HID:DOWN])
        unit1 = unit1_ref[rows, :].astype(F32)
        small_ref[0:8, :] += fold_rows(normed * unit1)
        small_ref[8:16, :] += fold_rows(normed)
        summed = unit_back(normed, unit1, inv1_ref[rows, :], par_ref[0:1, :])
        base_ref[rows, :] = summed
        low = summed.astype(BF)
        att_ref[rows, :] = low
        for half in range(2):
            grad = nn(low, w_refs[half][:, :HALF])
            for pair in range(2):
                for part in range(tm // QB):
                    inv = inv_ref[pl.ds((i * (tm // QB) + part) * HEADS2 + half * 2 + pair, 1), :]
                    inv = jnp.concatenate([jnp.broadcast_to(inv[:, :QB], (64, QB)),
                                           jnp.broadcast_to(inv[:, QB:], (64, QB))], axis=0).T
                    value = grad[part * QB:(part + 1) * QB, pair * 128:(pair + 1) * 128] * inv
                    gm_ref[pl.ds(pl.multiple_of(i * tm + part * QB, QB), QB),
                           half * HALF + pair * 128:half * HALF + (pair + 1) * 128] = value.astype(BF)
        return carry

    lax.fori_loop(0, LEN // tm, chunk, 0)


def weight_stage(left_ref, right_ref, olds, outs, offset, width):
    cols = slice(offset, offset + width)
    for half in range(2):
        value = tn(left_ref[...], right_ref[:, half * width:(half + 1) * width])
        if olds is not None:
            value = value + olds[half][:, cols].astype(F32)
        outs[half][:, cols] = value.astype(BF)


def project_grad_stage(low_ref, grads_ref, olds, outs):
    for half in range(2):
        value = tn(low_ref[...], grads_ref[:, half * 3 * HALF:(half + 1) * 3 * HALF])
        if olds is not None:
            value = value + olds[half][...].astype(F32)
        outs[half][:, :3 * HALF] = value.astype(BF)


def input_stage(base_ref, grads_ref, w_refs, out_ref, size=LEN):
    def chunk(i, carry):
        rows = block_rows(i, TM)
        value = base_ref[rows, :]
        for half in range(2):
            value = value + nt(grads_ref[rows, half * 3 * HALF:(half + 1) * 3 * HALF], w_refs[half][:, :3 * HALF])
        out_ref[rows, :] = value
        return carry

    lax.fori_loop(0, size // TM, chunk, 0)


def add_row(x_ref, row, low_ref, keep):
    def chunk(i, carry):
        rows = block_rows(i, TM)
        value = x_ref[rows, :] + row
        if keep:
            x_ref[rows, :] = value
        if low_ref is not None:
            low_ref[rows, :] = value.astype(BF)
        return carry

    lax.fori_loop(0, LEN // TM, chunk, 0)


LIMIT = 64.0 ** 2
P_SHAPE = (NQ, HEADS2, LEN, 2 * QB)
VMEM = pltpu.VMEM


class Moves:
    def __init__(self, sem):
        self.sem, self.count, self.open = sem, 0, []

    def make(self, source, target):
        copy = pltpu.make_async_copy(source, target, self.sem.at[self.count])
        self.count += 1
        return copy

    def fetch(self, source, target):
        copy = self.make(source, target)
        copy.start()
        return copy

    def send(self, source, target):
        copy = self.fetch(source, target)
        self.open.append(copy)
        return copy

    def finish(self):
        wait(*self.open)
        self.open = []


def wait(*copies):
    for copy in copies:
        copy.wait()


class Group:
    def __init__(self, moves, copies, whole):
        self.copies, self.whole = copies, pltpu.make_async_copy(whole, whole, moves.sem.at[moves.count])
        moves.count += 1

    def start(self):
        for copy in self.copies:
            copy()

    def wait(self):
        self.whole.wait()


def pick(index, count, make):
    def start():
        pl.when(index < count)(lambda: make(0, jnp.minimum(index, count - 1)).start())
        pl.when(index >= count)(lambda: make(1, jnp.maximum(index - count, 0)).start())

    return start


def parts_in(moves, at_ref, half, sources, target):
    if len(sources) == 1:
        return rows_in(moves, at_ref, half, sources[0], target)
    count, rows, _ = sources[0].shape
    sem = moves.sem.at[moves.count]
    copies = [pick(at_ref[half, b], count, lambda ref, place, b=b: pltpu.make_async_copy(
        sources[ref].at[place], target.at[pl.ds(b * rows, rows), :], sem)) for b in range(2 * count)]
    group = Group(moves, copies, target)
    group.start()
    return [group]


def parts_out(moves, at_ref, half, source, targets):
    if len(targets) == 1:
        return rows_out(moves, at_ref, half, source, targets[0])
    count, rows, _ = targets[0].shape
    sem = moves.sem.at[moves.count]
    copies = [pick(at_ref[half, b], count, lambda ref, place, b=b: pltpu.make_async_copy(
        source.at[pl.ds(b * rows, rows), :], targets[ref].at[place], sem)) for b in range(2 * count)]
    group = Group(moves, copies, source)
    group.start()
    moves.open.append(group)


def rows_in(moves, at_ref, half, source, target):
    if len(source.shape) == 2:
        return [moves.fetch(source, target)]
    dp, rows, _ = source.shape
    sem = moves.sem.at[moves.count]
    group = Group(moves, [pltpu.make_async_copy(source.at[at_ref[half, b]], target.at[pl.ds(b * rows, rows), :], sem).start
                          for b in range(dp)], target)
    group.start()
    return [group]


def rows_out(moves, at_ref, half, source, target):
    if len(target.shape) == 2:
        moves.send(source, target)
        return
    dp, rows, _ = target.shape
    sem = moves.sem.at[moves.count]
    group = Group(moves, [pltpu.make_async_copy(source.at[pl.ds(b * rows, rows), :], target.at[at_ref[half, b]], sem).start
                          for b in range(dp)], source)
    group.start()
    moves.open.append(group)


ANY = pl.BlockSpec(memory_space=pl.ANY)
SMEM = pl.BlockSpec(memory_space=pltpu.SMEM)


def like(shapes):
    return [VMEM(s, t) for s, t in shapes]


def full(width, kind=BF):
    return ((LEN, width), kind)


def call(kernel, outs, scratch, sems, flops, *args):
    smem = sum(a.dtype == jnp.int32 for a in args)
    return pl.pallas_call(
        kernel,
        in_specs=[SMEM] * smem + [ANY] * (len(args) - smem),
        out_specs=[ANY] * len(outs),
        out_shape=[jax.ShapeDtypeStruct(s, t) for s, t in outs],
        scratch_shapes=scratch + [pltpu.SemaphoreType.DMA((sems,))],
        compiler_params=pltpu.CompilerParams(vmem_limit_bytes=VMEM_LIMIT),
        cost_estimate=pl.CostEstimate(flops=flops, bytes_accessed=8 << 20, transcendentals=0),
    )(*args)


HEADS_OUT = (full(D), full(D), full(D), full(D), full(D), ((NQ * HEADS2, 2 * QB), F32))
ATTEND_WORK = [VMEM((HEADS2, 144, LEN), BF), VMEM((LEN, 128), BF), VMEM((LEN, 128), BF),
               VMEM((2,) + P_SHAPE[1:], BF), pltpu.SemaphoreType.DMA((2,))]


def either(ends, bound, resident, heads, work, p_out, done):
    for shifted in (False, True):
        @pl.when((bound > LIMIT) if shifted else (bound <= LIMIT))
        def _(shifted=shifted):
            stage = attend_stage if shifted or resident else attend_stage_wide
            stage(ends, shifted, resident, *heads, *work[:4], p_out, work[4], done)


VT = ((HEADS2, 144, LEN), BF)


def open_kernel(pieces_ref, tag_ref, at_ref, emb_ref, own_ref, other_ref, *refs):
    outs, par_o, bound_o, refs = refs[:4], refs[4], refs[5], refs[6:]
    heads, par, x, low, wa, wb, sem = refs[:4], refs[4], refs[5], refs[6], refs[7], refs[8], refs[9]
    moves = Moves(sem)
    first = rows_in(moves, at_ref, 0, own_ref, wa)
    third = moves.fetch(emb_ref, x)
    second = rows_in(moves, at_ref, 1, other_ref, wb)
    wait(*first)
    par[...] = wa[:, 3 * HALF:].astype(F32).T[:8, :]
    moves.send(par, par_o)
    wait(third)
    add_row(x, par[pl.ds(4 + tag_ref[0], 1), :], low, False)
    wait(*second)
    bound_o[0] = project_stage(low, (wa, wb), *heads)
    for a, b in zip(heads, outs):
        moves.send(a, b)
    moves.finish()


def open_visit(pieces, tag, at, embedded, own, other):
    outs = (full(D), full(D), full(D), VT, ((8, D), F32))
    scratch = like(outs + (full(D, F32), full(D), ((D, FIRST), BF), ((D, FIRST), BF)))
    got = pl.pallas_call(
        open_kernel,
        in_specs=[SMEM] * 3 + [ANY] * 3,
        out_specs=[ANY] * 5 + [SMEM],
        out_shape=[jax.ShapeDtypeStruct(s, t) for s, t in outs + (((1,), F32),)],
        scratch_shapes=scratch + [pltpu.SemaphoreType.DMA((8,))],
        compiler_params=pltpu.CompilerParams(vmem_limit_bytes=VMEM_LIMIT),
        cost_estimate=pl.CostEstimate(flops=4_000_000_000, bytes_accessed=8 << 20, transcendentals=0),
    )(pieces, tag, at, embedded, own, other)
    return got[:4], got[4], got[5]


def attend_kernel(pieces_ref, bound_ref, q_ref, k_ref, v_ref, vt_ref, *refs):
    outs, p_o, refs = refs[:3], refs[3], refs[4:]
    heads, work, row_sem, sem = refs[:6], refs[6:11], refs[11], refs[12]
    moves = Moves(sem)
    ends = piece_ends(pieces_ref)
    first = [moves.fetch(a, b) for a, b in zip((q_ref, k_ref, vt_ref, v_ref), heads[:2] + work[:1] + heads[2:3])]
    segment_codes(ends, work[1], work[2])
    wait(*first)

    def sent(i, rows):
        return [pltpu.make_async_copy(heads[n].at[rows, :], outs[n - 3].at[rows, :], row_sem.at[n - 3, i])
                for n in (3, 4)]

    def done(i, rows):
        for copy in sent(i, rows):
            copy.start()

    either(ends, bound_ref[0], False, heads, work, p_o, done)
    moves.send(heads[5], outs[2])
    for i in range(NQ):
        wait(*sent(i, pl.ds(i * QB, QB)))
    moves.finish()


def attend_visit(pieces, bound, q, k, v, vt):
    outs = HEADS_OUT[3:] + ((P_SHAPE, BF),)
    scratch = like(HEADS_OUT) + ATTEND_WORK + [pltpu.SemaphoreType.DMA((2, NQ)), pltpu.SemaphoreType.DMA((8,))]
    got = pl.pallas_call(
        attend_kernel,
        in_specs=[SMEM] * 2 + [ANY] * 4,
        out_specs=[ANY] * 4,
        out_shape=[jax.ShapeDtypeStruct(s, t) for s, t in outs],
        scratch_shapes=scratch,
        compiler_params=pltpu.CompilerParams(vmem_limit_bytes=VMEM_LIMIT),
        cost_estimate=pl.CostEstimate(flops=8_000_000_000, bytes_accessed=8 << 20, transcendentals=0),
    )(pieces, bound, q, k, v, vt)
    return got[:3], got[3]


SAVED = (full(D), full(1, F32), full(D), full(FF), full(FF), full(D), full(1, F32))


def middle_kernel(parts, pieces_ref, tag_ref, at_ref, emb_ref, mixed_ref, inv_ref, par_ref, fa_ref, fb_ref, *refs):
    ra_ref, rb_ref, cot_ref, refs = refs[:parts], refs[parts:2 * parts], refs[2 * parts], refs[2 * parts + 1:]
    saved_o, refs = refs[:7], refs[7:]
    result_o, p_o, base_o, gm_o, small_o, pro_o = refs[:5] + (refs[5:7],)
    keep_o, send_o, refs = refs[7:7 + parts], refs[7 + parts:7 + 2 * parts], refs[7 + 2 * parts:]
    x, base, cot, par, wf, wr, low, att, gm, small = (
        refs[0], refs[1], refs[2], refs[3], refs[4:6], refs[6:8], refs[8], refs[9], refs[10], refs[11])
    saved, heads, sums = refs[12:19], refs[19:25], refs[25:27]
    work, sem = refs[27:32], refs[32]
    unit1, inv1, norm, act, slope, unit2, inv2 = saved
    mixed, inv = heads[3], heads[5]
    moves = Moves(sem)
    ends = piece_ends(pieces_ref)
    first = [moves.fetch(emb_ref, x), moves.fetch(mixed_ref, mixed), moves.fetch(par_ref, par)]
    second = parts_in(moves, at_ref, 0, ra_ref, wr[0]) + parts_in(moves, at_ref, 1, rb_ref, wr[1])
    segment_codes(ends, work[1], work[2])
    wait(*first)
    add_row(x, par[pl.ds(4 + tag_ref[0], 1), :], None, True)
    wait(*second)
    third = rows_in(moves, at_ref, 0, fa_ref, wf[0]) + rows_in(moves, at_ref, 1, fb_ref, wf[1])
    for ref in (small, *sums):
        ref[...] = jnp.zeros_like(ref)
    sent = [moves.make(a, b) for a, b in zip(saved, saved_o)]
    seed = moves.make(cot_ref, cot)

    def forward(v, carry):
        feed_stage(x, mixed, wr, par, x, *saved)

        @pl.when(v == 0)
        def _():
            for copy in sent:
                copy.start()
            add_row(x, 0.0, low, False)
            wait(*third)
            bound = project_stage(low, wf, heads[0], heads[1], heads[2], work[0])
            either(ends, bound, True, heads, work, p_o, lambda i, rows: None)
            seed.start()
            wait(*sent)

        return carry

    lax.fori_loop(0, 2, forward, 0)
    out = moves.fetch(x, result_o)
    wait(seed)
    early = [moves.make(saved_o[n], saved[n]) for n in (3, 5, 6)]
    late = [moves.make(saved_o[n], saved[n]) for n in (0, 1, 2)] + [moves.make(inv_ref, inv)]
    last = [moves.make(mixed_ref, mixed), moves.make(saved_o[4], slope)]
    grads = slope.at[:, :3 * D]

    def backward(v, carry):
        total_stage(jnp.where(v == 0, ends[-2], LEN), cot, unit2, inv2, par, cot, att, small)
        weight_stage(att, act, sums, sums, DOWN, FF // 2)

        @pl.when(v == 0)
        def _():
            for copy in early:
                copy.start()

        @pl.when(v == 1)
        def _():
            wait(*late, *last)

        feed_back_stage(cot, att, unit1, inv1, slope, inv, wr, par, base, gm, small, slope, att)
        weight_stage(att, mixed, sums, sums, 0, HALF)
        weight_stage(norm, slope, sums, sums, HID, FF // 2)

        @pl.when(v == 0)
        def _():
            for copy in late:
                copy.start()
            wait(out)
            attend_back_stage(ends, True, *heads[:5], gm, work[0], p_o, work[3], work[4], x, cot, grads)
            last[0].start()
            input_stage(base, grads, wf, cot)
            project_grad_stage(low, grads, None, wf)
            last[1].start()
            wait(*early)

        return carry

    lax.fori_loop(0, 2, backward, 0)
    for a, b in ((base, base_o), (gm, gm_o), (small, small_o), (wf[0].at[:, :3 * HALF], pro_o[0]), (wf[1].at[:, :3 * HALF], pro_o[1])):
        moves.send(a, b)
    parts_out(moves, at_ref, 0, sums[0], keep_o)
    parts_out(moves, at_ref, 1, sums[1], send_o)
    moves.finish()


def middle(pieces, tag, at, embedded, mixed, inv, par, first, rest, cot):
    two = lambda *shape: ((shape, BF),) * 2
    small = ((32, D), F32)
    outs = (SAVED + (full(D, F32), (P_SHAPE, BF), full(D, F32), full(D), small) + two(D, 3 * HALF)
            + tuple((r.shape, BF) for r in rest))
    parts = len(rest) // 2
    scratch = like((full(D, F32),) * 3 + (((8, D), F32),) + two(D, FIRST) + two(D, REST) + (full(D),) * 3
                   + (small,) + SAVED + HEADS_OUT + two(D, REST)) + ATTEND_WORK
    got = call(functools.partial(middle_kernel, parts), outs, scratch, 40, 60_000_000_000,
               pieces, tag, at, embedded, mixed, inv, par, *first, *rest, cot)
    return got[7], got[9], got[10], got[11], got[12:14], got[14:]


def heads_back_kernel(pieces_ref, q_ref, k_ref, v_ref, mixed_ref, low_ref, gm_ref, p_ref, grads_o, *refs):
    heads, refs = refs[:6], refs[6:]
    p_slots, kt, dk, dv, grads, p_sem, sem = refs
    moves = Moves(sem)
    ends = piece_ends(pieces_ref)
    first = [moves.fetch(a, b) for a, b in zip((q_ref, k_ref, v_ref, mixed_ref, low_ref, gm_ref), heads)]
    attend_back_stage_wide(ends, False, *heads, kt, p_ref, p_slots, p_sem, dk, dv, grads, first)
    moves.send(grads, grads_o)
    moves.finish()


def heads_back(pieces, heads, gm, p):
    scratch = like((full(D),) * 6)
    scratch += [VMEM((2,) + P_SHAPE[1:], BF), VMEM((HEADS2, 128, LEN), BF), VMEM((LEN, D), F32), VMEM((LEN, D), F32),
                VMEM((LEN, 3 * D), BF), pltpu.SemaphoreType.DMA((2,))]
    return call(heads_back_kernel, (full(3 * D),), scratch, 16, 18_000_000_000, pieces, *heads, gm, p)[0]


def last_kernel(tag_ref, at_ref, grads_ref, emb_ref, par_ref, base_ref, fa_ref, fb_ref, old_a_ref, old_b_ref, small_ref,
                *refs):
    out_o, keep_o, send_o = refs[:3]
    grads, x, low, par, base, wf, old, small, pro, sem = (
        refs[3], refs[4], refs[5], refs[6], refs[7], refs[8:10], refs[10:12], refs[12], refs[13:15], refs[15])
    moves = Moves(sem)
    first = [moves.fetch(a, b) for a, b in ((par_ref, par), (emb_ref, x), (grads_ref, grads))]
    second = [moves.fetch(a, b) for a, b in ((old_a_ref, old[0]), (old_b_ref, old[1]))]
    third = [moves.fetch(a, b) for a, b in ((base_ref, base), (small_ref, small))]
    third += rows_in(moves, at_ref, 0, fa_ref, wf[0]) + rows_in(moves, at_ref, 1, fb_ref, wf[1])
    wait(*first[:2])
    add_row(x, par[pl.ds(4 + tag_ref[0], 1), :], low, False)
    wait(*first[2:], *second)
    project_grad_stage(low, grads, old, pro)
    wait(*third)
    input_stage(base, grads, wf, base)
    moves.send(base, out_o)
    column = jnp.sum(base[...], axis=0, keepdims=True)
    norms = jnp.sum(small[...].reshape(4, 8, D), axis=1)
    tags = lax.broadcasted_iota(jnp.int32, (PAIRS, D), 0) == tag_ref[0]
    table = jnp.where(tags, jnp.broadcast_to(column, (PAIRS, D)), 0.0)
    stats = jnp.concatenate([norms, table, jnp.zeros((120, D), F32)], axis=0).T.astype(BF)
    for half, target in enumerate((keep_o, send_o)):
        pro[half][:, 3 * HALF:] = stats
        rows_out(moves, at_ref, half, pro[half], target)
    moves.finish()


def last_back(tag, at, part, grads, embedded, par, base, first, old, small):
    two = lambda *shape: ((shape, BF),) * 2
    scratch = like((full(3 * D), full(D, F32), full(D), ((8, D), F32), full(D, F32)) + two(D, FIRST)
                   + two(D, 3 * HALF) + (((32, D), F32),) + two(D, FIRST))
    return call(last_kernel, (full(D, F32),) + two(*part(FIRST)), scratch, 16, 8_000_000_000,
                tag, at, grads, embedded, par, base, *first, *old, small)


GROUP = ("dp", "tensor")


def plan(dp):
    if dp == 16:
        return (8, 4, 1, 2), (8, 4, 2, 1)
    bits = [1 << i for i in range(dp.bit_length() - 1)]
    side = len(bits) // 3
    x, y, z = bits[:side], bits[side:2 * side], bits[2 * side:]
    return tuple(z[::-1] + x[::-1] + y[::-1]), tuple(z[::-1] + y[::-1] + x[::-1])


def flip(value, dp, masks):
    pairs = [(d * 2 + t, (d ^ masks[t]) * 2 + t) for d in range(dp) for t in range(2)]
    return lax.ppermute(value, GROUP, pairs)


def swap(value):
    return lax.ppermute(value, "tensor", [(0, 1), (1, 0)])


def doubled(held, dp, masks):
    return jnp.concatenate([held, flip(held, dp, masks)], axis=0)


def after(value, *others):
    return lax.optimization_barrier((value, *others))[0]


def places(dp, mine, tensor):
    rel = jnp.arange(dp, dtype=jnp.int32) ^ mine
    found = []
    for order in plan(dp):
        found.append(sum(((rel & mask) // mask) << i for i, mask in enumerate(order)))
    return jnp.stack([jnp.where(tensor == t, found[0], found[1]) for t in (0, 1)])


def reduced(held, dp, masks, kind=BF):
    half = held.shape[0] // 2
    return add(held[:half], flip(held[half:], dp, masks), kind)


def add(a, b, kind=BF):
    return (a.astype(F32) + b.astype(F32)).astype(kind)


def body(embedded, piece_lengths, pair_tags, pair_embedding, w_query, w_key, w_value, w_output, w_hidden,
         w_down, first_gain, first_shift, second_gain, second_shift, cotangent):
    dp = lax.axis_size("dp")
    mine, tensor = lax.axis_index("dp"), lax.axis_index("tensor")
    rows = D // dp
    blocked = rows % 16 == 0
    pieces = lax.dynamic_index_in_dim(piece_lengths, tensor, 0, keepdims=False)
    tag = lax.dynamic_index_in_dim(pair_tags, tensor, 0, keepdims=True)
    small = jnp.concatenate([jnp.stack([first_gain, first_shift, second_gain, second_shift]), pair_embedding], axis=0)
    small = tn(small, jnp.eye(8, 128, dtype=BF)).astype(BF)
    at = places(dp, mine, tensor)

    def arranged(held):
        both = held, swap(held)
        if blocked:
            return both
        return tuple(h[at[i]].reshape(D, -1) for i, h in enumerate(both))

    def part(width):
        return (dp, rows, width) if blocked else (D, width)

    def swapped(keep, send):
        if not blocked:
            keep, send = (v.reshape(dp, rows, -1)[jnp.zeros((dp,), jnp.int32).at[at[i]].set(jnp.arange(dp))]
                          for i, v in enumerate((keep, send)))
        return add(keep, swap(send))

    def summed(held, phases):
        for i, masks in enumerate(phases):
            held = reduced(held, dp, masks, F32 if i == len(phases) - 1 else BF)
        return held[0]

    phases = list(zip(*plan(dp)))
    split = len(phases) - 1
    first = jnp.concatenate([w_query, w_key, w_value, small], axis=1)[None]
    rest = jnp.concatenate([w_output.T, w_hidden, w_down.T], axis=1)[None]
    for i, masks in enumerate(phases):
        first = doubled(first, dp, masks)
        if i < split - 1:
            rest = doubled(after(rest, first, *((tag, pieces, at) if i == 0 else ())), dp, masks)
        elif i == split - 1:
            rest = after(rest, first)
            arrived = flip(rest, dp, masks)
    first = arranged(after(first, rest))
    heads, par, bound = open_visit(pieces, tag, at, embedded, *first)
    rest = jnp.concatenate([after(rest, *heads), arrived], axis=0)
    rest, heads = lax.optimization_barrier((rest, heads))
    arrived, swapped_rest = flip(rest, dp, phases[-1]), swap(rest)
    q, k, v, vt = heads
    (mixed, low, inv), probs = attend_visit(pieces, bound, q, k, v, vt)
    arrived = after(arrived, mixed)
    if blocked:
        rest = (rest, arrived, swapped_rest, swap(arrived))
    else:
        rest = arranged(jnp.concatenate([rest, arrived], axis=0))
    result, base, gm, stats, old, sums = middle(pieces, tag, at, embedded, mixed, inv, par, first, rest, cotangent)
    if blocked:
        keep, keep_out, send, send_out = sums
        out = add(keep_out, swap(send_out))
        gm = after(gm, out)
        out = flip(out, dp, phases[-1])
        sums = add(add(keep, swap(send), F32), out)
    else:
        sums = reduced(swapped(*sums), dp, phases[-1])
    grads = heads_back(pieces, (q, k, v, mixed, low), gm, probs)
    sums, grads = lax.optimization_barrier((sums, grads))
    half = sums.shape[0] // 2
    out = flip(sums[half:], dp, phases[-2])
    grad, *da = last_back(tag, at, part, grads, embedded, par, base, first, old, stats)
    *da, out = lax.optimization_barrier((*da, out))
    sums = add(sums[:half], out)
    da = swapped(*da)
    sums = summed(sums, phases[-3::-1])
    da = summed(da, phases[::-1])
    small = da[:, 3 * HALF:3 * HALF + 8].T
    return (result, grad, small[4:], da[:, :HALF], da[:, HALF:2 * HALF], da[:, 2 * HALF:3 * HALF],
            sums[:, :HALF].T, sums[:, HID:DOWN], sums[:, DOWN:].T, small[0], small[1], small[2], small[3])


def solution(mesh):
    both = P(GROUP, None)
    params = (P("dp", "tensor"),) * 3 + (P("tensor", "dp"), P("dp", "tensor"), P("tensor", "dp"))
    in_specs = (both, P("dp", None), P("dp"), P(None, "dp")) + params + (P("dp"),) * 4 + (both,)
    out_specs = (both, both, P(None, "dp")) + params + (P("dp"),) * 4
    return jax.shard_map(body, mesh=mesh, in_specs=in_specs, out_specs=out_specs, check_vma=False)
```

```python
import functools
import math

import jax
import jax.numpy as jnp
from jax import lax
from jax.sharding import PartitionSpec as P
from jax.experimental import pallas as pl
from jax.experimental.pallas import tpu as pltpu

HEAD_DIM = 64
LEN = 1024
PIECES = 8
PAIRS = 4
D = 512
FF = 2048
HALF = 256
HEADS2 = 4
QB = 256
KB = 128
NQ = LEN // QB
NK = LEN // KB
BIG = 1e30
LOG2E = math.log2(math.e)
QSCALE = LOG2E / math.sqrt(HEAD_DIM)
KSCALE = math.log(2.0)
WIDTHS = (3, 5, 8)
EPS = 1e-5
C1 = math.sqrt(2.0 / math.pi)
C2 = C1 * 0.044715
F32 = jnp.float32
BF = jnp.bfloat16
VMEM_LIMIT = 60 * 1024 * 1024
TM = 512


def nn(a, b):
    return jnp.dot(a, b, preferred_element_type=F32)


def nt(a, b):
    return lax.dot_general(a, b, (((1,), (1,)), ((), ())), preferred_element_type=F32)


def tn(a, b):
    return lax.dot_general(a, b, (((0,), (0,)), ((), ())), preferred_element_type=F32)


def piece_ends(pieces_ref):
    ends, at = [], 0
    for j in range(PIECES):
        at = at + pieces_ref[j]
        ends.append(at)
    return ends


def window(block, ends):
    first = block * QB
    last = first + QB - 1
    low, high = jnp.int32(0), jnp.int32(LEN)
    for end in ends[:-1]:
        low = jnp.maximum(low, jnp.where(end <= first, end, 0))
        high = jnp.minimum(high, jnp.where(end > last, end, LEN))
    low = jnp.where(first >= ends[-2], first, low)
    high = jnp.where(last >= ends[-2], last + 1, high)
    return low // KB, (high + KB - 1) // KB


def over_widths(block, ends, run):
    low, high = window(block, ends)
    count = high - low
    previous = 0
    for wide in WIDTHS:
        begin = jnp.minimum(low, NK - wide)

        @pl.when((count > previous) & (count <= wide))
        def _(wide=wide, begin=begin):
            run(wide, pl.multiple_of(begin * KB, KB))

        previous = wide


def segment_codes(ends, segq_ref, segk_ref):
    rows = lax.broadcasted_iota(jnp.int32, (LEN, 128), 0)
    lanes = lax.broadcasted_iota(jnp.int32, (LEN, 128), 1)
    ids = jnp.zeros((LEN, 128), jnp.int32)
    for end in ends[:-1]:
        ids = ids + jnp.where(rows >= end, 1, 0)
    same = lanes == ids
    segk_ref[...] = jnp.where(same, 1.0, 0.0).astype(BF)
    free = (lanes >= PIECES) | (same & (lanes < PIECES - 1))
    segq_ref[...] = jnp.where(free, 0.0, -BIG).astype(BF)


def lane_half(shape):
    return lax.broadcasted_iota(jnp.int32, shape, 1) < HEAD_DIM


def two_heads(block):
    left = lane_half(block.shape)
    zero = jnp.zeros_like(block)
    return jnp.where(left, block, zero), jnp.where(left, zero, block)


def block_rows(index, size):
    return pl.ds(pl.multiple_of(index * size, size), size)


def head_norms(values, half):
    heads = lax.broadcasted_iota(jnp.int32, (HALF, 128), 0) // HEAD_DIM + half * (HALF // HEAD_DIM)
    pick = jnp.where(heads == lax.broadcasted_iota(jnp.int32, (HALF, 128), 1), 1.0, 0.0).astype(BF)
    return jnp.max(nn((values * values).astype(BF), pick), axis=0, keepdims=True)


def project_stage(x_ref, w_refs, q_ref, k_ref, v_ref, vt_ref):
    def chunk(i, carry):
        rows = block_rows(i, TM)
        low = x_ref[rows, :]
        q_top, k_top = carry
        for half in range(2):
            cols = slice(half * HALF, (half + 1) * HALF)
            queries = nn(low, w_refs[half][:, :HALF]) * QSCALE
            keys = nn(low, w_refs[half][:, HALF:2 * HALF])
            q_ref[rows, cols] = queries.astype(BF)
            k_ref[rows, cols] = keys.astype(BF)
            q_top = jnp.maximum(q_top, head_norms(queries, half))
            k_top = jnp.maximum(k_top, head_norms(keys, half))
            values = nn(low, w_refs[half][:, 2 * HALF:3 * HALF])
            v_ref[rows, cols] = values.astype(BF)
            for pair in range(2):
                vt_ref[half * 2 + pair, :128, rows] = values[:, pair * 128:(pair + 1) * 128].T.astype(BF)
        return q_top, k_top

    zero = jnp.zeros((1, 128), F32)
    q_top, k_top = lax.fori_loop(0, LEN // TM, chunk, (zero, zero))
    for pair in range(HEADS2):
        vt_ref[pair, 128:, :] = jnp.ones((16, LEN), BF)
    return jnp.max(q_top * k_top)


def pair_columns(pair):
    return pl.ds(pl.multiple_of(pair * 128, 128), 128)


def probs_copy(p_slots, p_hbm, sem, i, wide, out):
    slot = i % 2
    here = p_slots.at[slot, :, pl.ds(0, wide * KB), :]
    there = p_hbm.at[i, :, pl.ds(0, wide * KB), :]
    return pltpu.make_async_copy(here, there, sem.at[slot]) if out else pltpu.make_async_copy(there, here, sem.at[slot])


def attend_stage(ends, shifted, resident, q_ref, k_ref, v_ref, mixed_ref, low_ref, inv_ref, vt_ref, segq_ref, segk_ref,
                 p_slots, p_out, p_sem, done):
    def block(i, carry):
        rows = block_rows(i, QB)
        p_ref = p_slots.at[i % 2]

        @pl.when(i >= 2)
        def _():
            over_widths(i - 2, ends, lambda wide, begin: probs_copy(p_slots, p_out, p_sem, i - 2, wide, True).wait())

        pad = lax.broadcasted_iota(jnp.int32, (QB, 128), 0) + i * QB >= ends[-2]

        def run(wide, begin):
            keys = pl.ds(begin, wide * KB)
            segq = segq_ref[rows, :]

            def query(cols):
                even, odd = two_heads(q_ref[rows, cols])
                return jnp.concatenate(
                    [jnp.concatenate([even, segq], axis=1), jnp.concatenate([odd, segq], axis=1)], axis=0)

            def score(query, cols, keys):
                return nt(jnp.concatenate([k_ref[keys, cols], segk_ref[keys, :]], axis=1), query)

            def finish(pair, cols, out):
                inv = 1.0 / jnp.maximum(out[128:129, :], 1e-30)
                inv_ref[pl.ds(i * HEADS2 + pair, 1), :] = inv
                inv_both = jnp.concatenate(
                    [jnp.broadcast_to(inv[:, :QB], (64, QB)), jnp.broadcast_to(inv[:, QB:], (64, QB))], axis=0)
                exact = (jnp.concatenate([out[:64, :QB], out[64:128, QB:]], axis=0) * inv_both).T
                mixed = jnp.where(pad, v_ref[rows, cols].astype(F32), exact).astype(BF)
                mixed_ref[rows, cols] = mixed
                low_ref[rows, cols] = (exact - mixed.astype(F32)).astype(BF)

            def shifted_pair(pair, carry):
                cols = pair_columns(pair)
                asked = query(cols)

                def part(c):
                    return score(asked, cols, pl.ds(pl.multiple_of(begin + c * KB, KB), KB))

                top = lax.fori_loop(0, wide, lambda c, top: jnp.maximum(top, jnp.max(part(c), axis=0, keepdims=True)),
                                    jnp.full((1, 2 * QB), -2 * BIG, F32))

                def add_part(c, out):
                    at = pl.multiple_of(c * KB, KB)
                    probs = jnp.exp2(part(c) - top).astype(BF)
                    p_ref[pair, pl.ds(at, KB), :] = probs
                    return out + nn(vt_ref[pair, :, pl.ds(pl.multiple_of(begin + at, KB), KB)], probs)

                finish(pair, cols, lax.fori_loop(0, wide, add_part, jnp.zeros((144, 2 * QB), F32)))
                return carry

            def group(g, carry):
                pairs = [2 * g + r for r in range(2)]
                cols = [pair_columns(pair) for pair in pairs]
                scores = [score(query(c), c, keys) for c in cols]
                outs = []
                for pair, value in zip(pairs, scores):
                    probs = jnp.exp2(value).astype(BF)
                    p_ref[pair, :wide * KB, :] = probs
                    outs.append(nn(vt_ref[pair, :, keys], probs))
                for args in zip(pairs, cols, outs):
                    finish(*args)
                return carry

            if shifted:
                lax.fori_loop(0, HEADS2, shifted_pair, 0)
            else:
                lax.fori_loop(0, HEADS2 // 2, group, 0)
            out = probs_copy(p_slots, p_out, p_sem, i, wide, True)
            if resident:
                pl.when(i < NQ - 2)(out.start)
            else:
                out.start()

        over_widths(i, ends, run)
        done(i, rows)
        return carry

    lax.fori_loop(0, NQ, block, 0)
    if not resident:
        for i in range(NQ - 2, NQ):
            over_widths(i, ends, lambda wide, begin, i=i: probs_copy(p_slots, p_out, p_sem, i, wide, True).wait())


def grad_columns(part, pair):
    at = pair // 2 * 3 * HALF + part * HALF + pair % 2 * 128
    return slice(at, at + 128)


def attend_back_stage(ends, resident, q_ref, k_ref, v_ref, mixed_ref, low_ref, grad_ref, kt_ref, p_in, p_slots, p_sem,
                      dk_ref, dv_ref, grads_ref, first=(), later=()):
    if not resident:
        for i in (NQ - 1, NQ - 2):
            over_widths(i, ends, lambda wide, begin, i=i: probs_copy(p_slots, p_in, p_sem, i, wide, False).start())
    dk_ref[...] = jnp.zeros_like(dk_ref)
    dv_ref[...] = jnp.zeros_like(dv_ref)
    wait(*first)
    for pair in range(HEADS2):
        kt_ref[pair, :128, :] = k_ref[:, pair * 128:(pair + 1) * 128].astype(F32).T.astype(BF)
    span = [slice(pair * 128, (pair + 1) * 128) for pair in range(HEADS2)]

    def block(j, carry):
        i = NQ - 1 - j
        rows = block_rows(i, QB)
        p_ref = p_slots.at[i % 2]

        def run(wide, begin):
            keys = pl.ds(begin, wide * KB)
            arrived = probs_copy(p_slots, p_in, p_sem, i, wide, False)
            if resident:
                pl.when(j >= 2)(arrived.wait)
            else:
                arrived.wait()

            def outer(cols):
                return jnp.concatenate(two_heads(grad_ref[rows, cols]), axis=0)

            def slope(cols):
                grad = grad_ref[rows, cols]
                exact = mixed_ref[rows, cols].astype(F32) + low_ref[rows, cols].astype(F32)
                inner = grad.astype(F32) * exact
                high = inner.astype(BF)
                rest = pltpu.roll(inner - high.astype(F32), HEAD_DIM, 1).astype(BF)
                left = lane_half(inner.shape)
                inner = jnp.concatenate([jnp.where(left, high, rest), jnp.where(left, rest, high)], axis=0)
                both = jnp.concatenate([outer(cols), inner], axis=1)
                value = jnp.concatenate([v_ref[keys, cols], jnp.full((wide * KB, 128), -1.0, BF)], axis=1)
                return nt(value, both)

            def rest(pair, cols, target, scores):
                query = jnp.concatenate(two_heads(q_ref[rows, cols]), axis=0)
                dk_ref[keys, cols] += nn(scores, query)
                out = nn(kt_ref[pair, :128, keys], scores)
                out = jnp.concatenate([out[:64, :QB], out[64:, QB:]], axis=0)
                grads_ref[rows, target] = (out.T * (HEAD_DIM ** -0.5)).astype(BF)

            def group(g, carry):
                pairs = [2 * g + r for r in range(2)]
                cols = [pair_columns(pair) for pair in pairs]
                slopes = [slope(c) for c in cols]
                scores = []
                for pair, c, value in zip(pairs, cols, slopes):
                    probs = p_ref[pair, :wide * KB, :]
                    scores.append((probs.astype(F32) * value).astype(BF))
                    dv_ref[keys, c] += nn(probs, outer(c))
                for r in range(2):
                    target = pl.ds(pl.multiple_of(g * 3 * HALF + r * 128, 128), 128)
                    rest(pairs[r], cols[r], target, scores[r])
                return carry

            lax.fori_loop(0, HEADS2 // 2, group, 0)

        over_widths(i, ends, run)

        if later:
            @pl.when(j == 0)
            def _():
                for copy in later:
                    copy.start()

        @pl.when(j < NQ - 2)
        def _():
            over_widths(i - 2, ends, lambda wide, begin: probs_copy(p_slots, p_in, p_sem, i - 2, wide, False).start())

        return carry

    lax.fori_loop(0, NQ, block, 0)
    for pair in range(HEADS2):
        grads_ref[:, grad_columns(1, pair)] = (dk_ref[:, span[pair]] * KSCALE).astype(BF)
        grads_ref[:, grad_columns(2, pair)] = dv_ref[:, span[pair]].astype(BF)


def attend_stage_wide(ends, shifted, resident, q_ref, k_ref, v_ref, mixed_ref, low_ref, inv_ref, vt_ref, segq_ref, segk_ref,
                 p_slots, p_out, p_sem, done):
    def block(i, carry):
        rows = block_rows(i, QB)
        p_ref = p_slots.at[i % 2]

        @pl.when(i >= 2)
        def _():
            over_widths(i - 2, ends, lambda wide, begin: probs_copy(p_slots, p_out, p_sem, i - 2, wide, True).wait())

        def run(wide, begin):
            keys = pl.ds(begin, wide * KB)
            segq = segq_ref[rows, :]
            segk = segk_ref[keys, :]
            pad = lax.broadcasted_iota(jnp.int32, (QB, 128), 0) + i * QB >= ends[-2]
            span = [slice(pair * 128, (pair + 1) * 128) for pair in range(HEADS2)]

            def score(pair):
                even, odd = two_heads(q_ref[rows, span[pair]])
                query = jnp.concatenate(
                    [jnp.concatenate([even, segq], axis=1), jnp.concatenate([odd, segq], axis=1)], axis=0)
                key = jnp.concatenate([k_ref[keys, span[pair]], segk], axis=1)
                return nt(key, query)

            def soften(pair, scores):
                probs = jnp.exp2(scores).astype(BF)
                p_ref[pair, :wide * KB, :] = probs
                return probs

            def mix(pair, probs):
                return nn(vt_ref[pair, :, keys], probs)

            def finish(pair, out):
                cols = span[pair]
                inv = 1.0 / jnp.maximum(out[128:129, :], 1e-30)
                inv_ref[pl.ds(i * HEADS2 + pair, 1), :] = inv
                inv_both = jnp.concatenate(
                    [jnp.broadcast_to(inv[:, :QB], (64, QB)), jnp.broadcast_to(inv[:, QB:], (64, QB))], axis=0)
                exact = (jnp.concatenate([out[:64, :QB], out[64:128, QB:]], axis=0) * inv_both).T
                mixed = jnp.where(pad, v_ref[rows, cols].astype(F32), exact).astype(BF)
                mixed_ref[rows, cols] = mixed
                low_ref[rows, cols] = (exact - mixed.astype(F32)).astype(BF)

            s = {0: score(0), 1: score(1)}
            p, o = {}, {}
            for pair in range(HEADS2):
                p[pair] = soften(pair, s[pair])
                if pair + 2 < HEADS2:
                    s[pair + 2] = score(pair + 2)
                if pair:
                    o[pair - 1] = mix(pair - 1, p[pair - 1])
                if pair > 1:
                    finish(pair - 2, o[pair - 2])
            out = probs_copy(p_slots, p_out, p_sem, i, wide, True)
            if resident:
                pl.when(i < NQ - 2)(out.start)
            else:
                out.start()
            o[HEADS2 - 1] = mix(HEADS2 - 1, p[HEADS2 - 1])
            finish(HEADS2 - 2, o[HEADS2 - 2])
            finish(HEADS2 - 1, o[HEADS2 - 1])

        over_widths(i, ends, run)
        done(i, rows)
        return carry

    lax.fori_loop(0, NQ, block, 0)
    if not resident:
        for i in range(NQ - 2, NQ):
            over_widths(i, ends, lambda wide, begin, i=i: probs_copy(p_slots, p_out, p_sem, i, wide, True).wait())


def attend_back_stage_wide(ends, resident, q_ref, k_ref, v_ref, mixed_ref, low_ref, grad_ref, kt_ref, p_in, p_slots, p_sem,
                      dk_ref, dv_ref, grads_ref, first=(), later=()):
    if not resident:
        for i in (NQ - 1, NQ - 2):
            over_widths(i, ends, lambda wide, begin, i=i: probs_copy(p_slots, p_in, p_sem, i, wide, False).start())
    dk_ref[...] = jnp.zeros_like(dk_ref)
    dv_ref[...] = jnp.zeros_like(dv_ref)
    wait(*first)
    for pair in range(HEADS2):
        kt_ref[pair, :128, :] = k_ref[:, pair * 128:(pair + 1) * 128].astype(F32).T.astype(BF)
    span = [slice(pair * 128, (pair + 1) * 128) for pair in range(HEADS2)]

    def block(j, carry):
        i = NQ - 1 - j
        rows = block_rows(i, QB)
        p_ref = p_slots.at[i % 2]

        def run(wide, begin):
            keys = pl.ds(begin, wide * KB)
            arrived = probs_copy(p_slots, p_in, p_sem, i, wide, False)
            if resident:
                pl.when(j >= 2)(arrived.wait)
            else:
                arrived.wait()

            def outer(pair):
                return jnp.concatenate(two_heads(grad_ref[rows, span[pair]]), axis=0)

            def slope(pair):
                grad = grad_ref[rows, span[pair]]
                exact = mixed_ref[rows, span[pair]].astype(F32) + low_ref[rows, span[pair]].astype(F32)
                inner = grad.astype(F32) * exact
                high = inner.astype(BF)
                rest = pltpu.roll(inner - high.astype(F32), HEAD_DIM, 1).astype(BF)
                left = lane_half(inner.shape)
                inner = jnp.concatenate([jnp.where(left, high, rest), jnp.where(left, rest, high)], axis=0)
                both = jnp.concatenate([outer(pair), inner], axis=1)
                value = jnp.concatenate([v_ref[keys, span[pair]], jnp.full((wide * KB, 128), -1.0, BF)], axis=1)
                return nt(value, both)

            def bend(pair, slope):
                return (p_ref[pair, :wide * KB, :].astype(F32) * slope).astype(BF)

            def values(pair):
                dv_ref[keys, span[pair]] += nn(p_ref[pair, :wide * KB, :], outer(pair))

            def rest(pair, scores):
                query = jnp.concatenate(two_heads(q_ref[rows, span[pair]]), axis=0)
                dk_ref[keys, span[pair]] += nn(scores, query)
                out = nn(kt_ref[pair, :128, keys], scores)
                out = jnp.concatenate([out[:64, :QB], out[64:, QB:]], axis=0)
                grads_ref[rows, grad_columns(0, pair)] = (out.T * (HEAD_DIM ** -0.5)).astype(BF)

            s = {0: slope(0), 1: slope(1)}
            d = {}
            for pair in range(HEADS2):
                d[pair] = bend(pair, s[pair])
                values(pair)
                if pair + 2 < HEADS2:
                    s[pair + 2] = slope(pair + 2)
                if pair:
                    rest(pair - 1, d[pair - 1])
            rest(HEADS2 - 1, d[HEADS2 - 1])

        over_widths(i, ends, run)

        if later:
            @pl.when(j == 0)
            def _():
                for copy in later:
                    copy.start()

        @pl.when(j < NQ - 2)
        def _():
            over_widths(i - 2, ends, lambda wide, begin: probs_copy(p_slots, p_in, p_sem, i - 2, wide, False).start())

        return carry

    lax.fori_loop(0, NQ, block, 0)
    for pair in range(HEADS2):
        grads_ref[:, grad_columns(1, pair)] = (dk_ref[:, span[pair]] * KSCALE).astype(BF)
        grads_ref[:, grad_columns(2, pair)] = dv_ref[:, span[pair]].astype(BF)


def unit_rows(values):
    center = values - jnp.mean(values, axis=-1, keepdims=True)
    spread = jnp.mean(center * center, axis=-1, keepdims=True)
    inv = lax.rsqrt(spread + EPS)
    return center * inv, inv


HID = HALF
DOWN = HALF + FF // 2
REST = HALF + FF
FIRST = 3 * HALF + 128
STEP = 512
PER_HALF = FF // 2 // STEP


def feed_stage(x_ref, mixed_ref, w_refs, par_ref, out_ref, unit1_ref, inv1_ref, norm_ref, act_ref, slope_ref,
               unit2_ref, inv2_ref, tm=512):
    def chunk(i, carry):
        rows = block_rows(i, tm)
        summed = x_ref[rows, :]
        for half in range(2):
            summed = summed + nt(mixed_ref[rows, half * HALF:(half + 1) * HALF], w_refs[half][:, :HALF])
        unit, inv = unit_rows(summed)
        unit1_ref[rows, :] = unit.astype(BF)
        inv1_ref[rows, :] = inv
        normed = unit * par_ref[0:1, :] + par_ref[1:2, :]
        low = normed.astype(BF)
        norm_ref[rows, :] = low
        for part in range(2 * PER_HALF):
            cols = slice(part * STEP, (part + 1) * STEP)
            at = HID + part % PER_HALF * STEP
            hidden = nn(low, w_refs[part // PER_HALF][:, at:at + STEP])
            square = hidden * hidden
            gate = 0.5 + 0.5 * jnp.tanh(hidden * (C1 + C2 * square))
            act_ref[rows, cols] = (hidden * gate).astype(BF)
            slope_ref[rows, cols] = (gate + gate * (1.0 - gate) * hidden * (2 * C1 + 6 * C2 * square)).astype(BF)
        total = normed
        for half in range(2):
            total = total + nt(act_ref[rows, half * (FF // 2):(half + 1) * (FF // 2)], w_refs[half][:, DOWN:])
        unit, inv = unit_rows(total)
        unit2_ref[rows, :] = unit.astype(BF)
        inv2_ref[rows, :] = inv
        out_ref[rows, :] = unit * par_ref[2:3, :] + par_ref[3:4, :]
        return carry

    lax.fori_loop(0, LEN // tm, chunk, 0)


def unit_back(grad, unit, inv, gain):
    scaled = grad * gain
    first = jnp.mean(scaled, axis=-1, keepdims=True)
    second = jnp.mean(scaled * unit, axis=-1, keepdims=True)
    return inv * (scaled - first - unit * second)


def fold_rows(values):
    return jnp.sum(values.reshape(-1, 8, values.shape[-1]), axis=0)


def total_stage(limit, grad_ref, unit2_ref, inv2_ref, par_ref, total_ref, low_ref, small_ref, tm=1024):
    def chunk(i, carry):
        rows = block_rows(i, tm)
        grad = grad_ref[rows, :]
        grad = jnp.where(lax.broadcasted_iota(jnp.int32, grad.shape, 0) + i * tm < limit, grad, 0.0)
        unit2 = unit2_ref[rows, :].astype(F32)
        small_ref[16:24, :] += fold_rows(grad * unit2)
        small_ref[24:32, :] += fold_rows(grad)
        total = unit_back(grad, unit2, inv2_ref[rows, :], par_ref[2:3, :])
        total_ref[rows, :] = total
        low_ref[rows, :] = total.astype(BF)
        return carry

    lax.fori_loop(0, LEN // tm, chunk, 0)


def feed_back_stage(total_ref, low_ref, unit1_ref, inv1_ref, slope_ref, inv_ref, w_refs, par_ref,
                    base_ref, gm_ref, small_ref, hid_ref, att_ref, tm=512):
    def chunk(i, carry):
        rows = block_rows(i, tm)
        low = low_ref[rows, :]
        for part in range(2 * PER_HALF):
            cols = slice(part * STEP, (part + 1) * STEP)
            at = DOWN + part % PER_HALF * STEP
            slope = nn(low, w_refs[part // PER_HALF][:, at:at + STEP])
            hid_ref[rows, cols] = (slope * slope_ref[rows, cols].astype(F32)).astype(BF)
        normed = total_ref[rows, :]
        for half in range(2):
            normed = normed + nt(hid_ref[rows, half * (FF // 2):(half + 1) * (FF // 2)], w_refs[half][:, HID:DOWN])
        unit1 = unit1_ref[rows, :].astype(F32)
        small_ref[0:8, :] += fold_rows(normed * unit1)
        small_ref[8:16, :] += fold_rows(normed)
        summed = unit_back(normed, unit1, inv1_ref[rows, :], par_ref[0:1, :])
        base_ref[rows, :] = summed
        low = summed.astype(BF)
        att_ref[rows, :] = low
        for half in range(2):
            grad = nn(low, w_refs[half][:, :HALF])
            for pair in range(2):
                for part in range(tm // QB):
                    inv = inv_ref[pl.ds((i * (tm // QB) + part) * HEADS2 + half * 2 + pair, 1), :]
                    inv = jnp.concatenate([jnp.broadcast_to(inv[:, :QB], (64, QB)),
                                           jnp.broadcast_to(inv[:, QB:], (64, QB))], axis=0).T
                    value = grad[part * QB:(part + 1) * QB, pair * 128:(pair + 1) * 128] * inv
                    gm_ref[pl.ds(pl.multiple_of(i * tm + part * QB, QB), QB),
                           half * HALF + pair * 128:half * HALF + (pair + 1) * 128] = value.astype(BF)
        return carry

    lax.fori_loop(0, LEN // tm, chunk, 0)


def weight_stage(left_ref, right_ref, olds, outs, offset, width):
    cols = slice(offset, offset + width)
    for half in range(2):
        value = tn(left_ref[...], right_ref[:, half * width:(half + 1) * width])
        if olds is not None:
            value = value + olds[half][:, cols].astype(F32)
        outs[half][:, cols] = value.astype(BF)


def project_grad_stage(low_ref, grads_ref, olds, outs):
    for half in range(2):
        value = tn(low_ref[...], grads_ref[:, half * 3 * HALF:(half + 1) * 3 * HALF])
        if olds is not None:
            value = value + olds[half][...].astype(F32)
        outs[half][:, :3 * HALF] = value.astype(BF)


def input_stage(base_ref, grads_ref, w_refs, out_ref, size=LEN):
    def chunk(i, carry):
        rows = block_rows(i, TM)
        value = base_ref[rows, :]
        for half in range(2):
            value = value + nt(grads_ref[rows, half * 3 * HALF:(half + 1) * 3 * HALF], w_refs[half][:, :3 * HALF])
        out_ref[rows, :] = value
        return carry

    lax.fori_loop(0, size // TM, chunk, 0)


def add_row(x_ref, row, low_ref, keep):
    def chunk(i, carry):
        rows = block_rows(i, TM)
        value = x_ref[rows, :] + row
        if keep:
            x_ref[rows, :] = value
        if low_ref is not None:
            low_ref[rows, :] = value.astype(BF)
        return carry

    lax.fori_loop(0, LEN // TM, chunk, 0)


LIMIT = 64.0 ** 2
P_SHAPE = (NQ, HEADS2, LEN, 2 * QB)
VMEM = pltpu.VMEM


class Moves:
    def __init__(self, sem):
        self.sem, self.count, self.open = sem, 0, []

    def make(self, source, target):
        copy = pltpu.make_async_copy(source, target, self.sem.at[self.count])
        self.count += 1
        return copy

    def fetch(self, source, target):
        copy = self.make(source, target)
        copy.start()
        return copy

    def send(self, source, target):
        copy = self.fetch(source, target)
        self.open.append(copy)
        return copy

    def finish(self):
        wait(*self.open)
        self.open = []


def wait(*copies):
    for copy in copies:
        copy.wait()


class Group:
    def __init__(self, moves, copies, whole):
        self.copies, self.whole = copies, pltpu.make_async_copy(whole, whole, moves.sem.at[moves.count])
        moves.count += 1

    def start(self):
        for copy in self.copies:
            copy()

    def wait(self):
        self.whole.wait()


def pick(index, count, make):
    def start():
        pl.when(index < count)(lambda: make(0, jnp.minimum(index, count - 1)).start())
        pl.when(index >= count)(lambda: make(1, jnp.maximum(index - count, 0)).start())

    return start


def parts_in(moves, at_ref, half, sources, target):
    if len(sources) == 1:
        return rows_in(moves, at_ref, half, sources[0], target)
    count, rows, _ = sources[0].shape
    sem = moves.sem.at[moves.count]
    copies = [pick(at_ref[half, b], count, lambda ref, place, b=b: pltpu.make_async_copy(
        sources[ref].at[place], target.at[pl.ds(b * rows, rows), :], sem)) for b in range(2 * count)]
    group = Group(moves, copies, target)
    group.start()
    return [group]


def parts_out(moves, at_ref, half, source, targets):
    if len(targets) == 1:
        return rows_out(moves, at_ref, half, source, targets[0])
    count, rows, _ = targets[0].shape
    sem = moves.sem.at[moves.count]
    copies = [pick(at_ref[half, b], count, lambda ref, place, b=b: pltpu.make_async_copy(
        source.at[pl.ds(b * rows, rows), :], targets[ref].at[place], sem)) for b in range(2 * count)]
    group = Group(moves, copies, source)
    group.start()
    moves.open.append(group)


def rows_in(moves, at_ref, half, source, target):
    if len(source.shape) == 2:
        return [moves.fetch(source, target)]
    dp, rows, _ = source.shape
    sem = moves.sem.at[moves.count]
    group = Group(moves, [pltpu.make_async_copy(source.at[at_ref[half, b]], target.at[pl.ds(b * rows, rows), :], sem).start
                          for b in range(dp)], target)
    group.start()
    return [group]


def rows_out(moves, at_ref, half, source, target):
    if len(target.shape) == 2:
        moves.send(source, target)
        return
    dp, rows, _ = target.shape
    sem = moves.sem.at[moves.count]
    group = Group(moves, [pltpu.make_async_copy(source.at[pl.ds(b * rows, rows), :], target.at[at_ref[half, b]], sem).start
                          for b in range(dp)], source)
    group.start()
    moves.open.append(group)


ANY = pl.BlockSpec(memory_space=pl.ANY)
SMEM = pl.BlockSpec(memory_space=pltpu.SMEM)


def like(shapes):
    return [VMEM(s, t) for s, t in shapes]


def full(width, kind=BF):
    return ((LEN, width), kind)


def call(kernel, outs, scratch, sems, flops, *args):
    smem = sum(a.dtype == jnp.int32 for a in args)
    return pl.pallas_call(
        kernel,
        in_specs=[SMEM] * smem + [ANY] * (len(args) - smem),
        out_specs=[ANY] * len(outs),
        out_shape=[jax.ShapeDtypeStruct(s, t) for s, t in outs],
        scratch_shapes=scratch + [pltpu.SemaphoreType.DMA((sems,))],
        compiler_params=pltpu.CompilerParams(vmem_limit_bytes=VMEM_LIMIT),
        cost_estimate=pl.CostEstimate(flops=flops, bytes_accessed=8 << 20, transcendentals=0),
    )(*args)


HEADS_OUT = (full(D), full(D), full(D), full(D), full(D), ((NQ * HEADS2, 2 * QB), F32))
ATTEND_WORK = [VMEM((HEADS2, 144, LEN), BF), VMEM((LEN, 128), BF), VMEM((LEN, 128), BF),
               VMEM((2,) + P_SHAPE[1:], BF), pltpu.SemaphoreType.DMA((2,))]


def either(ends, bound, resident, heads, work, p_out, done):
    for shifted in (False, True):
        @pl.when((bound > LIMIT) if shifted else (bound <= LIMIT))
        def _(shifted=shifted):
            stage = attend_stage if shifted or resident else attend_stage_wide
            stage(ends, shifted, resident, *heads, *work[:4], p_out, work[4], done)


VT = ((HEADS2, 144, LEN), BF)


def open_kernel(pieces_ref, tag_ref, at_ref, emb_ref, own_ref, other_ref, *refs):
    outs, par_o, bound_o, refs = refs[:4], refs[4], refs[5], refs[6:]
    heads, par, x, low, wa, wb, sem = refs[:4], refs[4], refs[5], refs[6], refs[7], refs[8], refs[9]
    moves = Moves(sem)
    first = rows_in(moves, at_ref, 0, own_ref, wa)
    third = moves.fetch(emb_ref, x)
    second = rows_in(moves, at_ref, 1, other_ref, wb)
    wait(*first)
    par[...] = wa[:, 3 * HALF:].astype(F32).T[:8, :]
    moves.send(par, par_o)
    wait(third)
    add_row(x, par[pl.ds(4 + tag_ref[0], 1), :], low, False)
    wait(*second)
    bound_o[0] = project_stage(low, (wa, wb), *heads)
    for a, b in zip(heads, outs):
        moves.send(a, b)
    moves.finish()


def open_visit(pieces, tag, at, embedded, own, other):
    outs = (full(D), full(D), full(D), VT, ((8, D), F32))
    scratch = like(outs + (full(D, F32), full(D), ((D, FIRST), BF), ((D, FIRST), BF)))
    got = pl.pallas_call(
        open_kernel,
        in_specs=[SMEM] * 3 + [ANY] * 3,
        out_specs=[ANY] * 5 + [SMEM],
        out_shape=[jax.ShapeDtypeStruct(s, t) for s, t in outs + (((1,), F32),)],
        scratch_shapes=scratch + [pltpu.SemaphoreType.DMA((8,))],
        compiler_params=pltpu.CompilerParams(vmem_limit_bytes=VMEM_LIMIT),
        cost_estimate=pl.CostEstimate(flops=4_000_000_000, bytes_accessed=8 << 20, transcendentals=0),
    )(pieces, tag, at, embedded, own, other)
    return got[:4], got[4], got[5]


def attend_kernel(pieces_ref, bound_ref, q_ref, k_ref, v_ref, vt_ref, *refs):
    outs, p_o, refs = refs[:3], refs[3], refs[4:]
    heads, work, row_sem, sem = refs[:6], refs[6:11], refs[11], refs[12]
    moves = Moves(sem)
    ends = piece_ends(pieces_ref)
    first = [moves.fetch(a, b) for a, b in zip((q_ref, k_ref, vt_ref, v_ref), heads[:2] + work[:1] + heads[2:3])]
    segment_codes(ends, work[1], work[2])
    wait(*first)

    def sent(i, rows):
        return [pltpu.make_async_copy(heads[n].at[rows, :], outs[n - 3].at[rows, :], row_sem.at[n - 3, i])
                for n in (3, 4)]

    def done(i, rows):
        for copy in sent(i, rows):
            copy.start()

    either(ends, bound_ref[0], False, heads, work, p_o, done)
    moves.send(heads[5], outs[2])
    for i in range(NQ):
        wait(*sent(i, pl.ds(i * QB, QB)))
    moves.finish()


def attend_visit(pieces, bound, q, k, v, vt):
    outs = HEADS_OUT[3:] + ((P_SHAPE, BF),)
    scratch = like(HEADS_OUT) + ATTEND_WORK + [pltpu.SemaphoreType.DMA((2, NQ)), pltpu.SemaphoreType.DMA((8,))]
    got = pl.pallas_call(
        attend_kernel,
        in_specs=[SMEM] * 2 + [ANY] * 4,
        out_specs=[ANY] * 4,
        out_shape=[jax.ShapeDtypeStruct(s, t) for s, t in outs],
        scratch_shapes=scratch,
        compiler_params=pltpu.CompilerParams(vmem_limit_bytes=VMEM_LIMIT),
        cost_estimate=pl.CostEstimate(flops=8_000_000_000, bytes_accessed=8 << 20, transcendentals=0),
    )(pieces, bound, q, k, v, vt)
    return got[:3], got[3]


SAVED = (full(D), full(1, F32), full(D), full(FF), full(FF), full(D), full(1, F32))


def middle_kernel(parts, pieces_ref, tag_ref, at_ref, emb_ref, mixed_ref, inv_ref, par_ref, fa_ref, fb_ref, *refs):
    ra_ref, rb_ref, cot_ref, refs = refs[:parts], refs[parts:2 * parts], refs[2 * parts], refs[2 * parts + 1:]
    saved_o, refs = refs[:7], refs[7:]
    result_o, p_o, base_o, gm_o, small_o, pro_o = refs[:5] + (refs[5:7],)
    keep_o, send_o, refs = refs[7:7 + parts], refs[7 + parts:7 + 2 * parts], refs[7 + 2 * parts:]
    x, base, cot, par, wf, wr, low, att, gm, small = (
        refs[0], refs[1], refs[2], refs[3], refs[4:6], refs[6:8], refs[8], refs[9], refs[10], refs[11])
    saved, heads, sums = refs[12:19], refs[19:25], refs[25:27]
    work, sem = refs[27:32], refs[32]
    unit1, inv1, norm, act, slope, unit2, inv2 = saved
    mixed, inv = heads[3], heads[5]
    moves = Moves(sem)
    ends = piece_ends(pieces_ref)
    first = [moves.fetch(emb_ref, x), moves.fetch(mixed_ref, mixed), moves.fetch(par_ref, par)]
    second = parts_in(moves, at_ref, 0, ra_ref, wr[0]) + parts_in(moves, at_ref, 1, rb_ref, wr[1])
    segment_codes(ends, work[1], work[2])
    wait(*first)
    add_row(x, par[pl.ds(4 + tag_ref[0], 1), :], None, True)
    wait(*second)
    third = rows_in(moves, at_ref, 0, fa_ref, wf[0]) + rows_in(moves, at_ref, 1, fb_ref, wf[1])
    for ref in (small, *sums):
        ref[...] = jnp.zeros_like(ref)
    sent = [moves.make(a, b) for a, b in zip(saved, saved_o)]
    seed = moves.make(cot_ref, cot)

    def forward(v, carry):
        feed_stage(x, mixed, wr, par, x, *saved)

        @pl.when(v == 0)
        def _():
            for copy in sent:
                copy.start()
            add_row(x, 0.0, low, False)
            wait(*third)
            bound = project_stage(low, wf, heads[0], heads[1], heads[2], work[0])
            either(ends, bound, True, heads, work, p_o, lambda i, rows: None)
            seed.start()
            wait(*sent)

        return carry

    lax.fori_loop(0, 2, forward, 0)
    out = moves.fetch(x, result_o)
    wait(seed)
    early = [moves.make(saved_o[n], saved[n]) for n in (3, 5, 6)]
    late = [moves.make(saved_o[n], saved[n]) for n in (0, 1, 2)] + [moves.make(inv_ref, inv)]
    last = [moves.make(mixed_ref, mixed), moves.make(saved_o[4], slope)]
    grads = slope.at[:, :3 * D]
    ended = [moves.make(a, b) for a, b in ((base, base_o), (gm, gm_o), (small, small_o))]
    projected = [moves.make(wf[half].at[:, :3 * HALF], pro_o[half]) for half in range(2)]

    def backward(v, carry):
        total_stage(jnp.where(v == 0, ends[-2], LEN), cot, unit2, inv2, par, cot, att, small)
        weight_stage(att, act, sums, sums, DOWN, FF // 2)

        @pl.when(v == 0)
        def _():
            for copy in early:
                copy.start()

        @pl.when(v == 1)
        def _():
            wait(*late, *last)

        feed_back_stage(cot, att, unit1, inv1, slope, inv, wr, par, base, gm, small, slope, att)

        @pl.when(v == 1)
        def _():
            for copy in ended:
                copy.start()

        weight_stage(att, mixed, sums, sums, 0, HALF)
        weight_stage(norm, slope, sums, sums, HID, FF // 2)

        @pl.when(v == 0)
        def _():
            for copy in late:
                copy.start()
            wait(out)
            attend_back_stage(ends, True, *heads[:5], gm, work[0], p_o, work[3], work[4], x, cot, grads)
            last[0].start()
            input_stage(base, grads, wf, cot)
            project_grad_stage(low, grads, None, wf)
            for copy in projected:
                copy.start()
            last[1].start()
            wait(*early)

        return carry

    lax.fori_loop(0, 2, backward, 0)
    parts_out(moves, at_ref, 0, sums[0], keep_o)
    parts_out(moves, at_ref, 1, sums[1], send_o)
    wait(*ended, *projected)
    moves.finish()


def middle(pieces, tag, at, embedded, mixed, inv, par, first, rest, cot):
    two = lambda *shape: ((shape, BF),) * 2
    small = ((32, D), F32)
    outs = (SAVED + (full(D, F32), (P_SHAPE, BF), full(D, F32), full(D), small) + two(D, 3 * HALF)
            + tuple((r.shape, BF) for r in rest))
    parts = len(rest) // 2
    scratch = like((full(D, F32),) * 3 + (((8, D), F32),) + two(D, FIRST) + two(D, REST) + (full(D),) * 3
                   + (small,) + SAVED + HEADS_OUT + two(D, REST)) + ATTEND_WORK
    got = call(functools.partial(middle_kernel, parts), outs, scratch, 40, 60_000_000_000,
               pieces, tag, at, embedded, mixed, inv, par, *first, *rest, cot)
    return got[7], got[9], got[10], got[11], got[12:14], got[14:]


def heads_back_kernel(pieces_ref, q_ref, k_ref, v_ref, mixed_ref, low_ref, gm_ref, p_ref, grads_o, *refs):
    heads, refs = refs[:6], refs[6:]
    p_slots, kt, dk, dv, grads, p_sem, sem = refs
    moves = Moves(sem)
    ends = piece_ends(pieces_ref)
    first = [moves.fetch(a, b) for a, b in zip((q_ref, k_ref, v_ref, mixed_ref, low_ref, gm_ref), heads)]
    attend_back_stage_wide(ends, False, *heads, kt, p_ref, p_slots, p_sem, dk, dv, grads, first)
    moves.send(grads, grads_o)
    moves.finish()


def heads_back(pieces, heads, gm, p):
    scratch = like((full(D),) * 6)
    scratch += [VMEM((2,) + P_SHAPE[1:], BF), VMEM((HEADS2, 128, LEN), BF), VMEM((LEN, D), F32), VMEM((LEN, D), F32),
                VMEM((LEN, 3 * D), BF), pltpu.SemaphoreType.DMA((2,))]
    return call(heads_back_kernel, (full(3 * D),), scratch, 16, 18_000_000_000, pieces, *heads, gm, p)[0]


def last_kernel(tag_ref, at_ref, grads_ref, emb_ref, par_ref, base_ref, fa_ref, fb_ref, old_a_ref, old_b_ref, small_ref,
                *refs):
    out_o, keep_o, send_o = refs[:3]
    grads, x, low, par, base, wf, old, small, pro, sem = (
        refs[3], refs[4], refs[5], refs[6], refs[7], refs[8:10], refs[10:12], refs[12], refs[13:15], refs[15])
    moves = Moves(sem)
    first = [moves.fetch(a, b) for a, b in ((par_ref, par), (emb_ref, x), (grads_ref, grads))]
    second = [moves.fetch(a, b) for a, b in ((old_a_ref, old[0]), (old_b_ref, old[1]))]
    third = [moves.fetch(a, b) for a, b in ((base_ref, base), (small_ref, small))]
    third += rows_in(moves, at_ref, 0, fa_ref, wf[0]) + rows_in(moves, at_ref, 1, fb_ref, wf[1])
    wait(*first[:2])
    add_row(x, par[pl.ds(4 + tag_ref[0], 1), :], low, False)
    wait(*first[2:], *second)
    project_grad_stage(low, grads, old, pro)
    wait(*third)
    input_stage(base, grads, wf, base)
    moves.send(base, out_o)
    column = jnp.sum(base[...], axis=0, keepdims=True)
    norms = jnp.sum(small[...].reshape(4, 8, D), axis=1)
    tags = lax.broadcasted_iota(jnp.int32, (PAIRS, D), 0) == tag_ref[0]
    table = jnp.where(tags, jnp.broadcast_to(column, (PAIRS, D)), 0.0)
    stats = jnp.concatenate([norms, table, jnp.zeros((120, D), F32)], axis=0).T.astype(BF)
    for half, target in enumerate((keep_o, send_o)):
        pro[half][:, 3 * HALF:] = stats
        rows_out(moves, at_ref, half, pro[half], target)
    moves.finish()


def last_back(tag, at, part, grads, embedded, par, base, first, old, small):
    two = lambda *shape: ((shape, BF),) * 2
    scratch = like((full(3 * D), full(D, F32), full(D), ((8, D), F32), full(D, F32)) + two(D, FIRST)
                   + two(D, 3 * HALF) + (((32, D), F32),) + two(D, FIRST))
    return call(last_kernel, (full(D, F32),) + two(*part(FIRST)), scratch, 16, 8_000_000_000,
                tag, at, grads, embedded, par, base, *first, *old, small)


GROUP = ("dp", "tensor")


def plan(dp):
    if dp == 16:
        return (8, 4, 1, 2), (8, 4, 2, 1)
    bits = [1 << i for i in range(dp.bit_length() - 1)]
    side = len(bits) // 3
    x, y, z = bits[:side], bits[side:2 * side], bits[2 * side:]
    return tuple(z[::-1] + x[::-1] + y[::-1]), tuple(z[::-1] + y[::-1] + x[::-1])


def flip(value, dp, masks):
    pairs = [(d * 2 + t, (d ^ masks[t]) * 2 + t) for d in range(dp) for t in range(2)]
    return lax.ppermute(value, GROUP, pairs)


def swap(value):
    return lax.ppermute(value, "tensor", [(0, 1), (1, 0)])


def doubled(held, dp, masks):
    return jnp.concatenate([held, flip(held, dp, masks)], axis=0)


def after(value, *others):
    return lax.optimization_barrier((value, *others))[0]


def places(dp, mine, tensor):
    rel = jnp.arange(dp, dtype=jnp.int32) ^ mine
    found = []
    for order in plan(dp):
        found.append(sum(((rel & mask) // mask) << i for i, mask in enumerate(order)))
    return jnp.stack([jnp.where(tensor == t, found[0], found[1]) for t in (0, 1)])


def reduced(held, dp, masks, kind=BF):
    half = held.shape[0] // 2
    return add(held[:half], flip(held[half:], dp, masks), kind)


def add(a, b, kind=BF):
    return (a.astype(F32) + b.astype(F32)).astype(kind)


def body(embedded, piece_lengths, pair_tags, pair_embedding, w_query, w_key, w_value, w_output, w_hidden,
         w_down, first_gain, first_shift, second_gain, second_shift, cotangent):
    dp = lax.axis_size("dp")
    mine, tensor = lax.axis_index("dp"), lax.axis_index("tensor")
    rows = D // dp
    blocked = rows % 16 == 0
    pieces = lax.dynamic_index_in_dim(piece_lengths, tensor, 0, keepdims=False)
    tag = lax.dynamic_index_in_dim(pair_tags, tensor, 0, keepdims=True)
    small = jnp.concatenate([jnp.stack([first_gain, first_shift, second_gain, second_shift]), pair_embedding], axis=0)
    small = tn(small, jnp.eye(8, 128, dtype=BF)).astype(BF)
    at = places(dp, mine, tensor)

    def arranged(held):
        both = held, swap(held)
        if blocked:
            return both
        return tuple(h[at[i]].reshape(D, -1) for i, h in enumerate(both))

    def part(width):
        return (dp, rows, width) if blocked else (D, width)

    def swapped(keep, send):
        if not blocked:
            keep, send = (v.reshape(dp, rows, -1)[jnp.zeros((dp,), jnp.int32).at[at[i]].set(jnp.arange(dp))]
                          for i, v in enumerate((keep, send)))
        return add(keep, swap(send))

    def summed(held, phases):
        for i, masks in enumerate(phases):
            held = reduced(held, dp, masks, F32 if i == len(phases) - 1 else BF)
        return held[0]

    phases = list(zip(*plan(dp)))
    split = len(phases) - 1
    first = jnp.concatenate([w_query, w_key, w_value, small], axis=1)[None]
    rest = jnp.concatenate([w_output.T, w_hidden, w_down.T], axis=1)[None]
    for i, masks in enumerate(phases):
        first = doubled(first, dp, masks)
        if i < split - 1:
            rest = doubled(after(rest, first, *((tag, pieces, at) if i == 0 else ())), dp, masks)
        elif i == split - 1:
            rest = after(rest, first)
            arrived = flip(rest, dp, masks)
    first = arranged(after(first, rest))
    heads, par, bound = open_visit(pieces, tag, at, embedded, *first)
    rest = jnp.concatenate([after(rest, *heads), arrived], axis=0)
    rest, heads = lax.optimization_barrier((rest, heads))
    arrived, swapped_rest = flip(rest, dp, phases[-1]), swap(rest)
    q, k, v, vt = heads
    (mixed, low, inv), probs = attend_visit(pieces, bound, q, k, v, vt)
    arrived = after(arrived, mixed)
    if blocked:
        rest = (rest, arrived, swapped_rest, swap(arrived))
    else:
        rest = arranged(jnp.concatenate([rest, arrived], axis=0))
    result, base, gm, stats, old, sums = middle(pieces, tag, at, embedded, mixed, inv, par, first, rest, cotangent)
    if blocked:
        keep, keep_out, send, send_out = sums
        out = add(keep_out, swap(send_out))
        gm = after(gm, out)
        out = flip(out, dp, phases[-1])
        sums = add(add(keep, swap(send), F32), out)
    else:
        sums = reduced(swapped(*sums), dp, phases[-1])
    grads = heads_back(pieces, (q, k, v, mixed, low), gm, probs)
    sums, grads = lax.optimization_barrier((sums, grads))
    half = sums.shape[0] // 2
    out = flip(sums[half:], dp, phases[-2])
    grad, *da = last_back(tag, at, part, grads, embedded, par, base, first, old, stats)
    *da, out = lax.optimization_barrier((*da, out))
    sums = add(sums[:half], out)
    da = swapped(*da)
    sums = summed(sums, phases[-3::-1])
    da = summed(da, phases[::-1])
    small = da[:, 3 * HALF:3 * HALF + 8].T
    return (result, grad, small[4:], da[:, :HALF], da[:, HALF:2 * HALF], da[:, 2 * HALF:3 * HALF],
            sums[:, :HALF].T, sums[:, HID:DOWN], sums[:, DOWN:].T, small[0], small[1], small[2], small[3])


def solution(mesh):
    both = P(GROUP, None)
    params = (P("dp", "tensor"),) * 3 + (P("tensor", "dp"), P("dp", "tensor"), P("tensor", "dp"))
    in_specs = (both, P("dp", None), P("dp"), P(None, "dp")) + params + (P("dp"),) * 4 + (both,)
    out_specs = (both, both, P(None, "dp")) + params + (P("dp"),) * 4
    return jax.shard_map(body, mesh=mesh, in_specs=in_specs, out_specs=out_specs, check_vma=False)
```
